128 devices in a mesh: section: 2 (over z_lo), seq: 16 (over y, z_hi, core), tensor: 4 (over x).
Axes of the slice: x: 4, y: 4, z: 4 (z_hi: 2, z_lo: 2; z = z_hi * 2 + z_lo), core: 2. Of those that a mesh axis runs over, the one named last changes fastest.
Arguments:
- tokens: bfloat16 [8192, 8192], P(('section', 'seq')), may hold values from -6 to 6
- w_query: bfloat16 [8192, 4096], P(('section', 'seq'), 'tensor'), may hold values from -0.0625 to 0.0625
- query_gain: float32 [8192], replicated, may hold values from 0.125 to 2
- state_kv: bfloat16 [8192, 1792], P('tensor'), may hold values from -0.0625 to 0.0625
- neighbours: bfloat16 [2, 64, 2, 128, 896], P('section', ('seq', 'tensor')), may hold values from -6 to 6
- enc_gain: float32 [896], replicated, may hold values from 0.5 to 2
- enc_query: bfloat16 [896, 896], replicated, may hold values from -0.1875 to 0.1875
- enc_out: bfloat16 [896, 896], replicated, may hold values from -0.1875 to 0.1875
- w_key: bfloat16 [896, 4096], P(None, 'tensor'), may hold values from -0.1875 to 0.1875
- w_value: bfloat16 [896, 4096], P(None, 'tensor'), may hold values from -0.1875 to 0.1875
- counts: int32 [128], P(('section', 'seq')), may hold values from 0 to 2
- d_context: bfloat16 [8192, 4096], P(('section', 'seq'), 'tensor'), may hold values from -1.5 to 1.5
Outputs:
- context: bfloat16 [8192, 4096], P(('section', 'seq'), 'tensor')
- d_hidden: bfloat16 [8192, 8192], P(('section', 'seq'), 'tensor')
- d_query_weight: float32 [8192, 4096], P(('section', 'seq'), 'tensor')
- d_encoded: bfloat16 [2, 64, 2, 128, 896], P('section', ('seq', 'tensor'))
- row_dots: float32 [8192], P(('section', 'seq'))
The draws below stay inside these ranges and needn't reach their ends.
Inputs may be any that keep to these rules, and one draw needn't show every extreme that they name: `counts`: slots of a block from its count on hold padding.
All inputs are finite; a program needn't handle non-finite values.
Results may differ from the reference program's by a relative error of at most 0.039.
Values may be sent and summed in bfloat16 or wider, within the bound.
A program may use at most 192 MiB of HBM per device.

```python
import math
import jax
import jax.numpy as jnp
from jax import lax

D = 8192
HD = 128
E = 896
HEADS = 32
EHD = 64
BLOCK = 64
NBR = 2
RLEN = 128
TOK_DEV = 256
TOKENS = 8192
HALF_BLOCKS = 64
BLOCKS = 128
N_SECTION = 2
N_SEQ = 16
N_TENSOR = 4


def log_spread(key, length, low_end, high_end):
    return jnp.exp(jax.random.uniform(key, (length,), jnp.float32, math.log(low_end), math.log(high_end)))


def rising_ramp(length, factor):
    position = jnp.arange(length, dtype=jnp.float32) / (length - 1)
    return jnp.exp(position * math.log(factor))


def draw_query_gain(key, part):
    key = jax.random.fold_in(key, 11)
    return log_spread(key, D, 0.25, 0.5) * rising_ramp(D, 4.0)


def draw_enc_gain(key, part):
    key = jax.random.fold_in(key, 23)
    return log_spread(key, E, 0.5, 2.0)


def plant(values, stream_key, smallest, largest):
    longest = values.shape.index(max(values.shape))
    spots = []
    for shift in (0, 1):
        where = [jax.random.randint(jax.random.fold_in(stream_key, axis), (), 0, length) for axis, length in enumerate(values.shape)]
        where[longest] = (where[longest] + shift) % values.shape[longest]
        spots.append(tuple(where))
    return values.at[spots[0]].set(smallest).at[spots[1]].set(largest)


def levels(rng, dims, split, low, largest):
    def one(dim, parts):
        heights = jax.random.uniform(jax.random.fold_in(jax.random.fold_in(rng, 6), dim), (parts,), jnp.float32, low / len(split), largest / len(split))
        return jnp.repeat(jnp.exp(heights), dims[dim] // parts).reshape((-1,) + (1,) * (len(dims) - dim - 1))

    factor_of = one(*split[0])
    for cut in split[1:]:
        factor_of = factor_of * one(*cut)
    return factor_of


def centred(own_key, shape, spread, most, cuts=(), kind=jnp.bfloat16):
    factor_of = levels(own_key, shape, cuts, -0.22, 0.18) if cuts else 1.0
    entries = jax.random.normal(own_key, shape, jnp.float32) * spread * factor_of
    return jnp.minimum(jnp.maximum(entries, -most), most).astype(kind)


def setup_inputs(seed: int = 0) -> dict:
    arg_keys = jax.random.split(jax.random.key(seed), 13)
    return {
        "tokens": centred(arg_keys[0], (TOKENS, D), 1.0, 6.0, ((0, 32),)),
        "w_query": centred(arg_keys[1], (D, HEADS * HD), D ** -0.5, 0.0625, ((0, 32), (1, 4))),
        "query_gain": draw_query_gain(jax.random.fold_in(arg_keys[12], 71), 0),
        "state_kv": centred(arg_keys[3], (D, 2 * E), D ** -0.5, 0.0625, ((0, 4),)),
        "neighbours": centred(arg_keys[4], (N_SECTION, HALF_BLOCKS, NBR, RLEN, E), 1.0, 6.0, ((0, 2), (1, 64))),
        "enc_gain": draw_enc_gain(jax.random.fold_in(arg_keys[12], 71), 0),
        "enc_query": centred(arg_keys[6], (E, E), E ** -0.5, 0.1875),
        "enc_out": centred(arg_keys[7], (E, E), E ** -0.5, 0.1875),
        "w_key": centred(arg_keys[8], (E, HEADS * HD), E ** -0.5, 0.1875, ((1, 4),)),
        "w_value": centred(arg_keys[9], (E, HEADS * HD), E ** -0.5, 0.1875, ((1, 4),)),
        "counts": plant(jax.random.randint(arg_keys[10], (BLOCKS,), 0, NBR + 1), jax.random.fold_in(arg_keys[10], 1), 0, NBR).astype(jnp.int32),
        "d_context": centred(arg_keys[11], (TOKENS, HEADS * HD), 0.25, 1.5, ((0, 32), (1, 4))),
    }


EPSILON = 1e-05
NEG_LARGE = -1e+30

def narrowed(values_in):
    return lax.optimization_barrier(values_in.astype(jnp.bfloat16)).astype(jnp.float32)

def encode(enc_in, block_states, enc_gain, enc_query, enc_out):
    block_count = enc_in.shape[0]
    heads_enc = E // EHD
    enc_rows = enc_in.astype(jnp.float32).reshape(-1, E)
    enc_scale = lax.rsqrt(lax.optimization_barrier(jnp.mean(enc_rows * enc_rows, axis=-1, keepdims=True)) + EPSILON)
    enc_normed = (enc_rows * enc_scale * enc_gain).astype(jnp.bfloat16)
    enc_queries = narrowed(jnp.dot(enc_normed, enc_query, preferred_element_type=jnp.float32))
    query_heads = enc_queries.reshape(block_count, NBR * RLEN, heads_enc, EHD)
    state_rows = block_states.reshape(block_count, BLOCK, 2 * E).astype(jnp.float32)
    key_heads = state_rows[:, :, :E].reshape(block_count, BLOCK, heads_enc, EHD)
    value_heads = state_rows[:, :, E:].reshape(block_count, BLOCK, heads_enc, EHD)
    scores = jnp.einsum('cqhd,ckhd->chqk', query_heads, key_heads) / math.sqrt(EHD)
    row_top = lax.optimization_barrier(jnp.max(scores, axis=-1, keepdims=True))
    weights = jnp.exp(scores - row_top)
    enc_weights = narrowed(weights / lax.optimization_barrier(jnp.sum(weights, axis=-1, keepdims=True)))
    enc_context = jnp.einsum('chqk,ckhd->cqhd', enc_weights, value_heads).astype(jnp.bfloat16).reshape(-1, E)
    mixed = enc_rows + jnp.dot(enc_context, enc_out, preferred_element_type=jnp.float32)
    return mixed.astype(jnp.bfloat16).reshape(block_count, NBR, RLEN, E)

def reference(tokens, w_query, query_gain, state_kv, neighbours, enc_gain, enc_query, enc_out, w_key, w_value, counts, d_context):
    hidden = tokens.astype(jnp.float32)
    inverse = lax.rsqrt(lax.optimization_barrier(jnp.mean(hidden * hidden, axis=-1, keepdims=True)) + EPSILON)
    unit_full = hidden * inverse
    unit_rows = unit_full.astype(jnp.bfloat16)
    normed = (unit_full * query_gain).astype(jnp.bfloat16)
    queries = narrowed(jnp.dot(normed, w_query, preferred_element_type=jnp.float32))
    width_share = D // N_TENSOR
    state_sum = jnp.zeros((TOKENS, 2 * E), jnp.float32)
    for block_index in range(N_TENSOR):
        row_start = block_index * width_share
        state_sum = state_sum + narrowed(jnp.dot(unit_rows[:, row_start:row_start + width_share], state_kv[row_start:row_start + width_share], preferred_element_type=jnp.float32))
    block_states = state_sum.astype(jnp.bfloat16)
    enc_in = jnp.concatenate([neighbours[1], neighbours[0]], axis=0)
    encoded = encode(enc_in, block_states, enc_gain, enc_query, enc_out)
    all_width = HEADS * HD
    enc_flat = encoded.reshape(-1, E)
    key_rows = narrowed(jnp.dot(enc_flat, w_key, preferred_element_type=jnp.float32))
    value_rows = narrowed(jnp.dot(enc_flat, w_value, preferred_element_type=jnp.float32))
    query_heads = queries.reshape(BLOCKS, BLOCK, HEADS, HD)
    key_heads = key_rows.reshape(BLOCKS, NBR * RLEN, HEADS, HD)
    value_heads = value_rows.reshape(BLOCKS, NBR * RLEN, HEADS, HD)
    score_scale = 1.0 / math.sqrt(HD)
    scores = jnp.einsum('cqhd,ckhd->chqk', query_heads, key_heads) * score_scale
    slot_index = jnp.arange(NBR * RLEN, dtype=jnp.int32) // RLEN
    valid_keys = (slot_index[None, :] < counts[:, None])[:, None, None, :]
    row_top = lax.optimization_barrier(jnp.max(jnp.where(valid_keys, scores, NEG_LARGE), axis=-1, keepdims=True))
    weights = jnp.where(valid_keys, jnp.exp(scores - row_top), 0.0)
    empty_rows = (counts == 0).astype(jnp.float32)[:, None, None, None]
    attn_probs = weights / (lax.optimization_barrier(jnp.sum(weights, axis=-1, keepdims=True)) + empty_rows)
    attn_weights = narrowed(attn_probs)
    context = jnp.einsum('chqk,ckhd->cqhd', attn_weights, value_heads).astype(jnp.bfloat16).reshape(TOKENS, all_width)
    grad_heads = d_context.astype(jnp.float32).reshape(BLOCKS, BLOCK, HEADS, HD)
    d_values = jnp.einsum('chqk,cqhd->ckhd', attn_weights, grad_heads).astype(jnp.bfloat16).reshape(-1, all_width)
    d_probs = jnp.einsum('cqhd,ckhd->chqk', grad_heads, value_heads)
    d_scores = narrowed(attn_probs * (d_probs - lax.optimization_barrier(jnp.sum(attn_probs * d_probs, axis=-1, keepdims=True))) * score_scale)
    d_queries = jnp.einsum('chqk,ckhd->cqhd', d_scores, key_heads).astype(jnp.bfloat16).reshape(TOKENS, all_width)
    d_keys = jnp.einsum('chqk,cqhd->ckhd', d_scores, query_heads).astype(jnp.bfloat16).reshape(-1, all_width)
    head_share = all_width // N_TENSOR
    grad_sum = jnp.zeros((BLOCKS * NBR * RLEN, E), jnp.float32)
    normed_sum = jnp.zeros((TOKENS, D), jnp.float32)
    for block_index in range(N_TENSOR):
        col_start = block_index * head_share
        col_end = col_start + head_share
        grad_term = jnp.dot(d_keys[:, col_start:col_end], w_key[:, col_start:col_end].T, preferred_element_type=jnp.float32)
        grad_term = grad_term + jnp.dot(d_values[:, col_start:col_end], w_value[:, col_start:col_end].T, preferred_element_type=jnp.float32)
        grad_sum = grad_sum + narrowed(grad_term)
        normed_sum = normed_sum + narrowed(jnp.dot(d_queries[:, col_start:col_end], w_query[:, col_start:col_end].T, preferred_element_type=jnp.float32))
    grad_blocks = grad_sum.astype(jnp.bfloat16).reshape(N_SECTION, HALF_BLOCKS, NBR, RLEN, E)
    d_encoded = jnp.concatenate([grad_blocks[1:2], grad_blocks[0:1]], axis=0)
    normed_groups = normed.reshape(N_SECTION * N_SEQ, TOK_DEV, D)
    query_groups = d_queries.reshape(N_SECTION * N_SEQ, TOK_DEV, all_width)

    def add_group(running, pair):
        group_rows, group_grads = pair
        return (running + narrowed(jnp.dot(group_rows.T, group_grads, preferred_element_type=jnp.float32)), None)
    d_query_weight, _ = lax.scan(add_group, jnp.zeros((D, all_width), jnp.float32), (normed_groups, query_groups))
    d_unit = normed_sum * query_gain
    row_sums = lax.optimization_barrier(jnp.sum(d_unit * unit_full, axis=-1, keepdims=True))
    row_dots = row_sums[:, 0] / math.sqrt(D)
    d_hidden = (inverse * (d_unit - unit_full * (row_sums / D))).astype(jnp.bfloat16)
    return (context, d_hidden, d_query_weight, d_encoded, row_dots)
```

```python
import functools
import math

import jax
import jax.numpy as jnp
from jax import lax
from jax.experimental import pallas as pl
from jax.experimental.pallas import tpu as pltpu
from jax.sharding import PartitionSpec as P

HD = 128
E = 896
EHD = 64
BLOCK = 64
NBR = 2
RLEN = 128
KEYS = NBR * RLEN

EPSILON = 1e-05
NEG_LARGE = -1e30
MESH = pl.DeviceIdType.MESH
F32 = jnp.float32
BF16 = jnp.bfloat16
LAST = (((1,), (1,)), ((), ()))
FIRST = (((0,), (0,)), ((), ()))


def dot(a, b, dims=(((1,), (0,)), ((), ()))):
    return lax.dot_general(a, b, dims, preferred_element_type=F32)


def swapped(value, axis, distance):
    mask = 2**distance
    pairs = [(source, source ^ mask) for source in range(lax.axis_size(axis))]
    return lax.ppermute(value, axis, pairs)


def encode(enc_in, block_states, enc_gain, enc_query, enc_out):
    block_count = enc_in.shape[0]
    heads_enc = E // EHD
    enc_rows = enc_in.astype(jnp.float32).reshape(-1, E)
    enc_scale = lax.rsqrt(jnp.mean(enc_rows * enc_rows, axis=-1, keepdims=True) + EPSILON)
    enc_normed = (enc_rows * enc_scale * enc_gain).astype(jnp.bfloat16)
    enc_queries = jnp.dot(enc_normed, enc_query, preferred_element_type=jnp.float32).astype(
        jnp.bfloat16
    )
    query_heads = enc_queries.reshape(block_count, NBR * RLEN, heads_enc, EHD)
    state_rows = block_states.reshape(block_count, BLOCK, 2 * E)
    key_heads = state_rows[:, :, :E].reshape(block_count, BLOCK, heads_enc, EHD)
    value_heads = state_rows[:, :, E:].reshape(block_count, BLOCK, heads_enc, EHD)
    scores = jnp.einsum(
        "cqhd,ckhd->chqk", query_heads, key_heads, preferred_element_type=jnp.float32
    ) / math.sqrt(EHD)
    row_top = jnp.max(scores, axis=-1, keepdims=True)
    weights = jnp.exp(scores - row_top)
    enc_weights = (weights / jnp.sum(weights, axis=-1, keepdims=True)).astype(jnp.bfloat16)
    enc_context = (
        jnp.einsum("chqk,ckhd->cqhd", enc_weights, value_heads, preferred_element_type=jnp.float32)
        .astype(jnp.bfloat16)
        .reshape(-1, E)
    )
    mixed = enc_rows + jnp.dot(enc_context, enc_out, preferred_element_type=jnp.float32)
    return mixed.astype(jnp.bfloat16).reshape(block_count, NBR, RLEN, E)


def attend_kernel(
    counts, q_ref, enc_ref, wk_ref, wv_ref, do_ref,
    ctx_ref, dq_ref, grad_ref, sums_ref,
    k_s, v_s, dk_s, dv_s,
):
    count = counts[pl.program_id(0)]
    enc = enc_ref[...]
    k_s[...] = dot(enc, wk_ref[...]).astype(BF16)
    v_s[...] = dot(enc, wv_ref[...]).astype(BF16)
    valid = lax.broadcasted_iota(jnp.int32, (BLOCK, KEYS), 1) < count * RLEN
    empty = jnp.where(count == 0, 1.0, 0.0).astype(F32)
    scale = 1.0 / math.sqrt(HD)
    total = jnp.zeros((BLOCK, HD), F32)
    for head in range(q_ref.shape[1] // HD):
        cols = slice(head * HD, (head + 1) * HD)
        q, k, v, do = q_ref[:, cols], k_s[:, cols], v_s[:, cols], do_ref[:, cols]
        scores = dot(q, k, LAST) * scale
        top = jnp.max(jnp.where(valid, scores, NEG_LARGE), axis=-1, keepdims=True)
        weights = jnp.where(valid, jnp.exp(scores - top), 0.0)
        probs = weights / (jnp.sum(weights, axis=-1, keepdims=True) + empty)
        rounded = probs.astype(BF16)
        ctx_ref[:, cols] = dot(rounded, v).astype(BF16)
        dv_s[:, cols] = dot(rounded, do, FIRST).astype(BF16)
        d_probs = dot(do, v, LAST)
        inner = jnp.sum(probs * d_probs, axis=-1, keepdims=True)
        d_scores = (probs * (d_probs - inner) * scale).astype(BF16)
        dq = dot(d_scores, k)
        dq_ref[:, cols] = dq.astype(BF16)
        total = total + dq * q.astype(F32)
        dk_s[:, cols] = dot(d_scores, q, FIRST).astype(BF16)
    grad = dot(dk_s[...], wk_ref[...], LAST) + dot(dv_s[...], wv_ref[...], LAST)
    grad_ref[0] = grad.astype(BF16)
    sums_ref[...] = jnp.broadcast_to(jnp.sum(total, axis=-1, keepdims=True), (BLOCK, HD))


def attend(counts, queries, encoded, w_key, w_value, d_context):
    blocks = counts.shape[0]
    rows, width = queries.shape
    row_block = pl.BlockSpec((BLOCK, width), lambda b: (b, 0))
    weight = pl.BlockSpec((E, width), lambda b: (0, 0))
    flops = 2 * (4 * rows * 4 * E * width + 6 * rows * KEYS * width)
    return pl.pallas_call(
        attend_kernel,
        grid=(blocks,),
        in_specs=[
            pl.BlockSpec(memory_space=pltpu.SMEM),
            row_block,
            pl.BlockSpec((KEYS, E), lambda b: (b, 0)),
            weight,
            weight,
            row_block,
        ],
        out_specs=[
            row_block,
            row_block,
            pl.BlockSpec((1, KEYS, E), lambda b: (b, 0, 0)),
            pl.BlockSpec((BLOCK, HD), lambda b: (b, 0)),
        ],
        out_shape=[
            jax.ShapeDtypeStruct((rows, width), BF16),
            jax.ShapeDtypeStruct((rows, width), BF16),
            jax.ShapeDtypeStruct((blocks, KEYS, E), BF16),
            jax.ShapeDtypeStruct((rows, HD), F32),
        ],
        scratch_shapes=[pltpu.VMEM((KEYS, width), BF16)] * 4,
        compiler_params=pltpu.CompilerParams(vmem_limit_bytes=50 * 2**20),
        cost_estimate=pl.CostEstimate(
            flops=flops, bytes_accessed=14 * 2**20, transcendentals=rows * 8 * KEYS
        ),
    )(counts, queries, encoded, w_key, w_value, d_context)


class Place:
    def __init__(self):
        self.section = lax.axis_index("section")
        seq = lax.axis_index("seq")
        self.x = lax.axis_index("tensor")
        self.core = seq % 2
        self.y = seq // 4
        self.z = 2 * ((seq // 2) % 2) + self.section

    def along(self, dim, off):
        if dim == "x":
            return (self.section, self.seq_of(self.y, self.z), (self.x + off) % 4)
        if dim == "y":
            return (self.section, self.seq_of((self.y + off) % 4, self.z), self.x)
        z = (self.z + off) % 4
        return (z % 2, self.seq_of(self.y, z), self.x)

    def seq_of(self, y, z):
        return y * 4 + (z // 2) * 2 + self.core

    def sibling(self):
        return (self.section, self.y * 4 + (self.z // 2) * 2 + 1 - self.core, self.x)

    def partner(self):
        return (1 - self.section, self.seq_of(self.y, self.z), self.x)

    def chunk(self, dy, dz):
        y, z = (self.y + dy) % 4, (self.z + dz) % 4
        return (z % 2) * 8 + y * 2 + z // 2


def greet(devices):
    barrier = pltpu.get_barrier_semaphore()
    for device in devices:
        pl.semaphore_signal(barrier, inc=1, device_id=device, device_id_type=MESH)
    pl.semaphore_wait(barrier, len(devices))


LINES = (2, 1, 3, 0)


def backward_kernel(
    dq_ref, mine_ref, sib_ref, w_ref, grad_ref, sums_ref, tokens_ref, inverse_ref, gain_ref,
    dw_ref, dh_ref, de_ref, dots_ref,
    dq2, dq_t, nrm, wc, prod, ra1, ra2, rb1, rb2, part, rn1, rn2, out_sib, in_sib,
    g1, gs, g2, gfin, gin, sums_in, tok, dh_s, column,
    load_sem, dh_sem, send_sem, recv_sem,
):
    at = Place()
    width = tokens_ref.shape[1]
    share = width // 4
    loads = [
        pltpu.make_async_copy(mine_ref, nrm.at[:, 0:256], load_sem.at[0]),
        pltpu.make_async_copy(sib_ref, nrm.at[:, 256:512], load_sem.at[1]),
        pltpu.make_async_copy(w_ref.at[:, at.core], wc, load_sem.at[2]),
    ]
    for i in range(8):
        first = pl.multiple_of(at.x * share + i * 256, 256)
        loads.append(
            pltpu.make_async_copy(tokens_ref.at[:, pl.ds(first, 256)], tok.at[i], load_sem.at[3 + i])
        )
    for load in loads:
        load.start()
    greet(
        [at.along("x", 1), at.along("x", 2), at.along("x", 3), at.along("y", 1), at.along("y", 3),
         at.along("z", 1), at.along("z", 3), at.sibling()]
    )

    copies = []

    def send(src, dst, device):
        index = len(copies)
        copy = pltpu.make_async_remote_copy(
            src_ref=src, dst_ref=dst, send_sem=send_sem.at[index], recv_sem=recv_sem.at[index],
            device_id=device, device_id_type=MESH,
        )
        copy.start()
        copies.append(copy)
        return copy

    def added(dst, first, second):
        dst[...] = (first[...].astype(F32) + second[...].astype(F32)).astype(BF16)

    c_dq = send(dq_ref, dq2.at[256:512], at.sibling())
    far = (at.x + 2) % 4
    up, down = (at.x + 1) % 4, (at.x + 3) % 4
    c_g1 = [
        send(grad_ref.at[far, 0:128], g1.at[0], at.along("x", 1)),
        send(grad_ref.at[far, 128:256], g1.at[1], at.along("x", 3)),
    ]
    c_sums = [send(sums_ref, sums_in.at[i], at.along("x", i + 1)) for i in range(3)]
    dq2[0:256] = dq_ref[...]
    for j in range(4):
        dq_t[256 * j : 256 * j + 256, 0:256] = jnp.transpose(dq_ref[:, 256 * j : 256 * j + 256])
    c_dq.wait_recv()
    for j in range(4):
        dq_t[256 * j : 256 * j + 256, 256:512] = jnp.transpose(
            dq2[256:512, 256 * j : 256 * j + 256]
        )
    loads[0].wait()
    loads[1].wait()

    def product(dy, dz):
        k = at.chunk(dy, dz)

        @pl.loop(0, 4)
        def _(i):
            rows = pl.ds(pl.multiple_of(i * 256, 256), 256)
            prod[k, rows, :] = dot(dq_t[rows, :], nrm[k]).astype(BF16)

    dims = (("z", "y"), ("y", "z"))

    def block(half, line, off, low=0, high=512):
        dy, dz = (line, off) if half == 0 else (off, line)
        return prod.at[at.chunk(dy, dz), half * 512 + low : half * 512 + high]

    c1 = {}

    def first_hop(half, line):
        dim = dims[half][0]
        slot = LINES.index(line)
        c1[half, line] = (
            send(block(half, line, 2, 0, 256), ra1.at[half, slot, 0], at.along(dim, 1)),
            send(block(half, line, 2, 256, 512), ra1.at[half, slot, 1], at.along(dim, 3)),
        )

    product(2, 2)
    first_hop(0, 2)
    first_hop(1, 2)
    for line in (1, 3, 0):
        product(line, 2)
        first_hop(0, line)
        product(2, line)
        first_hop(1, line)
    for dy in (1, 3, 0):
        for dz in (1, 3, 0):
            product(dy, dz)

    c_g1[0].wait_recv()
    c_g1[1].wait_recv()
    gs[0, 0:128] = (grad_ref[up, 0:128].astype(F32) + g1[0].astype(F32)).astype(BF16)
    gs[0, 128:256] = grad_ref[up, 128:256]
    gs[1, 0:128] = grad_ref[down, 0:128]
    gs[1, 128:256] = (grad_ref[down, 128:256].astype(F32) + g1[1].astype(F32)).astype(BF16)
    c_g2 = [
        send(gs.at[0], g2.at[0], at.along("x", 1)),
        send(gs.at[1], g2.at[1], at.along("x", 3)),
    ]

    c2 = {}

    def second_hop(half, line):
        dim = dims[half][0]
        slot = LINES.index(line)
        for way, off in ((0, 1), (1, 3)):
            c1[half, line][way].wait_recv()
            piece = block(half, line, off, 256 * way, 256 * way + 256)
            added(piece, piece, ra1.at[half, slot, way])
        c2[half, line] = (
            send(block(half, line, 1), ra2.at[half, slot, 0], at.along(dim, 1)),
            send(block(half, line, 3), ra2.at[half, slot, 1], at.along(dim, 3)),
        )

    def partial(k):
        @pl.loop(0, 2)
        def _(i):
            rows = pl.ds(pl.multiple_of(i * 256, 256), 256)
            part[k, rows, :] = dot(dq2[rows, :], wc[k], LAST).astype(BF16)

    n1, n2 = [], []
    loads[2].wait()
    second_hop(0, 2)
    second_hop(1, 2)
    for m in range(4):
        partial(far * 4 + m)
        n1.append(
            (
                send(part.at[far * 4 + m, 0:256], rn1.at[m, 0], at.along("x", 1)),
                send(part.at[far * 4 + m, 256:512], rn1.at[m, 1], at.along("x", 3)),
            )
        )
        if m > 0:
            second_hop(0, LINES[m])
            second_hop(1, LINES[m])

    for copy in c_sums:
        copy.wait_recv()
    sums = sums_ref[...] + sums_in[0] + sums_in[1] + sums_in[2]
    dots_ref[...] = sums * (1.0 / math.sqrt(width))
    column[...] = jnp.transpose(jnp.broadcast_to(sums[0:1], (128, 256)))

    for m in range(4):
        partial(up * 4 + m)
        partial(down * 4 + m)
        partial(at.x * 4 + m)
    for m in range(4):
        n1[m][0].wait_recv()
        piece = part.at[up * 4 + m, 0:256]
        added(piece, piece, rn1.at[m, 0])
        n1[m][1].wait_recv()
        piece = part.at[down * 4 + m, 256:512]
        added(piece, piece, rn1.at[m, 1])
        n2.append(
            (
                send(part.at[up * 4 + m], rn2.at[m, 0], at.along("x", 1)),
                send(part.at[down * 4 + m], rn2.at[m, 1], at.along("x", 3)),
            )
        )

    for copy in c_g2:
        copy.wait_recv()
    gfin[...] = (grad_ref[at.x].astype(F32) + g2[0].astype(F32) + g2[1].astype(F32)).astype(BF16)
    c_swap = send(gfin, gin, at.partner())

    def gathered(half, line):
        for way in (0, 1):
            c2[half, line][way].wait_recv()
        slot = LINES.index(line)
        piece = block(half, line, 0)
        total = piece[...].astype(F32) + ra2[half, slot, 0].astype(F32)
        piece[...] = (total + ra2[half, slot, 1].astype(F32)).astype(BF16)

    for load in loads[3:]:
        load.wait()
    stores = []

    def finish(i, d_normed):
        unit = tok[i].astype(F32) * inverse_ref[...]
        rows = jnp.concatenate([column[...], column[...]], axis=1)
        grads = d_normed * gain_ref[at.x * 8 + i]
        result = inverse_ref[...] * (grads - unit * (rows * (1.0 / width)))
        dh_s[i] = result.astype(BF16)
        first = pl.multiple_of(i * 256, 256)
        store = pltpu.make_async_copy(
            dh_s.at[i], dh_ref.at[:, pl.ds(first, 256)], dh_sem.at[len(stores)]
        )
        store.start()
        stores.append(store)

    c_sib = []

    def normed_sum(m):
        for copy in n2[m]:
            copy.wait_recv()

        def summed(low):
            rows = slice(low, low + 256)
            total = part[at.x * 4 + m, rows].astype(F32) + rn2[m, 0, rows].astype(F32)
            return total + rn2[m, 1, rows].astype(F32)

        out_sib[m] = summed(256).astype(BF16)
        c_sib.append(send(out_sib.at[m], in_sib.at[m], at.sibling()))
        finish(2 * m + at.core, summed(0))

    d1, d2 = {}, {}

    def turn(half):
        dim = dims[half][1]
        d1[half] = (
            send(block(half, 2, 0, 0, 256), rb1.at[half, 0], at.along(dim, 1)),
            send(block(half, 2, 0, 256, 512), rb1.at[half, 1], at.along(dim, 3)),
        )

    def turned(half):
        dim = dims[half][1]
        for way, off in ((0, 1), (1, 3)):
            d1[half][way].wait_recv()
            piece = block(half, off, 0, 256 * way, 256 * way + 256)
            added(piece, piece, rb1.at[half, way])
        d2[half] = (
            send(block(half, 1, 0), rb2.at[half, 0], at.along(dim, 1)),
            send(block(half, 3, 0), rb2.at[half, 1], at.along(dim, 3)),
        )

    def result(half):
        for way in (0, 1):
            c2[half, 0][way].wait_recv()
            d2[half][way].wait_recv()
        for low in (0, 256):
            rows = slice(low, low + 256)
            total = block(half, 0, 0)[rows].astype(F32)
            for extra in (ra2.at[half, 3, 0], ra2.at[half, 3, 1], rb2.at[half, 0], rb2.at[half, 1]):
                total = total + extra[rows].astype(F32)
            first = half * 512 + low
            dw_ref[:, first : first + 256] = jnp.transpose(total)

    for half in (0, 1):
        gathered(half, 2)
        turn(half)
    normed_sum(0)
    for half in (0, 1):
        gathered(half, 1)
    normed_sum(1)
    for half in (0, 1):
        gathered(half, 3)
    for half in (0, 1):
        turned(half)
    normed_sum(2)
    for half in (0, 1):
        result(half)
    normed_sum(3)
    for m in range(4):
        c_sib[m].wait_recv()
        finish(2 * m + 1 - at.core, in_sib[m].astype(F32))
    c_swap.wait_recv()
    de_ref[...] = gin[...]
    for copy in copies:
        copy.wait_send()
    for store in stores:
        store.wait()


SENDS = 1 + 2 + 3 + 16 + 2 + 16 + 8 + 8 + 1 + 4 + 8


def backward(d_queries, mine, theirs, w_all, grad, sums, tokens, inverse, gain):
    rows, width = d_queries.shape
    full = tokens.shape[1]
    vmem = pl.BlockSpec(memory_space=pltpu.VMEM)
    anywhere = pl.BlockSpec(memory_space=pl.ANY)

    def buffer(*shape, kind=BF16):
        return pltpu.VMEM(shape, kind)

    return pl.pallas_call(
        backward_kernel,
        in_specs=[vmem, anywhere, anywhere, anywhere, vmem, vmem, anywhere, vmem, vmem],
        out_specs=[vmem, anywhere, vmem, vmem],
        out_shape=[
            jax.ShapeDtypeStruct((256, width), F32),
            jax.ShapeDtypeStruct((rows, full // 4), BF16),
            jax.ShapeDtypeStruct((KEYS, E), BF16),
            jax.ShapeDtypeStruct((8, rows), F32),
        ],
        scratch_shapes=[
            buffer(512, 1024),
            buffer(1024, 512),
            buffer(16, 512, 256),
            buffer(16, 256, 1024),
            buffer(16, 1024, 256),
            buffer(2, 4, 2, 256, 256),
            buffer(2, 4, 2, 512, 256),
            buffer(2, 2, 256, 256),
            buffer(2, 2, 512, 256),
            buffer(16, 512, 256),
            buffer(4, 2, 256, 256),
            buffer(4, 2, 512, 256),
            buffer(4, 256, 256),
            buffer(4, 256, 256),
            buffer(2, 128, E),
            buffer(2, 256, E),
            buffer(2, 256, E),
            buffer(256, E),
            buffer(256, E),
            buffer(3, 8, 256, kind=F32),
            buffer(8, 256, 256),
            buffer(8, 256, 256),
            buffer(256, 128, kind=F32),
            pltpu.SemaphoreType.DMA((11,)),
            pltpu.SemaphoreType.DMA((8,)),
            pltpu.SemaphoreType.DMA((SENDS,)),
            pltpu.SemaphoreType.DMA((SENDS,)),
        ],
        compiler_params=pltpu.CompilerParams(
            collective_id=1, has_side_effects=True, vmem_limit_bytes=60 * 2**20
        ),
        cost_estimate=pl.CostEstimate(
            flops=4 * 512 * 1024 * 4096, bytes_accessed=20 * 2**20, transcendentals=0
        ),
    )(d_queries, mine, theirs, w_all, grad, sums, tokens, inverse, gain)


def shards(
    tokens,
    w_query,
    query_gain,
    state_kv,
    neighbours,
    enc_gain,
    enc_query,
    enc_out,
    w_key,
    w_value,
    counts,
    d_context,
):
    tensor_count = lax.axis_size("tensor")
    tensor_rank = lax.axis_index("tensor")
    core = lax.axis_index("seq") % 2
    tok_rows, width = tokens.shape
    width_share = width // tensor_count
    enc_in = swapped(neighbours[0], "section", 0)
    hidden = tokens.astype(jnp.float32)
    inverse = lax.rsqrt(jnp.mean(hidden * hidden, axis=-1, keepdims=True) + EPSILON)
    unit_full = hidden * inverse
    unit_rows = unit_full.astype(jnp.bfloat16)
    normed = (unit_full * query_gain).astype(jnp.bfloat16)
    unit_share = lax.dynamic_slice_in_dim(unit_rows, tensor_rank * width_share, width_share, 1)
    state_part = jnp.dot(unit_share, state_kv, preferred_element_type=jnp.float32)
    block_states = lax.psum_scatter(
        state_part.astype(jnp.bfloat16), "tensor", scatter_dimension=0, tiled=True
    )
    encoded_home = encode(enc_in, block_states, enc_gain, enc_query, enc_out)
    encoded_all = lax.all_gather(encoded_home, "tensor", axis=0, tiled=True)
    w_full = lax.all_gather(w_query, ("section", "seq"), axis=0, tiled=True)
    queries = jnp.dot(normed, w_full, preferred_element_type=jnp.float32).astype(jnp.bfloat16)
    context, d_queries, grad, sums = attend(
        counts, queries, encoded_all.reshape(-1, E), w_key, w_value, d_context
    )
    chunks = jnp.transpose(normed.reshape(tok_rows, 16, 2, 256), (2, 1, 0, 3))
    mine = lax.dynamic_index_in_dim(chunks, core, 0, keepdims=False)
    theirs = swapped(lax.dynamic_index_in_dim(chunks, 1 - core, 0, keepdims=False), "seq", 0)
    d_query_weight, d_hidden, d_encoded, row_dots = backward(
        d_queries,
        mine,
        theirs,
        w_full.reshape(16, 2, 256, -1),
        grad,
        jnp.broadcast_to(sums[:, 0][None], (8, tok_rows)),
        tokens,
        inverse,
        query_gain.reshape(32, 1, 256),
    )
    return (
        context,
        d_hidden,
        d_query_weight,
        d_encoded.reshape(1, 1, NBR, RLEN, E),
        row_dots[0],
    )


def solution(mesh):
    return jax.shard_map(
        shards,
        mesh=mesh,
        in_specs=(
            P(("section", "seq"), None),
            P(("section", "seq"), "tensor"),
            P(),
            P("tensor", None),
            P("section", ("seq", "tensor"), None, None, None),
            P(),
            P(),
            P(),
            P(None, "tensor"),
            P(None, "tensor"),
            P(("section", "seq")),
            P(("section", "seq"), "tensor"),
        ),
        out_specs=(
            P(("section", "seq"), "tensor"),
            P(("section", "seq"), "tensor"),
            P(("section", "seq"), "tensor"),
            P("section", ("seq", "tensor"), None, None, None),
            P(("section", "seq")),
        ),
        check_vma=False,
    )
```

```python
import functools
import math

import jax
import jax.numpy as jnp
from jax import lax
from jax.experimental import pallas as pl
from jax.experimental.pallas import tpu as pltpu
from jax.sharding import PartitionSpec as P

HD = 128
E = 896
EHD = 64
BLOCK = 64
NBR = 2
RLEN = 128
KEYS = NBR * RLEN

EPSILON = 1e-05
NEG_LARGE = -1e30
MESH = pl.DeviceIdType.MESH
F32 = jnp.float32
BF16 = jnp.bfloat16
LAST = (((1,), (1,)), ((), ()))
FIRST = (((0,), (0,)), ((), ()))


def dot(a, b, dims=(((1,), (0,)), ((), ()))):
    return lax.dot_general(a, b, dims, preferred_element_type=F32)


def attend_kernel(
    counts, q_ref, k_ref, v_ref, wk_ref, wv_ref, do_ref,
    ctx_ref, dq_ref, grad_ref, sums_ref,
    score_s, dprob_s, weight_s, dscore_s, dk_s, dv_s,
):
    count = counts[pl.program_id(0)]
    heads = q_ref.shape[1] // HD
    valid = lax.broadcasted_iota(jnp.int32, (BLOCK, KEYS), 1) < count * RLEN
    empty = jnp.where(count == 0, 1.0, 0.0).astype(F32)
    scale = 1.0 / math.sqrt(HD)
    spans = [slice(head * HD, (head + 1) * HD) for head in range(heads)]
    for head, cols in enumerate(spans):
        score_s[head] = dot(q_ref[:, cols], k_ref[:, cols], LAST) * scale
        dprob_s[head] = dot(do_ref[:, cols], v_ref[:, cols], LAST)
    for head in range(heads):
        scores = score_s[head]
        top = jnp.max(jnp.where(valid, scores, NEG_LARGE), axis=-1, keepdims=True)
        weights = jnp.where(valid, jnp.exp(scores - top), 0.0)
        probs = weights / (jnp.sum(weights, axis=-1, keepdims=True) + empty)
        weight_s[head] = probs.astype(BF16)
        d_probs = dprob_s[head]
        inner = jnp.sum(probs * d_probs, axis=-1, keepdims=True)
        dscore_s[head] = (probs * (d_probs - inner) * scale).astype(BF16)
    total = jnp.zeros((BLOCK, HD), F32)
    for head, cols in enumerate(spans):
        ctx_ref[:, cols] = dot(weight_s[head], v_ref[:, cols]).astype(BF16)
        dq = dot(dscore_s[head], k_ref[:, cols])
        dq_ref[:, cols] = dq.astype(BF16)
        total = total + dq * q_ref[:, cols].astype(F32)
        dv_s[:, cols] = dot(weight_s[head], do_ref[:, cols], FIRST).astype(BF16)
        dk_s[:, cols] = dot(dscore_s[head], q_ref[:, cols], FIRST).astype(BF16)
    grad = dot(dk_s[...], wk_ref[...], LAST) + dot(dv_s[...], wv_ref[...], LAST)
    grad_ref[0] = grad.astype(BF16)
    sums_ref[...] = jnp.broadcast_to(jnp.sum(total, axis=-1, keepdims=True), (BLOCK, HD))


def attend(counts, queries, keys, values, w_key, w_value, d_context):
    blocks = counts.shape[0]
    rows, width = queries.shape
    heads = width // HD
    row_block = pl.BlockSpec((BLOCK, width), lambda b: (b, 0))
    key_block = pl.BlockSpec((KEYS, width), lambda b: (b, 0))
    weight = pl.BlockSpec((E, width), lambda b: (0, 0))
    flops = 2 * (4 * rows * 2 * E * width + 6 * rows * KEYS * width)
    return pl.pallas_call(
        attend_kernel,
        grid=(blocks,),
        in_specs=[
            pl.BlockSpec(memory_space=pltpu.SMEM),
            row_block,
            key_block,
            key_block,
            weight,
            weight,
            row_block,
        ],
        out_specs=[
            row_block,
            row_block,
            pl.BlockSpec((1, KEYS, E), lambda b: (b, 0, 0)),
            pl.BlockSpec((BLOCK, HD), lambda b: (b, 0)),
        ],
        out_shape=[
            jax.ShapeDtypeStruct((rows, width), BF16),
            jax.ShapeDtypeStruct((rows, width), BF16),
            jax.ShapeDtypeStruct((blocks, KEYS, E), BF16),
            jax.ShapeDtypeStruct((rows, HD), F32),
        ],
        scratch_shapes=[pltpu.VMEM((heads, BLOCK, KEYS), F32)] * 2
        + [pltpu.VMEM((heads, BLOCK, KEYS), BF16)] * 2
        + [pltpu.VMEM((KEYS, width), BF16)] * 2,
        compiler_params=pltpu.CompilerParams(vmem_limit_bytes=50 * 2**20),
        cost_estimate=pl.CostEstimate(
            flops=flops, bytes_accessed=14 * 2**20, transcendentals=rows * 8 * KEYS
        ),
    )(counts, queries, keys, values, w_key, w_value, d_context)


class Place:
    def __init__(self):
        self.section = lax.axis_index("section")
        seq = lax.axis_index("seq")
        self.x = lax.axis_index("tensor")
        self.core = seq % 2
        self.y = seq // 4
        self.z = 2 * ((seq // 2) % 2) + self.section

    def along(self, dim, off):
        if dim == "x":
            return (self.section, self.seq_of(self.y, self.z), (self.x + off) % 4)
        if dim == "y":
            return (self.section, self.seq_of((self.y + off) % 4, self.z), self.x)
        z = (self.z + off) % 4
        return (z % 2, self.seq_of(self.y, z), self.x)

    def seq_of(self, y, z):
        return y * 4 + (z // 2) * 2 + self.core

    def sibling(self):
        return (self.section, self.y * 4 + (self.z // 2) * 2 + 1 - self.core, self.x)

    def partner(self):
        return (1 - self.section, self.seq_of(self.y, self.z), self.x)

    def chunk(self, dy, dz):
        y, z = (self.y + dy) % 4, (self.z + dz) % 4
        return (z % 2) * 8 + y * 2 + z // 2


def greet(devices):
    barrier = pltpu.get_barrier_semaphore()
    for device in devices:
        pl.semaphore_signal(barrier, inc=1, device_id=device, device_id_type=MESH)
    pl.semaphore_wait(barrier, len(devices))


class Sender:
    def __init__(self, send_sem, recv_sem):
        self.send_sem, self.recv_sem, self.copies = send_sem, recv_sem, []

    def __call__(self, src, dst, device):
        index = len(self.copies)
        copy = pltpu.make_async_remote_copy(
            src_ref=src, dst_ref=dst, send_sem=self.send_sem.at[index],
            recv_sem=self.recv_sem.at[index], device_id=device, device_id_type=MESH,
        )
        copy.start()
        self.copies.append(copy)
        return copy


Y_FIRST = 96
CHUNK = 256


def wide(column):
    return jnp.concatenate([column, column], axis=1)


def forward_kernel(
    tokens_ref, w_ref, gain_ref, state_ref, near_ref, egain_ref, equery_ref, eout_ref, wk_ref, wv_ref,
    q_ref, w_out, nrm_out, k_out, v_out, inv_ref,
    tok, wc, nrm, theirs, skv, unit, acc, q_send, q_in,
    sp, sr1, sr2, enc_in, eq_s, ectx, escore, equery, eout, enc, wk, wv, ks, vs,
    load_sem, out_sem, send_sem, recv_sem,
):
    at = Place()
    share = tok.shape[1] // 4
    send = Sender(send_sem, recv_sem)
    me = at.chunk(0, 0)
    pairs = (
        (w_ref, wc.at[me]), (tokens_ref, tok), (state_ref, skv), (equery_ref, equery),
        (eout_ref, eout), (wk_ref, wk), (wv_ref, wv),
    )
    loads = [pltpu.make_async_copy(src, dst, load_sem.at[i]) for i, (src, dst) in enumerate(pairs)]
    for load in loads:
        load.start()
    greet(
        [at.along("x", 1), at.along("x", 3), at.along("y", 1), at.along("y", 3),
         at.along("z", 1), at.along("z", 3), at.sibling()]
    )

    dims = (("y", "z"), ("z", "y"))
    spans = ((0, Y_FIRST), (Y_FIRST, CHUNK))

    def piece(half, first, second, part=None):
        dy, dz = (first, second) if half == 0 else (second, first)
        low, high = spans[half]
        middle = (low + high) // 2
        low, high = (low, high) if part is None else ((low, middle), (middle, high))[part]
        return wc.at[at.chunk(dy, dz), low:high]

    def pass_on(ref, dim, off):
        return send(ref, ref, at.along(dim, off))

    near, relay, cross, last = {}, {}, {}, {}

    def across(half, line):
        dim = dims[half][1]
        block = piece(half, line, 0)
        cross[half, line] = (pass_on(block, dim, 1), pass_on(block, dim, 3))

    def first_round(half):
        dim = dims[half][0]
        near[half][0].wait_recv()
        relay[half] = [pass_on(piece(half, 3, 0, 0), dim, 1)]
        across(half, 3)
        near[half][1].wait_recv()
        relay[half].append(pass_on(piece(half, 1, 0, 1), dim, 3))
        across(half, 1)

    def second_round(half):
        relay[half][0].wait_recv()
        relay[half][1].wait_recv()
        across(half, 2)

    def crossed(half, line):
        dim = dims[half][1]
        cross[half, line][0].wait_recv()
        first = pass_on(piece(half, line, 3, 0), dim, 1)
        cross[half, line][1].wait_recv()
        last[half, line] = (first, pass_on(piece(half, line, 1, 1), dim, 3))

    def landed(half, line):
        last[half, line][0].wait_recv()
        last[half, line][1].wait_recv()

    outs = []

    def write(src, dst):
        copy = pltpu.make_async_copy(src, dst, out_sem.at[len(outs)])
        copy.start()
        outs.append(copy)

    def accumulate(offsets, begin=False):
        chunks = [at.chunk(dy, dz) for dy, dz in offsets]
        for k in chunks:
            write(wc.at[k], w_out.at[k])

        @pl.loop(0, 4)
        def _(i):
            rows = pl.ds(pl.multiple_of((i // 2) * 256, 256), 256)
            cols = pl.ds(pl.multiple_of((i % 2) * 512, 512), 512)
            total = dot(nrm[chunks[0], rows, :], wc[chunks[0], :, cols])
            for k in chunks[1:]:
                total = total + dot(nrm[k, rows, :], wc[k, :, cols])
            acc[rows, cols] = total if begin else acc[rows, cols] + total

    loads[0].wait()
    for half in (0, 1):
        block = piece(half, 0, 0)
        near[half] = (pass_on(block, dims[half][0], 1), pass_on(block, dims[half][0], 3))
    c_near = send(near_ref, enc_in, at.partner())
    for half in (0, 1):
        across(half, 0)

    loads[1].wait()

    @pl.loop(0, 16)
    def _(i):
        rows = pl.ds(pl.multiple_of(i * 16, 16), 16)
        values = tok[rows, :].astype(F32)
        square = jnp.sum(values * values, axis=-1, keepdims=True)
        inverse = lax.rsqrt(square * (1.0 / tok.shape[1]) + EPSILON)
        inv_ref[rows, :] = jnp.broadcast_to(inverse, (16, 128))

    @pl.loop(0, 8)
    def _(i):
        source = pl.ds(pl.multiple_of(at.x * share + i * 256, 256), 256)
        target = pl.ds(pl.multiple_of(i * 256, 256), 256)
        unit[:, target] = (tok[:, source].astype(F32) * wide(inv_ref[...])).astype(BF16)

    loads[2].wait()

    @pl.loop(0, 7)
    def _(i):
        cols = pl.ds(pl.multiple_of(i * 256, 256), 256)
        part = dot(unit[...], skv[:, cols]).astype(BF16)
        for j in range(4):
            sp[j, :, cols] = part[64 * j : 64 * j + 64]

    far, up, down = (at.x + 2) % 4, (at.x + 1) % 4, (at.x + 3) % 4
    c_s1 = (
        send(sp.at[far, 0:32], sr1.at[0], at.along("x", 1)),
        send(sp.at[far, 32:64], sr1.at[1], at.along("x", 3)),
    )
    first_round(0)
    first_round(1)

    @pl.loop(0, 16)
    def _(k):
        def chunk(g):
            cols = pl.ds(pl.multiple_of(g * CHUNK, CHUNK), CHUNK)
            return (tok[:, cols].astype(F32) * wide(inv_ref[...]) * gain_ref[g]).astype(BF16)

        nrm[k, 0:256] = chunk(2 * k + at.core)
        theirs[k] = chunk(2 * k + 1 - at.core)

    c_nrm = send(theirs, nrm.at[:, 256:512], at.sibling())

    for way, block in ((0, up), (1, down)):
        c_s1[way].wait_recv()
        rows = slice(32 * way, 32 * way + 32)
        sp[block, rows] = (sp[block, rows].astype(F32) + sr1[way].astype(F32)).astype(BF16)
    c_s2 = (
        send(sp.at[up], sr2.at[0], at.along("x", 1)),
        send(sp.at[down], sr2.at[1], at.along("x", 3)),
    )
    second_round(0)
    second_round(1)

    loads[3].wait()
    c_near.wait_recv()
    enc_rows = enc_in[...].astype(F32)
    mean = jnp.sum(enc_rows * enc_rows, axis=-1, keepdims=True) * (1.0 / E)
    enc_normed = (enc_rows * lax.rsqrt(mean + EPSILON) * egain_ref[...]).astype(BF16)
    eq_s[...] = dot(enc_normed, equery[...]).astype(BF16)
    for half in (0, 1):
        crossed(half, 0)

    c_s2[0].wait_recv()
    c_s2[1].wait_recv()
    states = (sp[at.x].astype(F32) + sr2[0].astype(F32) + sr2[1].astype(F32)).astype(BF16)
    states = states.astype(F32)
    left = lax.broadcasted_iota(jnp.int32, (BLOCK, 128), 1) < EHD
    left_wide = lax.broadcasted_iota(jnp.int32, (KEYS, 128), 1) < EHD

    def doubled(cols):
        both = states[:, cols]
        return jnp.concatenate(
            [jnp.where(left, both, 0.0), jnp.where(left, 0.0, both)], axis=0
        ).astype(BF16)

    for j in range(7):
        keys = doubled(slice(128 * j, 128 * j + 128))
        escore[j] = dot(eq_s[:, 128 * j : 128 * j + 128], keys, LAST) * (1.0 / math.sqrt(EHD))
    for j in range(7):
        scores = escore[j]
        top_left = jnp.max(jnp.where(left_wide, scores, NEG_LARGE), axis=-1, keepdims=True)
        top_right = jnp.max(jnp.where(left_wide, NEG_LARGE, scores), axis=-1, keepdims=True)
        weights = jnp.exp(scores - jnp.where(left_wide, top_left, top_right))
        sum_left = jnp.sum(jnp.where(left_wide, weights, 0.0), axis=-1, keepdims=True)
        sum_right = jnp.sum(jnp.where(left_wide, 0.0, weights), axis=-1, keepdims=True)
        escore[j] = weights / jnp.where(left_wide, sum_left, sum_right)
    for j in range(7):
        values = doubled(slice(E + 128 * j, E + 128 * j + 128))
        ectx[:, 128 * j : 128 * j + 128] = dot(escore[j].astype(BF16), values).astype(BF16)
    loads[4].wait()
    enc[at.x] = (enc_in[...].astype(F32) + dot(ectx[...], eout[...])).astype(BF16)
    c_e1 = (
        send(enc.at[at.x], enc.at[at.x], at.along("x", 1)),
        send(enc.at[at.x], enc.at[at.x], at.along("x", 3)),
    )
    loads[5].wait()
    loads[6].wait()

    def project(block):
        @pl.loop(0, 4)
        def _(i):
            cols = pl.ds(pl.multiple_of(i * 256, 256), 256)
            ks[block, :, cols] = dot(enc[block], wk[:, cols]).astype(BF16)
            vs[block, :, cols] = dot(enc[block], wv[:, cols]).astype(BF16)

        write(ks.at[block], k_out.at[block])
        write(vs.at[block], v_out.at[block])

    c_nrm.wait_recv()
    write(nrm, nrm_out)
    accumulate([(0, 0), (1, 0), (3, 0), (0, 1), (0, 3)], begin=True)
    for line in (3, 1):
        for half in (0, 1):
            crossed(half, line)
    project(at.x)
    c_e1[0].wait_recv()
    c_e2 = [send(enc.at[down, 0:128], enc.at[down, 0:128], at.along("x", 1))]
    c_e1[1].wait_recv()
    c_e2.append(send(enc.at[up, 128:256], enc.at[up, 128:256], at.along("x", 3)))
    project(down)
    project(up)
    accumulate([(1, 1), (1, 3), (3, 1), (3, 3)])
    for half in (0, 1):
        crossed(half, 2)
    landed(0, 0)
    landed(1, 0)
    accumulate([(2, 0), (0, 2)])
    c_e2[0].wait_recv()
    c_e2[1].wait_recv()
    project(far)
    for line in (3, 1):
        landed(0, line)
        landed(1, line)
    accumulate([(2, 1), (2, 3), (1, 2), (3, 2)])
    landed(0, 2)
    landed(1, 2)
    accumulate([(2, 2)])
    q_send[...] = acc[256:512].astype(BF16)
    c_q = send(q_send, q_in, at.sibling())
    c_q.wait_recv()
    q_ref[...] = (acc[0:256] + q_in[...].astype(F32)).astype(BF16)
    for copy in send.copies:
        copy.wait_send()
    for copy in outs:
        copy.wait()


FORWARD_SENDS = 4 + 1 + 4 + 2 * 6 + 2 * 2 + 16 + 2 + 2 + 1 + 2 + 2 + 1


def forward(tokens, w_query, gain, state_kv, near, enc_gain, enc_query, enc_out, w_key, w_value):
    rows, full = tokens.shape
    width = w_query.shape[1]
    vmem = pl.BlockSpec(memory_space=pltpu.VMEM)
    anywhere = pl.BlockSpec(memory_space=pl.ANY)

    def buffer(*shape, kind=BF16):
        return pltpu.VMEM(shape, kind)

    return pl.pallas_call(
        forward_kernel,
        in_specs=[anywhere, anywhere, vmem, anywhere, anywhere, vmem] + [anywhere] * 4,
        out_specs=[vmem] + [anywhere] * 4 + [vmem],
        out_shape=[
            jax.ShapeDtypeStruct((rows, width), BF16),
            jax.ShapeDtypeStruct((16, CHUNK, width), BF16),
            jax.ShapeDtypeStruct((16, 2 * rows, CHUNK), BF16),
            jax.ShapeDtypeStruct((4, KEYS, width), BF16),
            jax.ShapeDtypeStruct((4, KEYS, width), BF16),
            jax.ShapeDtypeStruct((rows, 128), F32),
        ],
        scratch_shapes=[
            buffer(rows, full),
            buffer(16, CHUNK, width),
            buffer(16, 2 * rows, CHUNK),
            buffer(16, rows, CHUNK),
            buffer(full // 4, 2 * E),
            buffer(rows, full // 4),
            buffer(2 * rows, width, kind=F32),
            buffer(rows, width),
            buffer(rows, width),
            buffer(4, BLOCK, 2 * E),
            buffer(2, BLOCK // 2, 2 * E),
            buffer(2, BLOCK, 2 * E),
            buffer(KEYS, E),
            buffer(KEYS, E),
            buffer(KEYS, E),
            buffer(7, KEYS, 128, kind=F32),
            buffer(E, E),
            buffer(E, E),
            buffer(4, KEYS, E),
            buffer(E, width),
            buffer(E, width),
            buffer(4, KEYS, width),
            buffer(4, KEYS, width),
            pltpu.SemaphoreType.DMA((7,)),
            pltpu.SemaphoreType.DMA((25,)),
            pltpu.SemaphoreType.DMA((FORWARD_SENDS,)),
            pltpu.SemaphoreType.DMA((FORWARD_SENDS,)),
        ],
        compiler_params=pltpu.CompilerParams(
            collective_id=2, has_side_effects=True, vmem_limit_bytes=60 * 2**20
        ),
        cost_estimate=pl.CostEstimate(
            flops=2 * 5400 * 2**20, bytes_accessed=40 * 2**20, transcendentals=0
        ),
    )(tokens, w_query, gain, state_kv, near, enc_gain, enc_query, enc_out, w_key, w_value)


LINES = (2, 1, 3, 0)


def backward_kernel(
    dq_ref, nrm_ref, w_ref, grad_ref, sums_ref, tokens_ref, inverse_ref, gain_ref,
    dw_ref, dh_ref, de_ref, dots_ref,
    dq2, dq_t, nrm, wc, prod, ra1, ra2, rb1, rb2, part, rn1, rn2, out_sib, in_sib,
    g1, gs, g2, gfin, gin, sums_in, tok, dh_s, column,
    load_sem, dh_sem, send_sem, recv_sem,
):
    at = Place()
    width = tokens_ref.shape[1]
    share = width // 4
    loads = [
        pltpu.make_async_copy(nrm_ref, nrm, load_sem.at[0]),
        pltpu.make_async_copy(w_ref, wc, load_sem.at[1]),
    ]
    for i in range(8):
        first = pl.multiple_of(at.x * share + i * 256, 256)
        loads.append(
            pltpu.make_async_copy(tokens_ref.at[:, pl.ds(first, 256)], tok.at[i], load_sem.at[2 + i])
        )
    for load in loads:
        load.start()
    greet(
        [at.along("x", 1), at.along("x", 2), at.along("x", 3), at.along("y", 1), at.along("y", 3),
         at.along("z", 1), at.along("z", 3), at.sibling()]
    )

    send = Sender(send_sem, recv_sem)

    def added(dst, first, second):
        dst[...] = (first[...].astype(F32) + second[...].astype(F32)).astype(BF16)

    c_dq = send(dq_ref, dq2.at[256:512], at.sibling())
    far = (at.x + 2) % 4
    up, down = (at.x + 1) % 4, (at.x + 3) % 4
    c_g1 = [
        send(grad_ref.at[far, 0:128], g1.at[0], at.along("x", 1)),
        send(grad_ref.at[far, 128:256], g1.at[1], at.along("x", 3)),
    ]
    c_sums = [send(sums_ref, sums_in.at[i], at.along("x", i + 1)) for i in range(3)]
    dq2[0:256] = dq_ref[...]
    for j in range(4):
        dq_t[256 * j : 256 * j + 256, 0:256] = jnp.transpose(dq_ref[:, 256 * j : 256 * j + 256])
    c_dq.wait_recv()
    for j in range(4):
        dq_t[256 * j : 256 * j + 256, 256:512] = jnp.transpose(
            dq2[256:512, 256 * j : 256 * j + 256]
        )
    loads[0].wait()

    def product(dy, dz):
        k = at.chunk(dy, dz)

        @pl.loop(0, 4)
        def _(i):
            rows = pl.ds(pl.multiple_of(i * 256, 256), 256)
            prod[k, rows, :] = dot(dq_t[rows, :], nrm[k]).astype(BF16)

    dims = (("z", "y"), ("y", "z"))

    def block(half, line, off, low=0, high=512):
        dy, dz = (line, off) if half == 0 else (off, line)
        return prod.at[at.chunk(dy, dz), half * 512 + low : half * 512 + high]

    c1 = {}

    def first_hop(half, line):
        dim = dims[half][0]
        slot = LINES.index(line)
        c1[half, line] = (
            send(block(half, line, 2, 0, 256), ra1.at[half, slot, 0], at.along(dim, 1)),
            send(block(half, line, 2, 256, 512), ra1.at[half, slot, 1], at.along(dim, 3)),
        )

    product(2, 2)
    first_hop(0, 2)
    first_hop(1, 2)
    for line in (1, 3, 0):
        product(line, 2)
        first_hop(0, line)
        product(2, line)
        first_hop(1, line)
    for dy in (1, 3, 0):
        for dz in (1, 3, 0):
            product(dy, dz)

    c_g1[0].wait_recv()
    c_g1[1].wait_recv()
    gs[0, 0:128] = (grad_ref[up, 0:128].astype(F32) + g1[0].astype(F32)).astype(BF16)
    gs[0, 128:256] = grad_ref[up, 128:256]
    gs[1, 0:128] = grad_ref[down, 0:128]
    gs[1, 128:256] = (grad_ref[down, 128:256].astype(F32) + g1[1].astype(F32)).astype(BF16)
    c_g2 = [
        send(gs.at[0], g2.at[0], at.along("x", 1)),
        send(gs.at[1], g2.at[1], at.along("x", 3)),
    ]

    c2 = {}

    def second_hop(half, line):
        dim = dims[half][0]
        slot = LINES.index(line)
        for way, off in ((0, 1), (1, 3)):
            c1[half, line][way].wait_recv()
            piece = block(half, line, off, 256 * way, 256 * way + 256)
            added(piece, piece, ra1.at[half, slot, way])
        c2[half, line] = (
            send(block(half, line, 1), ra2.at[half, slot, 0], at.along(dim, 1)),
            send(block(half, line, 3), ra2.at[half, slot, 1], at.along(dim, 3)),
        )

    def partial(k):
        @pl.loop(0, 2)
        def _(i):
            rows = pl.ds(pl.multiple_of(i * 256, 256), 256)
            part[k, rows, :] = dot(dq2[rows, :], wc[k], LAST).astype(BF16)

    n1, n2 = [], []
    loads[1].wait()
    second_hop(0, 2)
    second_hop(1, 2)
    for m in range(4):
        partial(far * 4 + m)
        n1.append(
            (
                send(part.at[far * 4 + m, 0:256], rn1.at[m, 0], at.along("x", 1)),
                send(part.at[far * 4 + m, 256:512], rn1.at[m, 1], at.along("x", 3)),
            )
        )
        if m > 0:
            second_hop(0, LINES[m])
            second_hop(1, LINES[m])

    for copy in c_sums:
        copy.wait_recv()
    sums = sums_ref[...] + sums_in[0] + sums_in[1] + sums_in[2]
    dots_ref[...] = sums * (1.0 / math.sqrt(width))
    column[...] = jnp.transpose(jnp.broadcast_to(sums[0:1], (128, 256)))

    for m in range(4):
        partial(up * 4 + m)
        partial(down * 4 + m)
        partial(at.x * 4 + m)
    for m in range(4):
        n1[m][0].wait_recv()
        piece = part.at[up * 4 + m, 0:256]
        added(piece, piece, rn1.at[m, 0])
        n1[m][1].wait_recv()
        piece = part.at[down * 4 + m, 256:512]
        added(piece, piece, rn1.at[m, 1])
        n2.append(
            (
                send(part.at[up * 4 + m], rn2.at[m, 0], at.along("x", 1)),
                send(part.at[down * 4 + m], rn2.at[m, 1], at.along("x", 3)),
            )
        )

    for copy in c_g2:
        copy.wait_recv()
    gfin[...] = (grad_ref[at.x].astype(F32) + g2[0].astype(F32) + g2[1].astype(F32)).astype(BF16)
    c_swap = send(gfin, gin, at.partner())

    def gathered(half, line):
        for way in (0, 1):
            c2[half, line][way].wait_recv()
        slot = LINES.index(line)
        piece = block(half, line, 0)
        total = piece[...].astype(F32) + ra2[half, slot, 0].astype(F32)
        piece[...] = (total + ra2[half, slot, 1].astype(F32)).astype(BF16)

    for load in loads[2:]:
        load.wait()
    stores = []

    def finish(i, d_normed):
        inverse = wide(inverse_ref[...])
        unit = tok[i].astype(F32) * inverse
        rows = wide(column[...])
        grads = d_normed * gain_ref[at.x * 8 + i]
        result = inverse * (grads - unit * (rows * (1.0 / width)))
        dh_s[i] = result.astype(BF16)
        first = pl.multiple_of(i * 256, 256)
        store = pltpu.make_async_copy(
            dh_s.at[i], dh_ref.at[:, pl.ds(first, 256)], dh_sem.at[len(stores)]
        )
        store.start()
        stores.append(store)

    c_sib = []

    def normed_sum(m):
        for copy in n2[m]:
            copy.wait_recv()

        def summed(low):
            rows = slice(low, low + 256)
            total = part[at.x * 4 + m, rows].astype(F32) + rn2[m, 0, rows].astype(F32)
            return total + rn2[m, 1, rows].astype(F32)

        out_sib[m] = summed(256).astype(BF16)
        c_sib.append(send(out_sib.at[m], in_sib.at[m], at.sibling()))
        finish(2 * m + at.core, summed(0))

    d1, d2 = {}, {}

    def turn(half):
        dim = dims[half][1]
        d1[half] = (
            send(block(half, 2, 0, 0, 256), rb1.at[half, 0], at.along(dim, 1)),
            send(block(half, 2, 0, 256, 512), rb1.at[half, 1], at.along(dim, 3)),
        )

    def turned(half):
        dim = dims[half][1]
        for way, off in ((0, 1), (1, 3)):
            d1[half][way].wait_recv()
            piece = block(half, off, 0, 256 * way, 256 * way + 256)
            added(piece, piece, rb1.at[half, way])
        d2[half] = (
            send(block(half, 1, 0), rb2.at[half, 0], at.along(dim, 1)),
            send(block(half, 3, 0), rb2.at[half, 1], at.along(dim, 3)),
        )

    def result(half):
        for way in (0, 1):
            c2[half, 0][way].wait_recv()
            d2[half][way].wait_recv()
        for low in (0, 256):
            rows = slice(low, low + 256)
            total = block(half, 0, 0)[rows].astype(F32)
            for extra in (ra2.at[half, 3, 0], ra2.at[half, 3, 1], rb2.at[half, 0], rb2.at[half, 1]):
                total = total + extra[rows].astype(F32)
            first = half * 512 + low
            dw_ref[:, first : first + 256] = jnp.transpose(total)

    for half in (0, 1):
        gathered(half, 2)
        turn(half)
    normed_sum(0)
    for half in (0, 1):
        gathered(half, 1)
    normed_sum(1)
    for half in (0, 1):
        gathered(half, 3)
    for half in (0, 1):
        turned(half)
    normed_sum(2)
    for half in (0, 1):
        result(half)
    normed_sum(3)
    for m in range(4):
        c_sib[m].wait_recv()
        finish(2 * m + 1 - at.core, in_sib[m].astype(F32))
    c_swap.wait_recv()
    de_ref[...] = gin[...]
    for copy in send.copies:
        copy.wait_send()
    for store in stores:
        store.wait()


SENDS = 1 + 2 + 3 + 16 + 2 + 16 + 8 + 8 + 1 + 4 + 8


def backward(d_queries, normed, w_all, grad, sums, tokens, inverse, gain):
    rows, width = d_queries.shape
    full = tokens.shape[1]
    vmem = pl.BlockSpec(memory_space=pltpu.VMEM)
    anywhere = pl.BlockSpec(memory_space=pl.ANY)

    def buffer(*shape, kind=BF16):
        return pltpu.VMEM(shape, kind)

    return pl.pallas_call(
        backward_kernel,
        in_specs=[vmem, anywhere, anywhere, vmem, vmem, anywhere, vmem, vmem],
        out_specs=[vmem, anywhere, vmem, vmem],
        out_shape=[
            jax.ShapeDtypeStruct((256, width), F32),
            jax.ShapeDtypeStruct((rows, full // 4), BF16),
            jax.ShapeDtypeStruct((KEYS, E), BF16),
            jax.ShapeDtypeStruct((8, rows), F32),
        ],
        scratch_shapes=[
            buffer(512, 1024),
            buffer(1024, 512),
            buffer(16, 512, 256),
            buffer(16, 256, 1024),
            buffer(16, 1024, 256),
            buffer(2, 4, 2, 256, 256),
            buffer(2, 4, 2, 512, 256),
            buffer(2, 2, 256, 256),
            buffer(2, 2, 512, 256),
            buffer(16, 512, 256),
            buffer(4, 2, 256, 256),
            buffer(4, 2, 512, 256),
            buffer(4, 256, 256),
            buffer(4, 256, 256),
            buffer(2, 128, E),
            buffer(2, 256, E),
            buffer(2, 256, E),
            buffer(256, E),
            buffer(256, E),
            buffer(3, 8, 256, kind=F32),
            buffer(8, 256, 256),
            buffer(8, 256, 256),
            buffer(256, 128, kind=F32),
            pltpu.SemaphoreType.DMA((10,)),
            pltpu.SemaphoreType.DMA((8,)),
            pltpu.SemaphoreType.DMA((SENDS,)),
            pltpu.SemaphoreType.DMA((SENDS,)),
        ],
        compiler_params=pltpu.CompilerParams(
            collective_id=1, has_side_effects=True, vmem_limit_bytes=60 * 2**20
        ),
        cost_estimate=pl.CostEstimate(
            flops=4 * 512 * 1024 * 4096, bytes_accessed=20 * 2**20, transcendentals=0
        ),
    )(d_queries, normed, w_all, grad, sums, tokens, inverse, gain)


def shards(
    tokens,
    w_query,
    query_gain,
    state_kv,
    neighbours,
    enc_gain,
    enc_query,
    enc_out,
    w_key,
    w_value,
    counts,
    d_context,
):
    tok_rows = tokens.shape[0]
    gain = query_gain.reshape(32, 1, 256)
    queries, w_part, normed, keys, values, inverse = forward(
        tokens, w_query, gain, state_kv, neighbours.reshape(KEYS, E), enc_gain.reshape(1, E),
        enc_query, enc_out, w_key, w_value,
    )
    context, d_queries, grad, sums = attend(
        counts, queries, keys.reshape(4 * KEYS, -1), values.reshape(4 * KEYS, -1),
        w_key, w_value, d_context,
    )
    d_query_weight, d_hidden, d_encoded, row_dots = backward(
        d_queries, normed, w_part, grad,
        jnp.broadcast_to(sums[:, 0][None], (8, tok_rows)),
        tokens, inverse, gain,
    )
    return (
        context,
        d_hidden,
        d_query_weight,
        d_encoded.reshape(1, 1, NBR, RLEN, E),
        row_dots[0],
    )


def solution(mesh):
    return jax.shard_map(
        shards,
        mesh=mesh,
        in_specs=(
            P(("section", "seq"), None),
            P(("section", "seq"), "tensor"),
            P(),
            P("tensor", None),
            P("section", ("seq", "tensor"), None, None, None),
            P(),
            P(),
            P(),
            P(None, "tensor"),
            P(None, "tensor"),
            P(("section", "seq")),
            P(("section", "seq"), "tensor"),
        ),
        out_specs=(
            P(("section", "seq"), "tensor"),
            P(("section", "seq"), "tensor"),
            P(("section", "seq"), "tensor"),
            P("section", ("seq", "tensor"), None, None, None),
            P(("section", "seq")),
        ),
        check_vma=False,
    )
```

```python
import functools
import math

import jax
import jax.numpy as jnp
from jax import lax
from jax.experimental import pallas as pl
from jax.experimental.pallas import tpu as pltpu
from jax.sharding import PartitionSpec as P

HD = 128
E = 896
EHD = 64
BLOCK = 64
NBR = 2
RLEN = 128
KEYS = NBR * RLEN

EPSILON = 1e-05
NEG_LARGE = -1e30
MESH = pl.DeviceIdType.MESH
F32 = jnp.float32
BF16 = jnp.bfloat16
LAST = (((1,), (1,)), ((), ()))
FIRST = (((0,), (0,)), ((), ()))


def dot(a, b, dims=(((1,), (0,)), ((), ()))):
    return lax.dot_general(a, b, dims, preferred_element_type=F32)


def attend_kernel(
    counts, q_ref, k_ref, v_ref, wk_ref, wv_ref, do_ref,
    ctx_ref, dq_ref, grad_ref, sums_ref,
    score_s, dprob_s, weight_s, dscore_s, dk_s, dv_s,
):
    count = counts[pl.program_id(0)]
    heads = q_ref.shape[1] // HD
    valid = lax.broadcasted_iota(jnp.int32, (BLOCK, KEYS), 1) < count * RLEN
    empty = jnp.where(count == 0, 1.0, 0.0).astype(F32)
    scale = 1.0 / math.sqrt(HD)
    spans = [slice(head * HD, (head + 1) * HD) for head in range(heads)]
    for head, cols in enumerate(spans):
        score_s[head] = dot(q_ref[:, cols], k_ref[:, cols], LAST) * scale
        dprob_s[head] = dot(do_ref[:, cols], v_ref[:, cols], LAST)
    for head in range(heads):
        scores = score_s[head]
        top = jnp.max(jnp.where(valid, scores, NEG_LARGE), axis=-1, keepdims=True)
        weights = jnp.where(valid, jnp.exp(scores - top), 0.0)
        probs = weights / (jnp.sum(weights, axis=-1, keepdims=True) + empty)
        weight_s[head] = probs.astype(BF16)
        d_probs = dprob_s[head]
        inner = jnp.sum(probs * d_probs, axis=-1, keepdims=True)
        dscore_s[head] = (probs * (d_probs - inner) * scale).astype(BF16)
    total = jnp.zeros((BLOCK, HD), F32)
    for head, cols in enumerate(spans):
        ctx_ref[:, cols] = dot(weight_s[head], v_ref[:, cols]).astype(BF16)
        dq = dot(dscore_s[head], k_ref[:, cols])
        dq_ref[:, cols] = dq.astype(BF16)
        total = total + dq * q_ref[:, cols].astype(F32)
        dv_s[:, cols] = dot(weight_s[head], do_ref[:, cols], FIRST).astype(BF16)
        dk_s[:, cols] = dot(dscore_s[head], q_ref[:, cols], FIRST).astype(BF16)
    grad = dot(dk_s[...], wk_ref[...], LAST) + dot(dv_s[...], wv_ref[...], LAST)
    grad_ref[0] = grad.astype(BF16)
    sums_ref[...] = jnp.broadcast_to(jnp.sum(total, axis=-1, keepdims=True), (BLOCK, HD))


def attend(counts, queries, keys, values, w_key, w_value, d_context):
    blocks = counts.shape[0]
    rows, width = queries.shape
    heads = width // HD
    row_block = pl.BlockSpec((BLOCK, width), lambda b: (b, 0))
    key_block = pl.BlockSpec((KEYS, width), lambda b: (b, 0))
    weight = pl.BlockSpec((E, width), lambda b: (0, 0))
    flops = 2 * (4 * rows * 2 * E * width + 6 * rows * KEYS * width)
    return pl.pallas_call(
        attend_kernel,
        grid=(blocks,),
        in_specs=[
            pl.BlockSpec(memory_space=pltpu.SMEM),
            row_block,
            key_block,
            key_block,
            weight,
            weight,
            row_block,
        ],
        out_specs=[
            row_block,
            row_block,
            pl.BlockSpec((1, KEYS, E), lambda b: (b, 0, 0)),
            pl.BlockSpec((BLOCK, HD), lambda b: (b, 0)),
        ],
        out_shape=[
            jax.ShapeDtypeStruct((rows, width), BF16),
            jax.ShapeDtypeStruct((rows, width), BF16),
            jax.ShapeDtypeStruct((blocks, KEYS, E), BF16),
            jax.ShapeDtypeStruct((rows, HD), F32),
        ],
        scratch_shapes=[pltpu.VMEM((heads, BLOCK, KEYS), F32)] * 2
        + [pltpu.VMEM((heads, BLOCK, KEYS), BF16)] * 2
        + [pltpu.VMEM((KEYS, width), BF16)] * 2,
        compiler_params=pltpu.CompilerParams(vmem_limit_bytes=50 * 2**20),
        cost_estimate=pl.CostEstimate(
            flops=flops, bytes_accessed=14 * 2**20, transcendentals=rows * 8 * KEYS
        ),
    )(counts, queries, keys, values, w_key, w_value, d_context)


class Place:
    def __init__(self):
        self.section = lax.axis_index("section")
        seq = lax.axis_index("seq")
        self.x = lax.axis_index("tensor")
        self.core = seq % 2
        self.y = seq // 4
        self.z = 2 * ((seq // 2) % 2) + self.section

    def along(self, dim, off):
        if dim == "x":
            return (self.section, self.seq_of(self.y, self.z), (self.x + off) % 4)
        if dim == "y":
            return (self.section, self.seq_of((self.y + off) % 4, self.z), self.x)
        z = (self.z + off) % 4
        return (z % 2, self.seq_of(self.y, z), self.x)

    def seq_of(self, y, z):
        return y * 4 + (z // 2) * 2 + self.core

    def sibling(self):
        return (self.section, self.y * 4 + (self.z // 2) * 2 + 1 - self.core, self.x)

    def partner(self):
        return (1 - self.section, self.seq_of(self.y, self.z), self.x)

    def chunk(self, dy, dz):
        y, z = (self.y + dy) % 4, (self.z + dz) % 4
        return (z % 2) * 8 + y * 2 + z // 2


def greet(devices):
    barrier = pltpu.get_barrier_semaphore()
    for device in devices:
        pl.semaphore_signal(barrier, inc=1, device_id=device, device_id_type=MESH)
    pl.semaphore_wait(barrier, len(devices))


class Sender:
    def __init__(self, send_sem, recv_sem):
        self.send_sem, self.recv_sem, self.copies = send_sem, recv_sem, []

    def __call__(self, src, dst, device):
        index = len(self.copies)
        copy = pltpu.make_async_remote_copy(
            src_ref=src, dst_ref=dst, send_sem=self.send_sem.at[index],
            recv_sem=self.recv_sem.at[index], device_id=device, device_id_type=MESH,
        )
        copy.start()
        self.copies.append(copy)
        return copy


Y_FIRST = 96
CHUNK = 256


def wide(column):
    return jnp.concatenate([column, column], axis=1)


def forward_kernel(
    tokens_ref, w_ref, gain_ref, state_ref, near_ref, egain_ref, equery_ref, eout_ref, wk_ref, wv_ref,
    q_ref, w_out, nrm_out, k_out, v_out, inv_ref,
    tok, wc, nrm, theirs, skv, unit, acc, q_send, q_in,
    sp, sr1, sr2, enc_in, eq_s, ectx, escore, equery, eout, enc, wk, wv, ks, vs,
    load_sem, out_sem, send_sem, recv_sem,
):
    at = Place()
    share = tok.shape[1] // 4
    send = Sender(send_sem, recv_sem)
    me = at.chunk(0, 0)
    pairs = (
        (w_ref, wc.at[me]), (tokens_ref, tok), (state_ref, skv), (equery_ref, equery),
        (eout_ref, eout), (wk_ref, wk), (wv_ref, wv),
    )
    loads = [pltpu.make_async_copy(src, dst, load_sem.at[i]) for i, (src, dst) in enumerate(pairs)]
    for load in loads:
        load.start()
    greet(
        [at.along("x", 1), at.along("x", 3), at.along("y", 1), at.along("y", 3),
         at.along("z", 1), at.along("z", 3), at.sibling()]
    )

    dims = (("y", "z"), ("z", "y"))
    spans = ((0, Y_FIRST), (Y_FIRST, CHUNK))

    def piece(half, first, second, part=None):
        dy, dz = (first, second) if half == 0 else (second, first)
        low, high = spans[half]
        middle = (low + high) // 2
        low, high = (low, high) if part is None else ((low, middle), (middle, high))[part]
        return wc.at[at.chunk(dy, dz), low:high]

    def pass_on(ref, dim, off):
        return send(ref, ref, at.along(dim, off))

    near, relay, cross, last = {}, {}, {}, {}

    def across(half, line):
        dim = dims[half][1]
        block = piece(half, line, 0)
        cross[half, line] = (pass_on(block, dim, 1), pass_on(block, dim, 3))

    def relays(half):
        dim = dims[half][0]
        near[half][0].wait_recv()
        first = pass_on(piece(half, 3, 0, 0), dim, 1)
        near[half][1].wait_recv()
        relay[half] = (first, pass_on(piece(half, 1, 0, 1), dim, 3))

    def relayed(half):
        relay[half][0].wait_recv()
        relay[half][1].wait_recv()
        across(half, 2)

    def crossed(half, line):
        dim = dims[half][1]
        cross[half, line][0].wait_recv()
        first = pass_on(piece(half, line, 3, 0), dim, 1)
        cross[half, line][1].wait_recv()
        last[half, line] = (first, pass_on(piece(half, line, 1, 1), dim, 3))

    def landed(half, line):
        last[half, line][0].wait_recv()
        last[half, line][1].wait_recv()

    outs = []

    def write(src, dst):
        copy = pltpu.make_async_copy(src, dst, out_sem.at[len(outs)])
        copy.start()
        outs.append(copy)

    def accumulate(offsets, begin=False):
        chunks = [at.chunk(dy, dz) for dy, dz in offsets]
        for k in chunks:
            write(wc.at[k], w_out.at[k])

        @pl.loop(0, 4)
        def _(i):
            rows = pl.ds(pl.multiple_of((i // 2) * 256, 256), 256)
            cols = pl.ds(pl.multiple_of((i % 2) * 512, 512), 512)
            total = dot(nrm[chunks[0], rows, :], wc[chunks[0], :, cols])
            for k in chunks[1:]:
                total = total + dot(nrm[k, rows, :], wc[k, :, cols])
            acc[rows, cols] = total if begin else acc[rows, cols] + total

    loads[0].wait()
    for half in (0, 1):
        block = piece(half, 0, 0)
        near[half] = (pass_on(block, dims[half][0], 1), pass_on(block, dims[half][0], 3))
    c_near = send(near_ref, enc_in, at.partner())
    across(1, 0)

    loads[1].wait()

    @pl.loop(0, 16)
    def _(i):
        rows = pl.ds(pl.multiple_of(i * 16, 16), 16)
        values = tok[rows, :].astype(F32)
        square = jnp.sum(values * values, axis=-1, keepdims=True)
        inverse = lax.rsqrt(square * (1.0 / tok.shape[1]) + EPSILON)
        inv_ref[rows, :] = jnp.broadcast_to(inverse, (16, 128))

    @pl.loop(0, 8)
    def _(i):
        source = pl.ds(pl.multiple_of(at.x * share + i * 256, 256), 256)
        target = pl.ds(pl.multiple_of(i * 256, 256), 256)
        unit[:, target] = (tok[:, source].astype(F32) * wide(inv_ref[...])).astype(BF16)

    loads[2].wait()

    @pl.loop(0, 7)
    def _(i):
        cols = pl.ds(pl.multiple_of(i * 256, 256), 256)
        part = dot(unit[...], skv[:, cols]).astype(BF16)
        for j in range(4):
            sp[j, :, cols] = part[64 * j : 64 * j + 64]

    far, up, down = (at.x + 2) % 4, (at.x + 1) % 4, (at.x + 3) % 4
    c_s1 = (
        send(sp.at[far, 0:32], sr1.at[0], at.along("x", 1)),
        send(sp.at[far, 32:64], sr1.at[1], at.along("x", 3)),
    )
    relays(0)
    relays(1)
    across(1, 3)
    across(1, 1)
    for line in (0, 3, 1):
        across(0, line)

    @pl.loop(0, 16)
    def _(k):
        def chunk(g):
            cols = pl.ds(pl.multiple_of(g * CHUNK, CHUNK), CHUNK)
            return (tok[:, cols].astype(F32) * wide(inv_ref[...]) * gain_ref[g]).astype(BF16)

        nrm[k, 0:256] = chunk(2 * k + at.core)
        theirs[k] = chunk(2 * k + 1 - at.core)

    c_nrm = send(theirs, nrm.at[:, 256:512], at.sibling())

    for way, block in ((0, up), (1, down)):
        c_s1[way].wait_recv()
        rows = slice(32 * way, 32 * way + 32)
        sp[block, rows] = (sp[block, rows].astype(F32) + sr1[way].astype(F32)).astype(BF16)
    c_s2 = (
        send(sp.at[up], sr2.at[0], at.along("x", 1)),
        send(sp.at[down], sr2.at[1], at.along("x", 3)),
    )
    relayed(0)
    crossed(1, 0)

    loads[3].wait()
    c_near.wait_recv()
    enc_rows = enc_in[...].astype(F32)
    mean = jnp.sum(enc_rows * enc_rows, axis=-1, keepdims=True) * (1.0 / E)
    enc_normed = (enc_rows * lax.rsqrt(mean + EPSILON) * egain_ref[...]).astype(BF16)
    eq_s[...] = dot(enc_normed, equery[...]).astype(BF16)

    c_s2[0].wait_recv()
    c_s2[1].wait_recv()
    states = (sp[at.x].astype(F32) + sr2[0].astype(F32) + sr2[1].astype(F32)).astype(BF16)
    states = states.astype(F32)
    left = lax.broadcasted_iota(jnp.int32, (BLOCK, 128), 1) < EHD
    left_wide = lax.broadcasted_iota(jnp.int32, (KEYS, 128), 1) < EHD

    def doubled(cols):
        both = states[:, cols]
        return jnp.concatenate(
            [jnp.where(left, both, 0.0), jnp.where(left, 0.0, both)], axis=0
        ).astype(BF16)

    for j in range(7):
        keys = doubled(slice(128 * j, 128 * j + 128))
        escore[j] = dot(eq_s[:, 128 * j : 128 * j + 128], keys, LAST) * (1.0 / math.sqrt(EHD))
    for j in range(7):
        scores = escore[j]
        top_left = jnp.max(jnp.where(left_wide, scores, NEG_LARGE), axis=-1, keepdims=True)
        top_right = jnp.max(jnp.where(left_wide, NEG_LARGE, scores), axis=-1, keepdims=True)
        weights = jnp.exp(scores - jnp.where(left_wide, top_left, top_right))
        sum_left = jnp.sum(jnp.where(left_wide, weights, 0.0), axis=-1, keepdims=True)
        sum_right = jnp.sum(jnp.where(left_wide, 0.0, weights), axis=-1, keepdims=True)
        escore[j] = weights / jnp.where(left_wide, sum_left, sum_right)
    for j in range(7):
        values = doubled(slice(E + 128 * j, E + 128 * j + 128))
        ectx[:, 128 * j : 128 * j + 128] = dot(escore[j].astype(BF16), values).astype(BF16)
    loads[4].wait()
    enc[at.x] = (enc_in[...].astype(F32) + dot(ectx[...], eout[...])).astype(BF16)
    c_e1 = (
        send(enc.at[at.x], enc.at[at.x], at.along("x", 1)),
        send(enc.at[at.x], enc.at[at.x], at.along("x", 3)),
    )
    relayed(1)
    loads[5].wait()
    loads[6].wait()

    def project(block):
        @pl.loop(0, 4)
        def _(i):
            cols = pl.ds(pl.multiple_of(i * 256, 256), 256)
            ks[block, :, cols] = dot(enc[block], wk[:, cols]).astype(BF16)
            vs[block, :, cols] = dot(enc[block], wv[:, cols]).astype(BF16)

        write(ks.at[block], k_out.at[block])
        write(vs.at[block], v_out.at[block])

    c_nrm.wait_recv()
    write(nrm, nrm_out)
    crossed(0, 0)
    accumulate([(0, 0), (1, 0), (3, 0), (0, 1), (0, 3)], begin=True)
    crossed(1, 3)
    crossed(1, 1)
    project(at.x)
    crossed(0, 3)
    crossed(0, 1)
    c_e1[0].wait_recv()
    c_e2 = [send(enc.at[down, 0:128], enc.at[down, 0:128], at.along("x", 1))]
    c_e1[1].wait_recv()
    c_e2.append(send(enc.at[up, 128:256], enc.at[up, 128:256], at.along("x", 3)))
    project(down)
    project(up)
    accumulate([(1, 1), (1, 3), (3, 1), (3, 3)])
    crossed(1, 2)
    crossed(0, 2)
    landed(0, 0)
    landed(1, 0)
    accumulate([(2, 0), (0, 2)])
    c_e2[0].wait_recv()
    c_e2[1].wait_recv()
    project(far)
    for line in (3, 1):
        landed(0, line)
        landed(1, line)
    accumulate([(2, 1), (2, 3), (1, 2), (3, 2)])
    landed(0, 2)
    landed(1, 2)
    accumulate([(2, 2)])
    q_send[...] = acc[256:512].astype(BF16)
    c_q = send(q_send, q_in, at.sibling())
    c_q.wait_recv()
    q_ref[...] = (acc[0:256] + q_in[...].astype(F32)).astype(BF16)
    for copy in send.copies:
        copy.wait_send()
    for copy in outs:
        copy.wait()


FORWARD_SENDS = 4 + 1 + 4 + 2 * 6 + 2 * 2 + 16 + 2 + 2 + 1 + 2 + 2 + 1


def forward(tokens, w_query, gain, state_kv, near, enc_gain, enc_query, enc_out, w_key, w_value):
    rows, full = tokens.shape
    width = w_query.shape[1]
    vmem = pl.BlockSpec(memory_space=pltpu.VMEM)
    anywhere = pl.BlockSpec(memory_space=pl.ANY)

    def buffer(*shape, kind=BF16):
        return pltpu.VMEM(shape, kind)

    return pl.pallas_call(
        forward_kernel,
        in_specs=[anywhere, anywhere, vmem, anywhere, anywhere, vmem] + [anywhere] * 4,
        out_specs=[vmem] + [anywhere] * 4 + [vmem],
        out_shape=[
            jax.ShapeDtypeStruct((rows, width), BF16),
            jax.ShapeDtypeStruct((16, CHUNK, width), BF16),
            jax.ShapeDtypeStruct((16, 2 * rows, CHUNK), BF16),
            jax.ShapeDtypeStruct((4, KEYS, width), BF16),
            jax.ShapeDtypeStruct((4, KEYS, width), BF16),
            jax.ShapeDtypeStruct((rows, 128), F32),
        ],
        scratch_shapes=[
            buffer(rows, full),
            buffer(16, CHUNK, width),
            buffer(16, 2 * rows, CHUNK),
            buffer(16, rows, CHUNK),
            buffer(full // 4, 2 * E),
            buffer(rows, full // 4),
            buffer(2 * rows, width, kind=F32),
            buffer(rows, width),
            buffer(rows, width),
            buffer(4, BLOCK, 2 * E),
            buffer(2, BLOCK // 2, 2 * E),
            buffer(2, BLOCK, 2 * E),
            buffer(KEYS, E),
            buffer(KEYS, E),
            buffer(KEYS, E),
            buffer(7, KEYS, 128, kind=F32),
            buffer(E, E),
            buffer(E, E),
            buffer(4, KEYS, E),
            buffer(E, width),
            buffer(E, width),
            buffer(4, KEYS, width),
            buffer(4, KEYS, width),
            pltpu.SemaphoreType.DMA((7,)),
            pltpu.SemaphoreType.DMA((25,)),
            pltpu.SemaphoreType.DMA((FORWARD_SENDS,)),
            pltpu.SemaphoreType.DMA((FORWARD_SENDS,)),
        ],
        compiler_params=pltpu.CompilerParams(
            collective_id=2, has_side_effects=True, vmem_limit_bytes=60 * 2**20
        ),
        cost_estimate=pl.CostEstimate(
            flops=2 * 5400 * 2**20, bytes_accessed=40 * 2**20, transcendentals=0
        ),
    )(tokens, w_query, gain, state_kv, near, enc_gain, enc_query, enc_out, w_key, w_value)


LINES = (2, 1, 3, 0)
Z_FIRST = 384


def backward_kernel(
    dq_ref, nrm_ref, w_ref, grad_ref, sums_ref, tokens_ref, inverse_ref, gain_ref,
    dw_ref, dh_ref, de_ref, dots_ref,
    dq2, dq_t, nrm, wc, prod, ra1, ra2, rb1, rb2, part, rn1, rn2, out_sib, in_sib,
    g1, gs, g2, gfin, gin, sums_in, tok, dh_s, column,
    load_sem, dh_sem, send_sem, recv_sem,
):
    at = Place()
    width = tokens_ref.shape[1]
    share = width // 4
    loads = [
        pltpu.make_async_copy(nrm_ref, nrm, load_sem.at[0]),
        pltpu.make_async_copy(w_ref, wc, load_sem.at[1]),
    ]
    for i in range(8):
        first = pl.multiple_of(at.x * share + i * 256, 256)
        loads.append(
            pltpu.make_async_copy(tokens_ref.at[:, pl.ds(first, 256)], tok.at[i], load_sem.at[2 + i])
        )
    for load in loads:
        load.start()
    greet(
        [at.along("x", 1), at.along("x", 2), at.along("x", 3), at.along("y", 1), at.along("y", 3),
         at.along("z", 1), at.along("z", 3), at.sibling()]
    )

    send = Sender(send_sem, recv_sem)

    def added(dst, first, second):
        dst[...] = (first[...].astype(F32) + second[...].astype(F32)).astype(BF16)

    c_dq = send(dq_ref, dq2.at[256:512], at.sibling())
    far = (at.x + 2) % 4
    up, down = (at.x + 1) % 4, (at.x + 3) % 4
    c_g1 = [
        send(grad_ref.at[far, 0:128], g1.at[0], at.along("x", 1)),
        send(grad_ref.at[far, 128:256], g1.at[1], at.along("x", 3)),
    ]
    c_sums = [send(sums_ref, sums_in.at[i], at.along("x", i + 1)) for i in range(3)]
    dq2[0:256] = dq_ref[...]
    for j in range(4):
        dq_t[256 * j : 256 * j + 256, 0:256] = jnp.transpose(dq_ref[:, 256 * j : 256 * j + 256])
    c_dq.wait_recv()
    for j in range(4):
        dq_t[256 * j : 256 * j + 256, 256:512] = jnp.transpose(
            dq2[256:512, 256 * j : 256 * j + 256]
        )
    loads[0].wait()

    def product(dy, dz):
        k = at.chunk(dy, dz)

        @pl.loop(0, 4)
        def _(i):
            rows = pl.ds(pl.multiple_of(i * 256, 256), 256)
            prod[k, rows, :] = dot(dq_t[rows, :], nrm[k]).astype(BF16)

    dims = (("z", "y"), ("y", "z"))
    spans = ((0, Z_FIRST), (Z_FIRST, 1024))
    size = (Z_FIRST, 1024 - Z_FIRST)

    def block(half, line, off, part=None):
        dy, dz = (line, off) if half == 0 else (off, line)
        low, high = spans[half]
        middle = (low + high) // 2
        low, high = (low, high) if part is None else ((low, middle), (middle, high))[part]
        return prod.at[at.chunk(dy, dz), low:high]

    def first_slot(half, line, way):
        return ra1.at[half, LINES.index(line), way, 0 : size[half] // 2]

    def second_slot(half, line, way):
        return ra2.at[half, LINES.index(line), way, 0 : size[half]]

    def both(dim, one, other):
        return send(*one, at.along(dim, 1)), send(*other, at.along(dim, 3))

    c1, c2, d1, d2 = {}, {}, {}, {}

    def first_hop(half, line):
        c1[half, line] = both(
            dims[half][0],
            (block(half, line, 2, 0), first_slot(half, line, 0)),
            (block(half, line, 2, 1), first_slot(half, line, 1)),
        )

    def second_hop(half, line):
        for way, off in ((0, 1), (1, 3)):
            c1[half, line][way].wait_recv()
            piece = block(half, line, off, way)
            added(piece, piece, first_slot(half, line, way))
        c2[half, line] = both(
            dims[half][0],
            (block(half, line, 1), second_slot(half, line, 0)),
            (block(half, line, 3), second_slot(half, line, 1)),
        )

    def gathered(half, line):
        for way in (0, 1):
            c2[half, line][way].wait_recv()
        piece = block(half, line, 0)
        total = piece[...].astype(F32) + second_slot(half, line, 0)[...].astype(F32)
        piece[...] = (total + second_slot(half, line, 1)[...].astype(F32)).astype(BF16)

    def turn_slot(half, way):
        return rb1.at[half, way, 0 : size[half] // 2]

    def last_slot(half, way):
        return rb2.at[half, way, 0 : size[half]]

    def turn(half):
        d1[half] = both(
            dims[half][1],
            (block(half, 2, 0, 0), turn_slot(half, 0)),
            (block(half, 2, 0, 1), turn_slot(half, 1)),
        )

    def turned(half):
        for way, off in ((0, 1), (1, 3)):
            d1[half][way].wait_recv()
            piece = block(half, off, 0, way)
            added(piece, piece, turn_slot(half, way))
        d2[half] = both(
            dims[half][1],
            (block(half, 1, 0), last_slot(half, 0)),
            (block(half, 3, 0), last_slot(half, 1)),
        )

    def result(half):
        for way in (0, 1):
            c2[half, 0][way].wait_recv()
            d2[half][way].wait_recv()
        extras = [second_slot(half, 0, 0), second_slot(half, 0, 1)]
        extras += [last_slot(half, 0), last_slot(half, 1)]
        for low in range(0, size[half], 128):
            total = block(half, 0, 0)[low : low + 128].astype(F32)
            for extra in extras:
                total = total + extra[low : low + 128].astype(F32)
            first = spans[half][0] + low
            dw_ref[:, first : first + 128] = jnp.transpose(total)

    def partial(k):
        @pl.loop(0, 2)
        def _(i):
            rows = pl.ds(pl.multiple_of(i * 256, 256), 256)
            part[k, rows, :] = dot(dq2[rows, :], wc[k], LAST).astype(BF16)

    n1, n2 = [], []

    def far_partial(m):
        partial(far * 4 + m)
        n1.append(
            both("x", (part.at[far * 4 + m, 0:256], rn1.at[m, 0]),
                 (part.at[far * 4 + m, 256:512], rn1.at[m, 1]))
        )

    def near_partial(m):
        n1[m][0].wait_recv()
        piece = part.at[up * 4 + m, 0:256]
        added(piece, piece, rn1.at[m, 0])
        n1[m][1].wait_recv()
        piece = part.at[down * 4 + m, 256:512]
        added(piece, piece, rn1.at[m, 1])
        n2.append(
            both("x", (part.at[up * 4 + m], rn2.at[m, 0]), (part.at[down * 4 + m], rn2.at[m, 1]))
        )

    product(2, 2)
    first_hop(1, 2)
    first_hop(0, 2)
    loads[1].wait()
    far_partial(0)
    for m, line in ((1, 1), (2, 3), (3, 0)):
        product(2, line)
        first_hop(1, line)
        product(line, 2)
        first_hop(0, line)
        far_partial(m)
    for dy, dz in ((1, 1), (3, 1), (1, 3), (3, 3)):
        product(dy, dz)

    c_g1[0].wait_recv()
    c_g1[1].wait_recv()
    gs[0, 0:128] = (grad_ref[up, 0:128].astype(F32) + g1[0].astype(F32)).astype(BF16)
    gs[0, 128:256] = grad_ref[up, 128:256]
    gs[1, 0:128] = grad_ref[down, 0:128]
    gs[1, 128:256] = (grad_ref[down, 128:256].astype(F32) + g1[1].astype(F32)).astype(BF16)
    c_g2 = both("x", (gs.at[0], g2.at[0]), (gs.at[1], g2.at[1]))

    second_hop(1, 2)
    second_hop(0, 2)
    for dy, dz in ((1, 0), (3, 0), (0, 1), (0, 3), (0, 0)):
        product(dy, dz)
    second_hop(1, 1)
    second_hop(0, 1)
    for m in range(4):
        partial(up * 4 + m)
        partial(down * 4 + m)
    second_hop(1, 3)
    second_hop(0, 3)
    second_hop(0, 0)
    for m in range(4):
        near_partial(m)

    for copy in c_sums:
        copy.wait_recv()
    sums = sums_ref[...] + sums_in[0] + sums_in[1] + sums_in[2]
    dots_ref[...] = sums * (1.0 / math.sqrt(width))
    column[...] = jnp.transpose(jnp.broadcast_to(sums[0:1], (128, 256)))

    for m in range(4):
        partial(at.x * 4 + m)
    gathered(0, 2)
    turn(0)
    for copy in c_g2:
        copy.wait_recv()
    gfin[...] = (grad_ref[at.x].astype(F32) + g2[0].astype(F32) + g2[1].astype(F32)).astype(BF16)
    c_swap = send(gfin, gin, at.partner())
    gathered(1, 2)
    turn(1)
    gathered(0, 1)
    gathered(0, 3)
    turned(0)
    second_hop(1, 0)

    for load in loads[2:]:
        load.wait()
    stores = []

    def finish(i, d_normed):
        inverse = wide(inverse_ref[...])
        unit = tok[i].astype(F32) * inverse
        rows = wide(column[...])
        grads = d_normed * gain_ref[at.x * 8 + i]
        result = inverse * (grads - unit * (rows * (1.0 / width)))
        dh_s[i] = result.astype(BF16)
        first = pl.multiple_of(i * 256, 256)
        store = pltpu.make_async_copy(
            dh_s.at[i], dh_ref.at[:, pl.ds(first, 256)], dh_sem.at[len(stores)]
        )
        store.start()
        stores.append(store)

    c_sib = []

    def normed_sum(m):
        for copy in n2[m]:
            copy.wait_recv()

        def summed(low):
            rows = slice(low, low + 256)
            total = part[at.x * 4 + m, rows].astype(F32) + rn2[m, 0, rows].astype(F32)
            return total + rn2[m, 1, rows].astype(F32)

        out_sib[m] = summed(256).astype(BF16)
        c_sib.append(send(out_sib.at[m], in_sib.at[m], at.sibling()))
        finish(2 * m + at.core, summed(0))

    def sibling_part(m):
        c_sib[m].wait_recv()
        finish(2 * m + 1 - at.core, in_sib[m].astype(F32))

    normed_sum(0)
    gathered(1, 1)
    normed_sum(1)
    sibling_part(0)
    gathered(1, 3)
    turned(1)
    normed_sum(2)
    sibling_part(1)
    normed_sum(3)
    sibling_part(2)
    result(0)
    result(1)
    sibling_part(3)
    c_swap.wait_recv()
    de_ref[...] = gin[...]
    for copy in send.copies:
        copy.wait_send()
    for store in stores:
        store.wait()


SENDS = 1 + 2 + 3 + 16 + 2 + 16 + 8 + 8 + 1 + 4 + 8


def backward(d_queries, normed, w_all, grad, sums, tokens, inverse, gain):
    rows, width = d_queries.shape
    full = tokens.shape[1]
    vmem = pl.BlockSpec(memory_space=pltpu.VMEM)
    anywhere = pl.BlockSpec(memory_space=pl.ANY)

    def buffer(*shape, kind=BF16):
        return pltpu.VMEM(shape, kind)

    return pl.pallas_call(
        backward_kernel,
        in_specs=[vmem, anywhere, anywhere, vmem, vmem, anywhere, vmem, vmem],
        out_specs=[vmem, anywhere, vmem, vmem],
        out_shape=[
            jax.ShapeDtypeStruct((256, width), F32),
            jax.ShapeDtypeStruct((rows, full // 4), BF16),
            jax.ShapeDtypeStruct((KEYS, E), BF16),
            jax.ShapeDtypeStruct((8, rows), F32),
        ],
        scratch_shapes=[
            buffer(512, 1024),
            buffer(1024, 512),
            buffer(16, 512, 256),
            buffer(16, 256, 1024),
            buffer(16, 1024, 256),
            buffer(2, 4, 2, (1024 - Z_FIRST) // 2, 256),
            buffer(2, 4, 2, 1024 - Z_FIRST, 256),
            buffer(2, 2, (1024 - Z_FIRST) // 2, 256),
            buffer(2, 2, 1024 - Z_FIRST, 256),
            buffer(16, 512, 256),
            buffer(4, 2, 256, 256),
            buffer(4, 2, 512, 256),
            buffer(4, 256, 256),
            buffer(4, 256, 256),
            buffer(2, 128, E),
            buffer(2, 256, E),
            buffer(2, 256, E),
            buffer(256, E),
            buffer(256, E),
            buffer(3, 8, 256, kind=F32),
            buffer(8, 256, 256),
            buffer(8, 256, 256),
            buffer(256, 128, kind=F32),
            pltpu.SemaphoreType.DMA((10,)),
            pltpu.SemaphoreType.DMA((8,)),
            pltpu.SemaphoreType.DMA((SENDS,)),
            pltpu.SemaphoreType.DMA((SENDS,)),
        ],
        compiler_params=pltpu.CompilerParams(
            collective_id=1, has_side_effects=True, vmem_limit_bytes=60 * 2**20
        ),
        cost_estimate=pl.CostEstimate(
            flops=4 * 512 * 1024 * 4096, bytes_accessed=20 * 2**20, transcendentals=0
        ),
    )(d_queries, normed, w_all, grad, sums, tokens, inverse, gain)


def shards(
    tokens,
    w_query,
    query_gain,
    state_kv,
    neighbours,
    enc_gain,
    enc_query,
    enc_out,
    w_key,
    w_value,
    counts,
    d_context,
):
    tok_rows = tokens.shape[0]
    gain = query_gain.reshape(32, 1, 256)
    queries, w_part, normed, keys, values, inverse = forward(
        tokens, w_query, gain, state_kv, neighbours.reshape(KEYS, E), enc_gain.reshape(1, E),
        enc_query, enc_out, w_key, w_value,
    )
    context, d_queries, grad, sums = attend(
        counts, queries, keys.reshape(4 * KEYS, -1), values.reshape(4 * KEYS, -1),
        w_key, w_value, d_context,
    )
    d_query_weight, d_hidden, d_encoded, row_dots = backward(
        d_queries, normed, w_part, grad,
        jnp.broadcast_to(sums[:, 0][None], (8, tok_rows)),
        tokens, inverse, gain,
    )
    return (
        context,
        d_hidden,
        d_query_weight,
        d_encoded.reshape(1, 1, NBR, RLEN, E),
        row_dots[0],
    )


def solution(mesh):
    return jax.shard_map(
        shards,
        mesh=mesh,
        in_specs=(
            P(("section", "seq"), None),
            P(("section", "seq"), "tensor"),
            P(),
            P("tensor", None),
            P("section", ("seq", "tensor"), None, None, None),
            P(),
            P(),
            P(),
            P(None, "tensor"),
            P(None, "tensor"),
            P(("section", "seq")),
            P(("section", "seq"), "tensor"),
        ),
        out_specs=(
            P(("section", "seq"), "tensor"),
            P(("section", "seq"), "tensor"),
            P(("section", "seq"), "tensor"),
            P("section", ("seq", "tensor"), None, None, None),
            P(("section", "seq")),
        ),
        check_vma=False,
    )
```

```python
import functools
import math

import jax
import jax.numpy as jnp
from jax import lax
from jax.experimental import pallas as pl
from jax.experimental.pallas import tpu as pltpu
from jax.sharding import PartitionSpec as P

HD = 128
E = 896
EHD = 64
BLOCK = 64
NBR = 2
RLEN = 128
KEYS = NBR * RLEN

EPSILON = 1e-05
NEG_LARGE = -1e30
MESH = pl.DeviceIdType.MESH
F32 = jnp.float32
BF16 = jnp.bfloat16
LAST = (((1,), (1,)), ((), ()))
FIRST = (((0,), (0,)), ((), ()))


def dot(a, b, dims=(((1,), (0,)), ((), ()))):
    return lax.dot_general(a, b, dims, preferred_element_type=F32)


class Place:
    def __init__(self):
        self.section = lax.axis_index("section")
        seq = lax.axis_index("seq")
        self.x = lax.axis_index("tensor")
        self.core = seq % 2
        self.y = seq // 4
        self.z = 2 * ((seq // 2) % 2) + self.section

    def along(self, dim, off):
        if dim == "x":
            return (self.section, self.seq_of(self.y, self.z), (self.x + off) % 4)
        if dim == "y":
            return (self.section, self.seq_of((self.y + off) % 4, self.z), self.x)
        z = (self.z + off) % 4
        return (z % 2, self.seq_of(self.y, z), self.x)

    def seq_of(self, y, z):
        return y * 4 + (z // 2) * 2 + self.core

    def sibling(self):
        return (self.section, self.y * 4 + (self.z // 2) * 2 + 1 - self.core, self.x)

    def partner(self):
        return (1 - self.section, self.seq_of(self.y, self.z), self.x)

    def chunk(self, dy, dz):
        y, z = (self.y + dy) % 4, (self.z + dz) % 4
        return (z % 2) * 8 + y * 2 + z // 2


def greet(devices):
    barrier = pltpu.get_barrier_semaphore()
    for device in devices:
        pl.semaphore_signal(barrier, inc=1, device_id=device, device_id_type=MESH)
    pl.semaphore_wait(barrier, len(devices))


class Sender:
    def __init__(self, send_sem, recv_sem):
        self.send_sem, self.recv_sem, self.copies = send_sem, recv_sem, []

    def __call__(self, src, dst, device):
        index = len(self.copies)
        copy = pltpu.make_async_remote_copy(
            src_ref=src, dst_ref=dst, send_sem=self.send_sem.at[index],
            recv_sem=self.recv_sem.at[index], device_id=device, device_id_type=MESH,
        )
        copy.start()
        self.copies.append(copy)
        return copy


Y_FIRST = 96
CHUNK = 256


def wide(column):
    return jnp.concatenate([column, column], axis=1)


def forward_kernel(
    tokens_ref, w_ref, gain_ref, state_ref, near_ref, egain_ref, equery_ref, eout_ref, wk_ref, wv_ref,
    q_ref, w_out, nrm_out, k_out, v_out, inv_ref,
    tok, wc, nrm, theirs, skv, unit, acc, q_send, q_in,
    sp, sr1, sr2, enc_in, eq_s, ectx, escore, equery, eout, enc, wk, wv, ks, vs,
    load_sem, out_sem, send_sem, recv_sem,
):
    at = Place()
    share = tok.shape[1] // 4
    send = Sender(send_sem, recv_sem)
    me = at.chunk(0, 0)
    pairs = (
        (w_ref, wc.at[me]), (tokens_ref, tok), (state_ref, skv), (equery_ref, equery),
        (eout_ref, eout), (wk_ref, wk), (wv_ref, wv),
    )
    loads = [pltpu.make_async_copy(src, dst, load_sem.at[i]) for i, (src, dst) in enumerate(pairs)]
    for load in loads:
        load.start()
    greet(
        [at.along("x", 1), at.along("x", 3), at.along("y", 1), at.along("y", 3),
         at.along("z", 1), at.along("z", 3), at.sibling()]
    )

    dims = (("y", "z"), ("z", "y"))
    spans = ((0, Y_FIRST), (Y_FIRST, CHUNK))

    def piece(half, first, second, part=None):
        dy, dz = (first, second) if half == 0 else (second, first)
        low, high = spans[half]
        middle = (low + high) // 2
        low, high = (low, high) if part is None else ((low, middle), (middle, high))[part]
        return wc.at[at.chunk(dy, dz), low:high]

    def pass_on(ref, dim, off):
        return send(ref, ref, at.along(dim, off))

    near, relay, cross, last = {}, {}, {}, {}

    def across(half, line):
        dim = dims[half][1]
        block = piece(half, line, 0)
        cross[half, line] = (pass_on(block, dim, 1), pass_on(block, dim, 3))

    def relays(half):
        dim = dims[half][0]
        near[half][0].wait_recv()
        first = pass_on(piece(half, 3, 0, 0), dim, 1)
        near[half][1].wait_recv()
        relay[half] = (first, pass_on(piece(half, 1, 0, 1), dim, 3))

    def relayed(half):
        relay[half][0].wait_recv()
        relay[half][1].wait_recv()
        across(half, 2)

    def crossed(half, line):
        dim = dims[half][1]
        cross[half, line][0].wait_recv()
        first = pass_on(piece(half, line, 3, 0), dim, 1)
        cross[half, line][1].wait_recv()
        last[half, line] = (first, pass_on(piece(half, line, 1, 1), dim, 3))

    def landed(half, line):
        last[half, line][0].wait_recv()
        last[half, line][1].wait_recv()

    outs = []

    def write(src, dst):
        copy = pltpu.make_async_copy(src, dst, out_sem.at[len(outs)])
        copy.start()
        outs.append(copy)

    def accumulate(offsets, begin=False):
        chunks = [at.chunk(dy, dz) for dy, dz in offsets]
        for k in chunks:
            write(wc.at[k], w_out.at[k])

        @pl.loop(0, 4)
        def _(i):
            rows = pl.ds(pl.multiple_of((i // 2) * 256, 256), 256)
            cols = pl.ds(pl.multiple_of((i % 2) * 512, 512), 512)
            total = dot(nrm[chunks[0], rows, :], wc[chunks[0], :, cols])
            for k in chunks[1:]:
                total = total + dot(nrm[k, rows, :], wc[k, :, cols])
            acc[rows, cols] = total if begin else acc[rows, cols] + total

    loads[0].wait()
    for half in (0, 1):
        block = piece(half, 0, 0)
        near[half] = (pass_on(block, dims[half][0], 1), pass_on(block, dims[half][0], 3))
    c_near = send(near_ref, enc_in, at.partner())
    across(1, 0)

    loads[1].wait()

    @pl.loop(0, 16)
    def _(i):
        rows = pl.ds(pl.multiple_of(i * 16, 16), 16)
        values = tok[rows, :].astype(F32)
        square = jnp.sum(values * values, axis=-1, keepdims=True)
        inverse = lax.rsqrt(square * (1.0 / tok.shape[1]) + EPSILON)
        inv_ref[rows, :] = jnp.broadcast_to(inverse, (16, 128))

    @pl.loop(0, 8)
    def _(i):
        source = pl.ds(pl.multiple_of(at.x * share + i * 256, 256), 256)
        target = pl.ds(pl.multiple_of(i * 256, 256), 256)
        unit[:, target] = (tok[:, source].astype(F32) * wide(inv_ref[...])).astype(BF16)

    loads[2].wait()

    @pl.loop(0, 7)
    def _(i):
        cols = pl.ds(pl.multiple_of(i * 256, 256), 256)
        part = dot(unit[...], skv[:, cols]).astype(BF16)
        for j in range(4):
            sp[j, :, cols] = part[64 * j : 64 * j + 64]

    far, up, down = (at.x + 2) % 4, (at.x + 1) % 4, (at.x + 3) % 4
    c_s1 = (
        send(sp.at[far, 0:32], sr1.at[0], at.along("x", 1)),
        send(sp.at[far, 32:64], sr1.at[1], at.along("x", 3)),
    )
    relays(0)
    relays(1)
    across(1, 3)
    across(1, 1)
    for line in (0, 3, 1):
        across(0, line)

    @pl.loop(0, 16)
    def _(k):
        def chunk(g):
            cols = pl.ds(pl.multiple_of(g * CHUNK, CHUNK), CHUNK)
            return (tok[:, cols].astype(F32) * wide(inv_ref[...]) * gain_ref[g]).astype(BF16)

        nrm[k, 0:256] = chunk(2 * k + at.core)
        theirs[k] = chunk(2 * k + 1 - at.core)

    c_nrm = send(theirs, nrm.at[:, 256:512], at.sibling())

    for way, block in ((0, up), (1, down)):
        c_s1[way].wait_recv()
        rows = slice(32 * way, 32 * way + 32)
        sp[block, rows] = (sp[block, rows].astype(F32) + sr1[way].astype(F32)).astype(BF16)
    c_s2 = (
        send(sp.at[up], sr2.at[0], at.along("x", 1)),
        send(sp.at[down], sr2.at[1], at.along("x", 3)),
    )
    relayed(0)
    crossed(1, 0)

    loads[3].wait()
    c_near.wait_recv()
    enc_rows = enc_in[...].astype(F32)
    mean = jnp.sum(enc_rows * enc_rows, axis=-1, keepdims=True) * (1.0 / E)
    enc_normed = (enc_rows * lax.rsqrt(mean + EPSILON) * egain_ref[...]).astype(BF16)
    eq_s[...] = dot(enc_normed, equery[...]).astype(BF16)

    c_s2[0].wait_recv()
    c_s2[1].wait_recv()
    states = (sp[at.x].astype(F32) + sr2[0].astype(F32) + sr2[1].astype(F32)).astype(BF16)
    states = states.astype(F32)
    left = lax.broadcasted_iota(jnp.int32, (BLOCK, 128), 1) < EHD
    left_wide = lax.broadcasted_iota(jnp.int32, (KEYS, 128), 1) < EHD

    def doubled(cols):
        both = states[:, cols]
        return jnp.concatenate(
            [jnp.where(left, both, 0.0), jnp.where(left, 0.0, both)], axis=0
        ).astype(BF16)

    for j in range(7):
        keys = doubled(slice(128 * j, 128 * j + 128))
        escore[j] = dot(eq_s[:, 128 * j : 128 * j + 128], keys, LAST) * (1.0 / math.sqrt(EHD))
    for j in range(7):
        scores = escore[j]
        top_left = jnp.max(jnp.where(left_wide, scores, NEG_LARGE), axis=-1, keepdims=True)
        top_right = jnp.max(jnp.where(left_wide, NEG_LARGE, scores), axis=-1, keepdims=True)
        weights = jnp.exp(scores - jnp.where(left_wide, top_left, top_right))
        sum_left = jnp.sum(jnp.where(left_wide, weights, 0.0), axis=-1, keepdims=True)
        sum_right = jnp.sum(jnp.where(left_wide, 0.0, weights), axis=-1, keepdims=True)
        escore[j] = weights / jnp.where(left_wide, sum_left, sum_right)
    for j in range(7):
        values = doubled(slice(E + 128 * j, E + 128 * j + 128))
        ectx[:, 128 * j : 128 * j + 128] = dot(escore[j].astype(BF16), values).astype(BF16)
    loads[4].wait()
    enc[at.x] = (enc_in[...].astype(F32) + dot(ectx[...], eout[...])).astype(BF16)
    c_e1 = (
        send(enc.at[at.x], enc.at[at.x], at.along("x", 1)),
        send(enc.at[at.x], enc.at[at.x], at.along("x", 3)),
    )
    relayed(1)
    loads[5].wait()
    loads[6].wait()

    def project(block):
        @pl.loop(0, 4)
        def _(i):
            cols = pl.ds(pl.multiple_of(i * 256, 256), 256)
            ks[block, :, cols] = dot(enc[block], wk[:, cols]).astype(BF16)
            vs[block, :, cols] = dot(enc[block], wv[:, cols]).astype(BF16)

        write(ks.at[block], k_out.at[block])
        write(vs.at[block], v_out.at[block])

    c_nrm.wait_recv()
    write(nrm, nrm_out)
    crossed(0, 0)
    accumulate([(0, 0), (1, 0), (3, 0), (0, 1), (0, 3)], begin=True)
    crossed(1, 3)
    crossed(1, 1)
    project(at.x)
    crossed(0, 3)
    crossed(0, 1)
    c_e1[0].wait_recv()
    c_e2 = [send(enc.at[down, 0:128], enc.at[down, 0:128], at.along("x", 1))]
    c_e1[1].wait_recv()
    c_e2.append(send(enc.at[up, 128:256], enc.at[up, 128:256], at.along("x", 3)))
    project(down)
    project(up)
    accumulate([(1, 1), (1, 3), (3, 1), (3, 3)])
    crossed(1, 2)
    crossed(0, 2)
    landed(0, 0)
    landed(1, 0)
    accumulate([(2, 0), (0, 2)])
    c_e2[0].wait_recv()
    c_e2[1].wait_recv()
    project(far)
    for line in (3, 1):
        landed(0, line)
        landed(1, line)
    accumulate([(2, 1), (2, 3), (1, 2), (3, 2)])
    landed(0, 2)
    landed(1, 2)
    accumulate([(2, 2)])
    q_send[...] = acc[256:512].astype(BF16)
    c_q = send(q_send, q_in, at.sibling())
    c_q.wait_recv()
    q_ref[...] = (acc[0:256] + q_in[...].astype(F32)).astype(BF16)
    for copy in send.copies:
        copy.wait_send()
    for copy in outs:
        copy.wait()


FORWARD_SENDS = 4 + 1 + 4 + 2 * 6 + 2 * 2 + 16 + 2 + 2 + 1 + 2 + 2 + 1


def forward(tokens, w_query, gain, state_kv, near, enc_gain, enc_query, enc_out, w_key, w_value):
    rows, full = tokens.shape
    width = w_query.shape[1]
    vmem = pl.BlockSpec(memory_space=pltpu.VMEM)
    anywhere = pl.BlockSpec(memory_space=pl.ANY)

    def buffer(*shape, kind=BF16):
        return pltpu.VMEM(shape, kind)

    return pl.pallas_call(
        forward_kernel,
        in_specs=[anywhere, anywhere, vmem, anywhere, anywhere, vmem] + [anywhere] * 4,
        out_specs=[vmem] + [anywhere] * 4 + [vmem],
        out_shape=[
            jax.ShapeDtypeStruct((rows, width), BF16),
            jax.ShapeDtypeStruct((16, CHUNK, width), BF16),
            jax.ShapeDtypeStruct((16, 2 * rows, CHUNK), BF16),
            jax.ShapeDtypeStruct((4, KEYS, width), BF16),
            jax.ShapeDtypeStruct((4, KEYS, width), BF16),
            jax.ShapeDtypeStruct((rows, 128), F32),
        ],
        scratch_shapes=[
            buffer(rows, full),
            buffer(16, CHUNK, width),
            buffer(16, 2 * rows, CHUNK),
            buffer(16, rows, CHUNK),
            buffer(full // 4, 2 * E),
            buffer(rows, full // 4),
            buffer(2 * rows, width, kind=F32),
            buffer(rows, width),
            buffer(rows, width),
            buffer(4, BLOCK, 2 * E),
            buffer(2, BLOCK // 2, 2 * E),
            buffer(2, BLOCK, 2 * E),
            buffer(KEYS, E),
            buffer(KEYS, E),
            buffer(KEYS, E),
            buffer(7, KEYS, 128, kind=F32),
            buffer(E, E),
            buffer(E, E),
            buffer(4, KEYS, E),
            buffer(E, width),
            buffer(E, width),
            buffer(4, KEYS, width),
            buffer(4, KEYS, width),
            pltpu.SemaphoreType.DMA((7,)),
            pltpu.SemaphoreType.DMA((25,)),
            pltpu.SemaphoreType.DMA((FORWARD_SENDS,)),
            pltpu.SemaphoreType.DMA((FORWARD_SENDS,)),
        ],
        compiler_params=pltpu.CompilerParams(
            collective_id=2, has_side_effects=True, vmem_limit_bytes=60 * 2**20
        ),
        cost_estimate=pl.CostEstimate(
            flops=2 * 5400 * 2**20, bytes_accessed=40 * 2**20, transcendentals=0
        ),
    )(tokens, w_query, gain, state_kv, near, enc_gain, enc_query, enc_out, w_key, w_value)


LINES = (2, 1, 3, 0)
GROUPS = ((0, 256, 96), (256, 1024, 288))
LOADS = 16


def halves(group):
    first, stop, z_first = GROUPS[group]
    return z_first, stop - first - z_first


def backward_kernel(
    counts, q_ref, k_ref, v_ref, do_ref, wk_ref, wv_ref, nrm_ref, w_ref, tokens_ref,
    inverse_ref, gain_ref,
    ctx_ref, dw_ref, dh_ref, de_ref, dots_ref,
    qs, dos, ks, vs, wk, wv, ctx, score_s, dprob_s, weight_s, dscore_s, sum_s,
    dq2, dq_t, nrm, wc, prod, dw_t, part, rn1, rn2, out_sib, in_sib,
    grads, g1, gs, g2, gfin, gin, sums, sums_in, tok, column,
    ra1_00, ra1_01, ra1_10, ra1_11, ra2_00, ra2_01, ra2_10, ra2_11,
    rb1_00, rb1_01, rb1_10, rb1_11, rb2_00, rb2_01, rb2_10, rb2_11,
    load_sem, out_sem, send_sem, recv_sem,
):
    at = Place()
    width = tokens_ref.shape[1]
    share = width // 4
    ra1 = ((ra1_00, ra1_01), (ra1_10, ra1_11))
    ra2 = ((ra2_00, ra2_01), (ra2_10, ra2_11))
    rb1 = ((rb1_00, rb1_01), (rb1_10, rb1_11))
    rb2 = ((rb2_00, rb2_01), (rb2_10, rb2_11))
    pairs = [
        (q_ref, qs), (do_ref, dos), (k_ref, ks), (v_ref, vs), (wk_ref, wk), (wv_ref, wv),
        (nrm_ref, nrm), (w_ref, wc),
    ]
    for i in range(8):
        first = pl.multiple_of(at.x * share + i * 256, 256)
        pairs.append((tokens_ref.at[:, pl.ds(first, 256)], tok.at[i]))
    loads = [pltpu.make_async_copy(src, dst, load_sem.at[i]) for i, (src, dst) in enumerate(pairs)]
    for load in loads:
        load.start()
    barrier = pltpu.get_barrier_semaphore()
    friends = [at.along("x", 1), at.along("x", 2), at.along("x", 3), at.along("y", 1),
               at.along("y", 3), at.along("z", 1), at.along("z", 3), at.sibling()]
    for friend in friends:
        pl.semaphore_signal(barrier, inc=1, device_id=friend, device_id_type=MESH)

    send = Sender(send_sem, recv_sem)
    far, up, down = (at.x + 2) % 4, (at.x + 1) % 4, (at.x + 3) % 4
    scale = 1.0 / math.sqrt(HD)

    def added(dst, first, second):
        dst[...] = (first[...].astype(F32) + second[...].astype(F32)).astype(BF16)

    def both(dim, one, other):
        return send(*one, at.along(dim, 1)), send(*other, at.along(dim, 3))

    def attention(b, group):
        first, stop, _ = GROUPS[group]
        spans = [slice(low, low + HD) for low in range(first, stop, HD)]
        rows = pl.ds(pl.multiple_of(b * BLOCK, BLOCK), BLOCK)
        count = counts[b]
        valid = lax.broadcasted_iota(jnp.int32, (BLOCK, KEYS), 1) < count * RLEN
        empty = jnp.where(count == 0, 1.0, 0.0).astype(F32)
        for i, cols in enumerate(spans):
            score_s[i] = dot(qs[rows, cols], ks[b, :, cols], LAST) * scale
            dprob_s[i] = dot(dos[rows, cols], vs[b, :, cols], LAST)
        for i in range(len(spans)):
            scores = score_s[i]
            top = jnp.max(jnp.where(valid, scores, NEG_LARGE), axis=-1, keepdims=True)
            weights = jnp.where(valid, jnp.exp(scores - top), 0.0)
            probs = weights / (jnp.sum(weights, axis=-1, keepdims=True) + empty)
            weight_s[i] = probs.astype(BF16)
            d_probs = dprob_s[i]
            inner = jnp.sum(probs * d_probs, axis=-1, keepdims=True)
            dscore_s[i] = (probs * (d_probs - inner) * scale).astype(BF16)
        total = jnp.zeros((BLOCK, HD), F32)
        for i, cols in enumerate(spans):
            ctx[rows, cols] = dot(weight_s[i], vs[b, :, cols]).astype(BF16)
            dq = dot(dscore_s[i], ks[b, :, cols])
            dq2[rows, cols] = dq.astype(BF16)
            total = total + dq * qs[rows, cols].astype(F32)
            vs[b, :, cols] = dot(weight_s[i], dos[rows, cols], FIRST).astype(BF16)
            ks[b, :, cols] = dot(dscore_s[i], qs[rows, cols], FIRST).astype(BF16)
        sum_s[rows, :] = total if group == 0 else sum_s[rows, :] + total

    def encoded_grad(b):
        grad = dot(ks[b], wk[...], LAST) + dot(vs[b], wv[...], LAST)
        grads[b] = grad.astype(BF16)

    def share_dq(group):
        first, stop, _ = GROUPS[group]
        return send(dq2.at[0:256, first:stop], dq2.at[256:512, first:stop], at.sibling())

    def transposed(group, rows):
        first, stop, _ = GROUPS[group]
        for low in range(first, stop, 256):
            dq_t[low : low + 256, rows] = jnp.transpose(dq2[rows, low : low + 256])

    def product(group, dy, dz):
        k = at.chunk(dy, dz)
        first, stop, _ = GROUPS[group]

        @pl.loop(0, (stop - first) // 256)
        def _(i):
            rows = pl.ds(pl.multiple_of(first + i * 256, 256), 256)
            prod[k, rows, :] = dot(dq_t[rows, :], nrm[k]).astype(BF16)

    dims = (("z", "y"), ("y", "z"))

    def block(group, half, line, off, part=None):
        dy, dz = (line, off) if half == 0 else (off, line)
        first, stop, z_first = GROUPS[group]
        low, high = ((first, first + z_first), (first + z_first, stop))[half]
        middle = (low + high) // 2
        low, high = (low, high) if part is None else ((low, middle), (middle, high))[part]
        return prod.at[at.chunk(dy, dz), low:high]

    c1, c2, d1, d2 = {}, {}, {}, {}

    def first_hop(group, half, line):
        slot = ra1[group][half].at[LINES.index(line)]
        c1[group, half, line] = both(
            dims[half][0],
            (block(group, half, line, 2, 0), slot.at[0]),
            (block(group, half, line, 2, 1), slot.at[1]),
        )

    def second_hop(group, half, line):
        for way, off in ((0, 1), (1, 3)):
            c1[group, half, line][way].wait_recv()
            piece = block(group, half, line, off, way)
            added(piece, piece, ra1[group][half].at[LINES.index(line), way])
        slot = ra2[group][half].at[LINES.index(line)]
        c2[group, half, line] = both(
            dims[half][0],
            (block(group, half, line, 1), slot.at[0]),
            (block(group, half, line, 3), slot.at[1]),
        )

    def gathered(group, half, line):
        for way in (0, 1):
            c2[group, half, line][way].wait_recv()
        slot = ra2[group][half].at[LINES.index(line)]
        piece = block(group, half, line, 0)
        total = piece[...].astype(F32) + slot[0].astype(F32) + slot[1].astype(F32)
        piece[...] = total.astype(BF16)

    def turn(group, half):
        d1[group, half] = both(
            dims[half][1],
            (block(group, half, 2, 0, 0), rb1[group][half].at[0]),
            (block(group, half, 2, 0, 1), rb1[group][half].at[1]),
        )

    def turned(group, half):
        for way, off in ((0, 1), (1, 3)):
            d1[group, half][way].wait_recv()
            piece = block(group, half, off, 0, way)
            added(piece, piece, rb1[group][half].at[way])
        d2[group, half] = both(
            dims[half][1],
            (block(group, half, 1, 0), rb2[group][half].at[0]),
            (block(group, half, 3, 0), rb2[group][half].at[1]),
        )

    def result(group):
        first, stop, _ = GROUPS[group]
        sizes = halves(group)
        for half in (0, 1):
            for way in (0, 1):
                c2[group, half, 0][way].wait_recv()
                d2[group, half][way].wait_recv()
            own = block(group, half, 0, 0)
            slot = ra2[group][half].at[LINES.index(0)]
            total = own[...].astype(F32) + slot[0].astype(F32) + slot[1].astype(F32)
            low = half * sizes[0]
            dw_t[low : low + sizes[half]] = (
                total + rb2[group][half][0].astype(F32) + rb2[group][half][1].astype(F32)
            )
        for low in range(0, stop - first, 128):
            dw_ref[:, first + low : first + low + 128] = jnp.transpose(dw_t[low : low + 128])

    def partial(k):
        @pl.loop(0, 2)
        def _(i):
            rows = pl.ds(pl.multiple_of(i * 256, 256), 256)
            part[k, rows, :] = dot(dq2[rows, :], wc[k], LAST).astype(BF16)

    n1, n2 = [], []

    def far_partial(m):
        partial(far * 4 + m)
        n1.append(
            both("x", (part.at[far * 4 + m, 0:256], rn1.at[m, 0]),
                 (part.at[far * 4 + m, 256:512], rn1.at[m, 1]))
        )

    def near_partial(m):
        n1[m][0].wait_recv()
        piece = part.at[up * 4 + m, 0:256]
        added(piece, piece, rn1.at[m, 0])
        n1[m][1].wait_recv()
        piece = part.at[down * 4 + m, 256:512]
        added(piece, piece, rn1.at[m, 1])
        n2.append(
            both("x", (part.at[up * 4 + m], rn2.at[m, 0]), (part.at[down * 4 + m], rn2.at[m, 1]))
        )

    outs = []

    def write(src, dst):
        copy = pltpu.make_async_copy(src, dst, out_sem.at[len(outs)])
        copy.start()
        outs.append(copy)

    def finish(i, d_normed):
        inverse = wide(inverse_ref[...])
        unit = tok[i].astype(F32) * inverse
        parts = d_normed * gain_ref[at.x * 8 + i]
        result = inverse * (parts - unit * (wide(column[...]) * (1.0 / width)))
        tok[i] = result.astype(BF16)
        first = pl.multiple_of(i * 256, 256)
        write(tok.at[i], dh_ref.at[:, pl.ds(first, 256)])

    c_sib = []

    def normed_sum(m):
        for copy in n2[m]:
            copy.wait_recv()

        def summed(low):
            rows = slice(low, low + 256)
            total = part[at.x * 4 + m, rows].astype(F32) + rn2[m, 0, rows].astype(F32)
            return total + rn2[m, 1, rows].astype(F32)

        out_sib[m] = summed(256).astype(BF16)
        c_sib.append(send(out_sib.at[m], in_sib.at[m], at.sibling()))
        finish(2 * m + at.core, summed(0))

    def sibling_part(m):
        c_sib[m].wait_recv()
        finish(2 * m + 1 - at.core, in_sib[m].astype(F32))

    for load in loads[:4]:
        load.wait()

    @pl.loop(0, 4)
    def _(b):
        attention(b, 0)

    pl.semaphore_wait(barrier, len(friends))
    c_dq = [share_dq(0)]
    own, other = slice(0, 256), slice(256, 512)
    transposed(0, own)
    for load in loads[4:8]:
        load.wait()
    attention(far, 1)
    encoded_grad(far)
    c_g1 = both("x", (grads.at[far, 0:128], g1.at[0]), (grads.at[far, 128:256], g1.at[1]))
    c_dq[0].wait_recv()
    transposed(0, other)
    product(0, 2, 2)
    first_hop(0, 1, 2)
    first_hop(0, 0, 2)
    for line in (1, 3, 0):
        product(0, 2, line)
        first_hop(0, 1, line)
        product(0, line, 2)
        first_hop(0, 0, line)
    attention(up, 1)
    attention(down, 1)
    for dy in (1, 3, 0):
        for dz in (1, 3, 0):
            product(0, dy, dz)
    second_hop(0, 1, 2)
    second_hop(0, 0, 2)
    attention(at.x, 1)
    c_dq.append(share_dq(1))
    write(ctx, ctx_ref)
    second_hop(0, 1, 1)
    second_hop(0, 0, 1)
    second_hop(0, 1, 3)
    second_hop(0, 0, 3)
    lanes = jnp.sum(jnp.transpose(sum_s[...]), axis=0, keepdims=True)
    sums[...] = jnp.broadcast_to(lanes, (8, 256))
    c_sums = [send(sums, sums_in.at[i], at.along("x", i + 1)) for i in range(3)]
    transposed(1, own)
    c_dq[1].wait_recv()
    transposed(1, other)
    product(1, 2, 2)
    first_hop(1, 1, 2)
    first_hop(1, 0, 2)
    for line in (1, 3, 0):
        product(1, 2, line)
        first_hop(1, 1, line)
        product(1, line, 2)
        first_hop(1, 0, line)

    encoded_grad(up)
    encoded_grad(down)
    c_g1[0].wait_recv()
    c_g1[1].wait_recv()
    gs[0, 0:128] = (grads[up, 0:128].astype(F32) + g1[0].astype(F32)).astype(BF16)
    gs[0, 128:256] = grads[up, 128:256]
    gs[1, 0:128] = grads[down, 0:128]
    gs[1, 128:256] = (grads[down, 128:256].astype(F32) + g1[1].astype(F32)).astype(BF16)
    c_g2 = both("x", (gs.at[0], g2.at[0]), (gs.at[1], g2.at[1]))
    for m in range(4):
        far_partial(m)

    gathered(0, 0, 2)
    turn(0, 0)
    for dy in (1, 3, 0):
        for dz in (1, 3, 0):
            product(1, dy, dz)
    second_hop(1, 1, 2)
    second_hop(1, 0, 2)
    gathered(0, 1, 2)
    turn(0, 1)
    for m in range(4):
        partial(up * 4 + m)
        partial(down * 4 + m)
    second_hop(1, 1, 1)
    second_hop(1, 0, 1)
    second_hop(1, 1, 3)
    second_hop(1, 0, 3)
    encoded_grad(at.x)
    for copy in c_g2:
        copy.wait_recv()
    gfin[...] = (grads[at.x].astype(F32) + g2[0].astype(F32) + g2[1].astype(F32)).astype(BF16)
    c_swap = send(gfin, gin, at.partner())
    gathered(0, 0, 1)
    gathered(0, 0, 3)
    turned(0, 0)
    gathered(0, 1, 1)
    gathered(0, 1, 3)
    turned(0, 1)
    for m in range(4):
        near_partial(m)
    second_hop(0, 0, 0)
    second_hop(1, 0, 0)

    for copy in c_sums:
        copy.wait_recv()
    whole = sums[...] + sums_in[0] + sums_in[1] + sums_in[2]
    dots_ref[...] = whole[0:1] * (1.0 / math.sqrt(width))
    column[...] = jnp.transpose(jnp.broadcast_to(whole[0:1], (128, 256)))
    for load in loads[8:]:
        load.wait()
    for m in range(4):
        partial(at.x * 4 + m)

    gathered(1, 0, 2)
    turn(1, 0)
    gathered(1, 1, 2)
    turn(1, 1)
    second_hop(0, 1, 0)
    normed_sum(0)
    gathered(1, 0, 1)
    gathered(1, 0, 3)
    turned(1, 0)
    second_hop(1, 1, 0)
    normed_sum(1)
    sibling_part(0)
    gathered(1, 1, 1)
    gathered(1, 1, 3)
    turned(1, 1)
    normed_sum(2)
    sibling_part(1)
    result(0)
    normed_sum(3)
    sibling_part(2)
    result(1)
    sibling_part(3)
    c_swap.wait_recv()
    write(gin, de_ref)
    for copy in send.copies:
        copy.wait_send()
    for copy in outs:
        copy.wait()


BACKWARD_SENDS = 2 + 2 + 2 + 8 + 8 + 3 + 1 + 4 + 2 * 40


def backward(
    counts, queries, keys, values, d_context, w_key, w_value, normed, w_all, tokens, inverse, gain
):
    rows, width = queries.shape
    full = tokens.shape[1]
    vmem = pl.BlockSpec(memory_space=pltpu.VMEM)
    anywhere = pl.BlockSpec(memory_space=pl.ANY)

    def buffer(*shape, kind=BF16):
        return pltpu.VMEM(shape, kind)

    sizes = [size for group in range(2) for size in halves(group)]
    return pl.pallas_call(
        backward_kernel,
        in_specs=[pl.BlockSpec(memory_space=pltpu.SMEM)] + [anywhere] * 9 + [vmem, vmem],
        out_specs=[anywhere, vmem, anywhere, anywhere, vmem],
        out_shape=[
            jax.ShapeDtypeStruct((rows, width), BF16),
            jax.ShapeDtypeStruct((256, width), F32),
            jax.ShapeDtypeStruct((rows, full // 4), BF16),
            jax.ShapeDtypeStruct((KEYS, E), BF16),
            jax.ShapeDtypeStruct((1, rows), F32),
        ],
        scratch_shapes=[
            buffer(rows, width),
            buffer(rows, width),
            buffer(4, KEYS, width),
            buffer(4, KEYS, width),
            buffer(E, width),
            buffer(E, width),
            buffer(rows, width),
            buffer(6, BLOCK, KEYS, kind=F32),
            buffer(6, BLOCK, KEYS, kind=F32),
            buffer(6, BLOCK, KEYS),
            buffer(6, BLOCK, KEYS),
            buffer(rows, HD, kind=F32),
            buffer(512, 1024),
            buffer(1024, 512),
            buffer(16, 512, 256),
            buffer(16, 256, 1024),
            buffer(16, 1024, 256),
            buffer(768, 256, kind=F32),
            buffer(16, 512, 256),
            buffer(4, 2, 256, 256),
            buffer(4, 2, 512, 256),
            buffer(4, 256, 256),
            buffer(4, 256, 256),
            buffer(4, KEYS, E),
            buffer(2, 128, E),
            buffer(2, 256, E),
            buffer(2, 256, E),
            buffer(256, E),
            buffer(256, E),
            buffer(8, 256, kind=F32),
            buffer(3, 8, 256, kind=F32),
            buffer(8, 256, 256),
            buffer(256, 128, kind=F32),
        ]
        + [buffer(4, 2, size // 2, 256) for size in sizes]
        + [buffer(4, 2, size, 256) for size in sizes]
        + [buffer(2, size // 2, 256) for size in sizes]
        + [buffer(2, size, 256) for size in sizes]
        + [
            pltpu.SemaphoreType.DMA((LOADS,)),
            pltpu.SemaphoreType.DMA((10,)),
            pltpu.SemaphoreType.DMA((BACKWARD_SENDS,)),
            pltpu.SemaphoreType.DMA((BACKWARD_SENDS,)),
        ],
        compiler_params=pltpu.CompilerParams(
            collective_id=1, has_side_effects=True, vmem_limit_bytes=62 * 2**20
        ),
        cost_estimate=pl.CostEstimate(
            flops=12 * 2**30, bytes_accessed=30 * 2**20, transcendentals=0
        ),
    )(counts, queries, keys, values, d_context, w_key, w_value, normed, w_all, tokens, inverse, gain)


def shards(
    tokens,
    w_query,
    query_gain,
    state_kv,
    neighbours,
    enc_gain,
    enc_query,
    enc_out,
    w_key,
    w_value,
    counts,
    d_context,
):
    gain = query_gain.reshape(32, 1, 256)
    queries, w_part, normed, keys, values, inverse = forward(
        tokens, w_query, gain, state_kv, neighbours.reshape(KEYS, E), enc_gain.reshape(1, E),
        enc_query, enc_out, w_key, w_value,
    )
    context, d_query_weight, d_hidden, d_encoded, row_dots = backward(
        counts, queries, keys, values, d_context, w_key, w_value, normed, w_part, tokens, inverse,
        gain,
    )
    return (
        context,
        d_hidden,
        d_query_weight,
        d_encoded.reshape(1, 1, NBR, RLEN, E),
        row_dots[0],
    )


def solution(mesh):
    return jax.shard_map(
        shards,
        mesh=mesh,
        in_specs=(
            P(("section", "seq"), None),
            P(("section", "seq"), "tensor"),
            P(),
            P("tensor", None),
            P("section", ("seq", "tensor"), None, None, None),
            P(),
            P(),
            P(),
            P(None, "tensor"),
            P(None, "tensor"),
            P(("section", "seq")),
            P(("section", "seq"), "tensor"),
        ),
        out_specs=(
            P(("section", "seq"), "tensor"),
            P(("section", "seq"), "tensor"),
            P(("section", "seq"), "tensor"),
            P("section", ("seq", "tensor"), None, None, None),
            P(("section", "seq")),
        ),
        check_vma=False,
    )
```

```python
import functools
import math

import jax
import jax.numpy as jnp
from jax import lax
from jax.experimental import pallas as pl
from jax.experimental.pallas import tpu as pltpu
from jax.sharding import PartitionSpec as P

HD = 128
E = 896
EHD = 64
BLOCK = 64
NBR = 2
RLEN = 128
KEYS = NBR * RLEN

EPSILON = 1e-05
NEG_LARGE = -1e30
MESH = pl.DeviceIdType.MESH
F32 = jnp.float32
BF16 = jnp.bfloat16
LAST = (((1,), (1,)), ((), ()))
FIRST = (((0,), (0,)), ((), ()))


def dot(a, b, dims=(((1,), (0,)), ((), ()))):
    return lax.dot_general(a, b, dims, preferred_element_type=F32)


class Place:
    def __init__(self):
        self.section = lax.axis_index("section")
        seq = lax.axis_index("seq")
        self.x = lax.axis_index("tensor")
        self.core = seq % 2
        self.y = seq // 4
        self.z = 2 * ((seq // 2) % 2) + self.section

    def along(self, dim, off):
        if dim == "x":
            return (self.section, self.seq_of(self.y, self.z), (self.x + off) % 4)
        if dim == "y":
            return (self.section, self.seq_of((self.y + off) % 4, self.z), self.x)
        z = (self.z + off) % 4
        return (z % 2, self.seq_of(self.y, z), self.x)

    def seq_of(self, y, z):
        return y * 4 + (z // 2) * 2 + self.core

    def sibling(self):
        return (self.section, self.y * 4 + (self.z // 2) * 2 + 1 - self.core, self.x)

    def partner(self):
        return (1 - self.section, self.seq_of(self.y, self.z), self.x)

    def chunk(self, dy, dz):
        y, z = (self.y + dy) % 4, (self.z + dz) % 4
        return (z % 2) * 8 + y * 2 + z // 2


def greet(devices):
    barrier = pltpu.get_barrier_semaphore()
    for device in devices:
        pl.semaphore_signal(barrier, inc=1, device_id=device, device_id_type=MESH)
    pl.semaphore_wait(barrier, len(devices))


class Sender:
    def __init__(self, send_sem, recv_sem):
        self.send_sem, self.recv_sem, self.copies = send_sem, recv_sem, []

    def __call__(self, src, dst, device):
        index = len(self.copies)
        copy = pltpu.make_async_remote_copy(
            src_ref=src, dst_ref=dst, send_sem=self.send_sem.at[index],
            recv_sem=self.recv_sem.at[index], device_id=device, device_id_type=MESH,
        )
        copy.start()
        self.copies.append(copy)
        return copy


Y_FIRST = 96
CHUNK = 256


def wide(column):
    return jnp.concatenate([column, column], axis=1)


def forward_kernel(
    tokens_ref, w_ref, gain_ref, state_ref, near_ref, egain_ref, equery_ref, eout_ref, wk_ref, wv_ref,
    q_ref, w_out, nrm_out, k_out, v_out, inv_ref,
    tok, wc, nrm, theirs, skv, unit, acc, q_send, q_in,
    sp, sr1, sr2, enc_in, eq_s, ectx, escore, equery, eout, enc, wk, wv, ks, vs,
    load_sem, out_sem, send_sem, recv_sem,
):
    at = Place()
    share = tok.shape[1] // 4
    send = Sender(send_sem, recv_sem)
    me = at.chunk(0, 0)
    pairs = (
        (w_ref, wc.at[me]), (tokens_ref, tok), (state_ref, skv), (equery_ref, equery),
        (eout_ref, eout), (wk_ref, wk), (wv_ref, wv),
    )
    loads = [pltpu.make_async_copy(src, dst, load_sem.at[i]) for i, (src, dst) in enumerate(pairs)]
    for load in loads:
        load.start()
    greet(
        [at.along("x", 1), at.along("x", 3), at.along("y", 1), at.along("y", 3),
         at.along("z", 1), at.along("z", 3), at.sibling()]
    )

    dims = (("y", "z"), ("z", "y"))
    spans = ((0, Y_FIRST), (Y_FIRST, CHUNK))

    def piece(half, first, second, part=None):
        dy, dz = (first, second) if half == 0 else (second, first)
        low, high = spans[half]
        middle = (low + high) // 2
        low, high = (low, high) if part is None else ((low, middle), (middle, high))[part]
        return wc.at[at.chunk(dy, dz), low:high]

    def pass_on(ref, dim, off):
        return send(ref, ref, at.along(dim, off))

    near, relay, cross, last = {}, {}, {}, {}

    def across(half, line):
        dim = dims[half][1]
        block = piece(half, line, 0)
        cross[half, line] = (pass_on(block, dim, 1), pass_on(block, dim, 3))

    def relays(half):
        dim = dims[half][0]
        near[half][0].wait_recv()
        first = pass_on(piece(half, 3, 0, 0), dim, 1)
        near[half][1].wait_recv()
        relay[half] = (first, pass_on(piece(half, 1, 0, 1), dim, 3))

    def relayed(half):
        relay[half][0].wait_recv()
        relay[half][1].wait_recv()
        across(half, 2)

    def crossed(half, line):
        dim = dims[half][1]
        cross[half, line][0].wait_recv()
        first = pass_on(piece(half, line, 3, 0), dim, 1)
        cross[half, line][1].wait_recv()
        last[half, line] = (first, pass_on(piece(half, line, 1, 1), dim, 3))

    def landed(half, line):
        last[half, line][0].wait_recv()
        last[half, line][1].wait_recv()

    outs = []

    def write(src, dst):
        copy = pltpu.make_async_copy(src, dst, out_sem.at[len(outs)])
        copy.start()
        outs.append(copy)

    def accumulate(offsets, begin=False):
        chunks = [at.chunk(dy, dz) for dy, dz in offsets]
        for k in chunks:
            write(wc.at[k], w_out.at[k])

        @pl.loop(0, 4)
        def _(i):
            rows = pl.ds(pl.multiple_of((i // 2) * 256, 256), 256)
            cols = pl.ds(pl.multiple_of((i % 2) * 512, 512), 512)
            total = dot(nrm[chunks[0], rows, :], wc[chunks[0], :, cols])
            for k in chunks[1:]:
                total = total + dot(nrm[k, rows, :], wc[k, :, cols])
            acc[rows, cols] = total if begin else acc[rows, cols] + total

    loads[0].wait()
    for half in (0, 1):
        block = piece(half, 0, 0)
        near[half] = (pass_on(block, dims[half][0], 1), pass_on(block, dims[half][0], 3))
    c_near = send(near_ref, enc_in, at.partner())
    across(1, 0)

    loads[1].wait()

    @pl.loop(0, 16)
    def _(i):
        rows = pl.ds(pl.multiple_of(i * 16, 16), 16)
        values = tok[rows, :].astype(F32)
        square = jnp.sum(values * values, axis=-1, keepdims=True)
        inverse = lax.rsqrt(square * (1.0 / tok.shape[1]) + EPSILON)
        inv_ref[rows, :] = jnp.broadcast_to(inverse, (16, 128))

    @pl.loop(0, 8)
    def _(i):
        source = pl.ds(pl.multiple_of(at.x * share + i * 256, 256), 256)
        target = pl.ds(pl.multiple_of(i * 256, 256), 256)
        unit[:, target] = (tok[:, source].astype(F32) * wide(inv_ref[...])).astype(BF16)

    loads[2].wait()

    @pl.loop(0, 7)
    def _(i):
        cols = pl.ds(pl.multiple_of(i * 256, 256), 256)
        part = dot(unit[...], skv[:, cols]).astype(BF16)
        for j in range(4):
            sp[j, :, cols] = part[64 * j : 64 * j + 64]

    far, up, down = (at.x + 2) % 4, (at.x + 1) % 4, (at.x + 3) % 4
    c_s1 = (
        send(sp.at[far, 0:32], sr1.at[0], at.along("x", 1)),
        send(sp.at[far, 32:64], sr1.at[1], at.along("x", 3)),
    )
    relays(0)
    relays(1)
    across(1, 3)
    across(1, 1)
    for line in (0, 3, 1):
        across(0, line)

    @pl.loop(0, 16)
    def _(k):
        def chunk(g):
            cols = pl.ds(pl.multiple_of(g * CHUNK, CHUNK), CHUNK)
            return (tok[:, cols].astype(F32) * wide(inv_ref[...]) * gain_ref[g]).astype(BF16)

        nrm[k, 0:256] = chunk(2 * k + at.core)
        theirs[k] = chunk(2 * k + 1 - at.core)

    c_nrm = send(theirs, nrm.at[:, 256:512], at.sibling())

    for way, block in ((0, up), (1, down)):
        c_s1[way].wait_recv()
        rows = slice(32 * way, 32 * way + 32)
        sp[block, rows] = (sp[block, rows].astype(F32) + sr1[way].astype(F32)).astype(BF16)
    c_s2 = (
        send(sp.at[up], sr2.at[0], at.along("x", 1)),
        send(sp.at[down], sr2.at[1], at.along("x", 3)),
    )
    relayed(0)
    crossed(1, 0)

    loads[3].wait()
    c_near.wait_recv()
    enc_rows = enc_in[...].astype(F32)
    mean = jnp.sum(enc_rows * enc_rows, axis=-1, keepdims=True) * (1.0 / E)
    enc_normed = (enc_rows * lax.rsqrt(mean + EPSILON) * egain_ref[...]).astype(BF16)
    eq_s[...] = dot(enc_normed, equery[...]).astype(BF16)

    c_s2[0].wait_recv()
    c_s2[1].wait_recv()
    states = (sp[at.x].astype(F32) + sr2[0].astype(F32) + sr2[1].astype(F32)).astype(BF16)
    states = states.astype(F32)
    left = lax.broadcasted_iota(jnp.int32, (BLOCK, 128), 1) < EHD
    left_wide = lax.broadcasted_iota(jnp.int32, (KEYS, 128), 1) < EHD

    def doubled(cols):
        both = states[:, cols]
        return jnp.concatenate(
            [jnp.where(left, both, 0.0), jnp.where(left, 0.0, both)], axis=0
        ).astype(BF16)

    for j in range(7):
        keys = doubled(slice(128 * j, 128 * j + 128))
        escore[j] = dot(eq_s[:, 128 * j : 128 * j + 128], keys, LAST) * (1.0 / math.sqrt(EHD))
    for j in range(7):
        scores = escore[j]
        top_left = jnp.max(jnp.where(left_wide, scores, NEG_LARGE), axis=-1, keepdims=True)
        top_right = jnp.max(jnp.where(left_wide, NEG_LARGE, scores), axis=-1, keepdims=True)
        weights = jnp.exp(scores - jnp.where(left_wide, top_left, top_right))
        sum_left = jnp.sum(jnp.where(left_wide, weights, 0.0), axis=-1, keepdims=True)
        sum_right = jnp.sum(jnp.where(left_wide, 0.0, weights), axis=-1, keepdims=True)
        escore[j] = weights / jnp.where(left_wide, sum_left, sum_right)
    for j in range(7):
        values = doubled(slice(E + 128 * j, E + 128 * j + 128))
        ectx[:, 128 * j : 128 * j + 128] = dot(escore[j].astype(BF16), values).astype(BF16)
    loads[4].wait()
    enc[at.x] = (enc_in[...].astype(F32) + dot(ectx[...], eout[...])).astype(BF16)
    c_e1 = (
        send(enc.at[at.x], enc.at[at.x], at.along("x", 1)),
        send(enc.at[at.x], enc.at[at.x], at.along("x", 3)),
    )
    relayed(1)
    loads[5].wait()
    loads[6].wait()

    def project(block):
        @pl.loop(0, 4)
        def _(i):
            cols = pl.ds(pl.multiple_of(i * 256, 256), 256)
            ks[block, :, cols] = dot(enc[block], wk[:, cols]).astype(BF16)
            vs[block, :, cols] = dot(enc[block], wv[:, cols]).astype(BF16)

        write(ks.at[block], k_out.at[block])
        write(vs.at[block], v_out.at[block])

    c_nrm.wait_recv()
    write(nrm, nrm_out)
    crossed(0, 0)
    accumulate([(0, 0), (1, 0), (3, 0), (0, 1), (0, 3)], begin=True)
    crossed(1, 3)
    crossed(1, 1)
    project(at.x)
    crossed(0, 3)
    crossed(0, 1)
    c_e1[0].wait_recv()
    c_e2 = [send(enc.at[down, 0:128], enc.at[down, 0:128], at.along("x", 1))]
    c_e1[1].wait_recv()
    c_e2.append(send(enc.at[up, 128:256], enc.at[up, 128:256], at.along("x", 3)))
    project(down)
    project(up)
    accumulate([(1, 1), (1, 3), (3, 1), (3, 3)])
    crossed(1, 2)
    crossed(0, 2)
    landed(0, 0)
    landed(1, 0)
    accumulate([(2, 0), (0, 2)])
    c_e2[0].wait_recv()
    c_e2[1].wait_recv()
    project(far)
    for line in (3, 1):
        landed(0, line)
        landed(1, line)
    accumulate([(2, 1), (2, 3), (1, 2), (3, 2)])
    landed(0, 2)
    landed(1, 2)
    accumulate([(2, 2)])
    q_send[...] = acc[256:512].astype(BF16)
    c_q = send(q_send, q_in, at.sibling())
    c_q.wait_recv()
    q_ref[...] = (acc[0:256] + q_in[...].astype(F32)).astype(BF16)
    for copy in send.copies:
        copy.wait_send()
    for copy in outs:
        copy.wait()


FORWARD_SENDS = 4 + 1 + 4 + 2 * 6 + 2 * 2 + 16 + 2 + 2 + 1 + 2 + 2 + 1


def forward(tokens, w_query, gain, state_kv, near, enc_gain, enc_query, enc_out, w_key, w_value):
    rows, full = tokens.shape
    width = w_query.shape[1]
    vmem = pl.BlockSpec(memory_space=pltpu.VMEM)
    anywhere = pl.BlockSpec(memory_space=pl.ANY)

    def buffer(*shape, kind=BF16):
        return pltpu.VMEM(shape, kind)

    return pl.pallas_call(
        forward_kernel,
        in_specs=[anywhere, anywhere, vmem, anywhere, anywhere, vmem] + [anywhere] * 4,
        out_specs=[vmem] + [anywhere] * 4 + [vmem],
        out_shape=[
            jax.ShapeDtypeStruct((rows, width), BF16),
            jax.ShapeDtypeStruct((16, CHUNK, width), BF16),
            jax.ShapeDtypeStruct((16, 2 * rows, CHUNK), BF16),
            jax.ShapeDtypeStruct((4, KEYS, width), BF16),
            jax.ShapeDtypeStruct((4, KEYS, width), BF16),
            jax.ShapeDtypeStruct((rows, 128), F32),
        ],
        scratch_shapes=[
            buffer(rows, full),
            buffer(16, CHUNK, width),
            buffer(16, 2 * rows, CHUNK),
            buffer(16, rows, CHUNK),
            buffer(full // 4, 2 * E),
            buffer(rows, full // 4),
            buffer(2 * rows, width, kind=F32),
            buffer(rows, width),
            buffer(rows, width),
            buffer(4, BLOCK, 2 * E),
            buffer(2, BLOCK // 2, 2 * E),
            buffer(2, BLOCK, 2 * E),
            buffer(KEYS, E),
            buffer(KEYS, E),
            buffer(KEYS, E),
            buffer(7, KEYS, 128, kind=F32),
            buffer(E, E),
            buffer(E, E),
            buffer(4, KEYS, E),
            buffer(E, width),
            buffer(E, width),
            buffer(4, KEYS, width),
            buffer(4, KEYS, width),
            pltpu.SemaphoreType.DMA((7,)),
            pltpu.SemaphoreType.DMA((25,)),
            pltpu.SemaphoreType.DMA((FORWARD_SENDS,)),
            pltpu.SemaphoreType.DMA((FORWARD_SENDS,)),
        ],
        compiler_params=pltpu.CompilerParams(
            collective_id=2, has_side_effects=True, vmem_limit_bytes=60 * 2**20
        ),
        cost_estimate=pl.CostEstimate(
            flops=2 * 5400 * 2**20, bytes_accessed=40 * 2**20, transcendentals=0
        ),
    )(tokens, w_query, gain, state_kv, near, enc_gain, enc_query, enc_out, w_key, w_value)


LINES = (2, 1, 3, 0)
GROUPS = ((0, 256, 96), (256, 1024, 288))
LOADS = 16


def halves(group):
    first, stop, z_first = GROUPS[group]
    return z_first, stop - first - z_first


def backward_kernel(
    counts, q_ref, k_ref, v_ref, do_ref, wk_ref, wv_ref, nrm_ref, w_ref, tokens_ref,
    inverse_ref, gain_ref,
    ctx_ref, dw_ref, dh_ref, de_ref, dots_ref,
    qs, dos, ks, vs, wk, wv, ctx, score_s, dprob_s, weight_s, dscore_s, sum_s,
    dq2, dq_t, nrm, wc, prod, dw_t, part, rn1, rn2, out_sib, in_sib,
    grads, g1, gs, g2, gfin, gin, sums, sums_in, tok, column,
    ra1_00, ra1_01, ra1_10, ra1_11, ra2_00, ra2_01, ra2_10, ra2_11,
    rb1_00, rb1_01, rb1_10, rb1_11, rb2_00, rb2_01, rb2_10, rb2_11,
    load_sem, out_sem, send_sem, recv_sem,
):
    at = Place()
    width = tokens_ref.shape[1]
    share = width // 4
    ra1 = ((ra1_00, ra1_01), (ra1_10, ra1_11))
    ra2 = ((ra2_00, ra2_01), (ra2_10, ra2_11))
    rb1 = ((rb1_00, rb1_01), (rb1_10, rb1_11))
    rb2 = ((rb2_00, rb2_01), (rb2_10, rb2_11))
    pairs = [
        (q_ref, qs), (do_ref, dos), (k_ref, ks), (v_ref, vs), (wk_ref, wk), (wv_ref, wv),
        (nrm_ref, nrm), (w_ref, wc),
    ]
    for i in range(8):
        first = pl.multiple_of(at.x * share + i * 256, 256)
        pairs.append((tokens_ref.at[:, pl.ds(first, 256)], tok.at[i]))
    loads = [pltpu.make_async_copy(src, dst, load_sem.at[i]) for i, (src, dst) in enumerate(pairs)]
    for load in loads:
        load.start()
    barrier = pltpu.get_barrier_semaphore()
    friends = [at.along("x", 1), at.along("x", 2), at.along("x", 3), at.along("y", 1),
               at.along("y", 3), at.along("z", 1), at.along("z", 3), at.sibling()]
    for friend in friends:
        pl.semaphore_signal(barrier, inc=1, device_id=friend, device_id_type=MESH)

    send = Sender(send_sem, recv_sem)
    far, up, down = (at.x + 2) % 4, (at.x + 1) % 4, (at.x + 3) % 4
    scale = 1.0 / math.sqrt(HD)

    def added(dst, first, second):
        dst[...] = (first[...].astype(F32) + second[...].astype(F32)).astype(BF16)

    def both(dim, one, other):
        return send(*one, at.along(dim, 1)), send(*other, at.along(dim, 3))

    def attention(b, group):
        first, stop, _ = GROUPS[group]
        spans = [slice(low, low + HD) for low in range(first, stop, HD)]
        rows = pl.ds(pl.multiple_of(b * BLOCK, BLOCK), BLOCK)
        count = counts[b]
        valid = lax.broadcasted_iota(jnp.int32, (BLOCK, KEYS), 1) < count * RLEN
        empty = jnp.where(count == 0, 1.0, 0.0).astype(F32)
        for i, cols in enumerate(spans):
            score_s[i] = dot(qs[rows, cols], ks[b, :, cols], LAST) * scale
            dprob_s[i] = dot(dos[rows, cols], vs[b, :, cols], LAST)
        for i in range(len(spans)):
            scores = score_s[i]
            top = jnp.max(jnp.where(valid, scores, NEG_LARGE), axis=-1, keepdims=True)
            weights = jnp.where(valid, jnp.exp(scores - top), 0.0)
            probs = weights / (jnp.sum(weights, axis=-1, keepdims=True) + empty)
            weight_s[i] = probs.astype(BF16)
            d_probs = dprob_s[i]
            inner = jnp.sum(probs * d_probs, axis=-1, keepdims=True)
            dscore_s[i] = (probs * (d_probs - inner) * scale).astype(BF16)
        total = jnp.zeros((BLOCK, HD), F32)
        for i, cols in enumerate(spans):
            ctx[rows, cols] = dot(weight_s[i], vs[b, :, cols]).astype(BF16)
            dq = dot(dscore_s[i], ks[b, :, cols])
            dq2[rows, cols] = dq.astype(BF16)
            total = total + dq * qs[rows, cols].astype(F32)
            vs[b, :, cols] = dot(weight_s[i], dos[rows, cols], FIRST).astype(BF16)
            ks[b, :, cols] = dot(dscore_s[i], qs[rows, cols], FIRST).astype(BF16)
        sum_s[rows, :] = total if group == 0 else sum_s[rows, :] + total

    def encoded_grad(b):
        grad = dot(ks[b], wk[...], LAST) + dot(vs[b], wv[...], LAST)
        grads[b] = grad.astype(BF16)

    def share_dq(group):
        first, stop, _ = GROUPS[group]
        return send(dq2.at[0:256, first:stop], dq2.at[256:512, first:stop], at.sibling())

    def transposed(group, rows):
        first, stop, _ = GROUPS[group]
        for low in range(first, stop, 256):
            dq_t[low : low + 256, rows] = jnp.transpose(dq2[rows, low : low + 256])

    def product(group, dy, dz):
        k = at.chunk(dy, dz)
        first, stop, _ = GROUPS[group]
        prod[k, first:stop] = dot(dq_t[first:stop], nrm[k]).astype(BF16)

    dims = (("z", "y"), ("y", "z"))

    def block(group, half, line, off, part=None):
        dy, dz = (line, off) if half == 0 else (off, line)
        first, stop, z_first = GROUPS[group]
        low, high = ((first, first + z_first), (first + z_first, stop))[half]
        middle = (low + high) // 2
        low, high = (low, high) if part is None else ((low, middle), (middle, high))[part]
        return prod.at[at.chunk(dy, dz), low:high]

    c1, c2, d1, d2 = {}, {}, {}, {}

    def first_hop(group, half, line):
        slot = ra1[group][half].at[LINES.index(line)]
        c1[group, half, line] = both(
            dims[half][0],
            (block(group, half, line, 2, 0), slot.at[0]),
            (block(group, half, line, 2, 1), slot.at[1]),
        )

    def second_hop(group, half, line):
        for way, off in ((0, 1), (1, 3)):
            c1[group, half, line][way].wait_recv()
            piece = block(group, half, line, off, way)
            added(piece, piece, ra1[group][half].at[LINES.index(line), way])
        slot = ra2[group][half].at[LINES.index(line)]
        c2[group, half, line] = both(
            dims[half][0],
            (block(group, half, line, 1), slot.at[0]),
            (block(group, half, line, 3), slot.at[1]),
        )

    def gathered(group, half, line):
        for way in (0, 1):
            c2[group, half, line][way].wait_recv()
        slot = ra2[group][half].at[LINES.index(line)]
        piece = block(group, half, line, 0)
        total = piece[...].astype(F32) + slot[0].astype(F32) + slot[1].astype(F32)
        piece[...] = total.astype(BF16)

    def turn(group, half):
        d1[group, half] = both(
            dims[half][1],
            (block(group, half, 2, 0, 0), rb1[group][half].at[0]),
            (block(group, half, 2, 0, 1), rb1[group][half].at[1]),
        )

    def turned(group, half):
        for way, off in ((0, 1), (1, 3)):
            d1[group, half][way].wait_recv()
            piece = block(group, half, off, 0, way)
            added(piece, piece, rb1[group][half].at[way])
        d2[group, half] = both(
            dims[half][1],
            (block(group, half, 1, 0), rb2[group][half].at[0]),
            (block(group, half, 3, 0), rb2[group][half].at[1]),
        )

    def result(group):
        first, stop, _ = GROUPS[group]
        sizes = halves(group)
        for half in (0, 1):
            for way in (0, 1):
                c2[group, half, 0][way].wait_recv()
                d2[group, half][way].wait_recv()
            own = block(group, half, 0, 0)
            slot = ra2[group][half].at[LINES.index(0)]
            total = own[...].astype(F32) + slot[0].astype(F32) + slot[1].astype(F32)
            low = half * sizes[0]
            dw_t[low : low + sizes[half]] = (
                total + rb2[group][half][0].astype(F32) + rb2[group][half][1].astype(F32)
            )
        for low in range(0, stop - first, 128):
            dw_ref[:, first + low : first + low + 128] = jnp.transpose(dw_t[low : low + 128])

    def partial(k):
        part[k] = dot(dq2[...], wc[k], LAST).astype(BF16)

    n1, n2 = [], []

    def far_partial(m):
        partial(far * 4 + m)
        n1.append(
            both("x", (part.at[far * 4 + m, 0:256], rn1.at[m, 0]),
                 (part.at[far * 4 + m, 256:512], rn1.at[m, 1]))
        )

    def near_partial(m):
        n1[m][0].wait_recv()
        piece = part.at[up * 4 + m, 0:256]
        added(piece, piece, rn1.at[m, 0])
        n1[m][1].wait_recv()
        piece = part.at[down * 4 + m, 256:512]
        added(piece, piece, rn1.at[m, 1])
        n2.append(
            both("x", (part.at[up * 4 + m], rn2.at[m, 0]), (part.at[down * 4 + m], rn2.at[m, 1]))
        )

    outs = []

    def write(src, dst):
        copy = pltpu.make_async_copy(src, dst, out_sem.at[len(outs)])
        copy.start()
        outs.append(copy)

    def finish(i, d_normed):
        inverse = wide(inverse_ref[...])
        unit = tok[i].astype(F32) * inverse
        parts = d_normed * gain_ref[at.x * 8 + i]
        result = inverse * (parts - unit * (wide(column[...]) * (1.0 / width)))
        tok[i] = result.astype(BF16)
        first = pl.multiple_of(i * 256, 256)
        write(tok.at[i], dh_ref.at[:, pl.ds(first, 256)])

    c_sib = []

    def normed_sum(m):
        for copy in n2[m]:
            copy.wait_recv()

        def summed(low):
            rows = slice(low, low + 256)
            total = part[at.x * 4 + m, rows].astype(F32) + rn2[m, 0, rows].astype(F32)
            return total + rn2[m, 1, rows].astype(F32)

        out_sib[m] = summed(256).astype(BF16)
        c_sib.append(send(out_sib.at[m], in_sib.at[m], at.sibling()))
        finish(2 * m + at.core, summed(0))

    def sibling_part(m):
        c_sib[m].wait_recv()
        finish(2 * m + 1 - at.core, in_sib[m].astype(F32))

    for load in loads[:4]:
        load.wait()

    @pl.loop(0, 4)
    def _(b):
        attention(b, 0)

    pl.semaphore_wait(barrier, len(friends))
    c_dq = [share_dq(0)]
    own, other = slice(0, 256), slice(256, 512)
    transposed(0, own)
    for load in loads[4:8]:
        load.wait()
    attention(far, 1)
    encoded_grad(far)
    c_g1 = both("x", (grads.at[far, 0:128], g1.at[0]), (grads.at[far, 128:256], g1.at[1]))
    c_dq[0].wait_recv()
    transposed(0, other)
    product(0, 2, 2)
    first_hop(0, 1, 2)
    first_hop(0, 0, 2)
    for line in (1, 3, 0):
        product(0, 2, line)
        first_hop(0, 1, line)
        product(0, line, 2)
        first_hop(0, 0, line)
    attention(up, 1)
    second_hop(0, 1, 2)
    second_hop(0, 0, 2)
    corners = ((1, 1), (3, 1), (1, 3), (3, 3))
    rest = ((1, 0), (3, 0), (0, 1), (0, 3), (0, 0))
    for dy, dz in corners:
        product(0, dy, dz)
    for line in (1, 3):
        second_hop(0, 1, line)
        second_hop(0, 0, line)
    attention(down, 1)
    encoded_grad(up)
    encoded_grad(down)
    c_g1[0].wait_recv()
    c_g1[1].wait_recv()
    gs[0, 0:128] = (grads[up, 0:128].astype(F32) + g1[0].astype(F32)).astype(BF16)
    gs[0, 128:256] = grads[up, 128:256]
    gs[1, 0:128] = grads[down, 0:128]
    gs[1, 128:256] = (grads[down, 128:256].astype(F32) + g1[1].astype(F32)).astype(BF16)
    c_g2 = both("x", (gs.at[0], g2.at[0]), (gs.at[1], g2.at[1]))
    attention(at.x, 1)
    c_dq.append(share_dq(1))
    write(ctx, ctx_ref)
    for half in (0, 1):
        gathered(0, half, 2)
        turn(0, half)
    lanes = jnp.sum(jnp.transpose(sum_s[...]), axis=0, keepdims=True)
    sums[...] = jnp.broadcast_to(lanes, (8, 256))
    c_sums = [send(sums, sums_in.at[i], at.along("x", i + 1)) for i in range(3)]
    transposed(1, own)
    c_dq[1].wait_recv()
    transposed(1, other)
    product(1, 2, 2)
    first_hop(1, 1, 2)
    first_hop(1, 0, 2)
    for line in (1, 3, 0):
        product(1, 2, line)
        first_hop(1, 1, line)
        product(1, line, 2)
        first_hop(1, 0, line)
    for dy, dz in rest:
        product(0, dy, dz)
    for half in (0, 1):
        gathered(0, half, 1)
        gathered(0, half, 3)
        turned(0, half)
    second_hop(1, 0, 2)
    for m in range(4):
        far_partial(m)
    second_hop(1, 1, 2)
    for dy, dz in corners:
        product(1, dy, dz)
    for line in (1, 3):
        second_hop(1, 0, line)
        second_hop(1, 1, line)
    for m in range(4):
        partial(up * 4 + m)
        partial(down * 4 + m)
        near_partial(m)
    for dy, dz in rest:
        product(1, dy, dz)
    second_hop(0, 0, 0)
    second_hop(1, 0, 0)
    gathered(1, 0, 2)
    turn(1, 0)
    encoded_grad(at.x)
    for copy in c_g2:
        copy.wait_recv()
    gfin[...] = (grads[at.x].astype(F32) + g2[0].astype(F32) + g2[1].astype(F32)).astype(BF16)
    gathered(1, 1, 2)
    turn(1, 1)
    c_swap = send(gfin, gin, at.partner())
    second_hop(0, 1, 0)
    gathered(1, 0, 1)
    gathered(1, 0, 3)
    turned(1, 0)
    second_hop(1, 1, 0)

    for copy in c_sums:
        copy.wait_recv()
    whole = sums[...] + sums_in[0] + sums_in[1] + sums_in[2]
    dots_ref[...] = whole[0:1] * (1.0 / math.sqrt(width))
    column[...] = jnp.transpose(jnp.broadcast_to(whole[0:1], (128, 256)))
    for load in loads[8:]:
        load.wait()
    for m in range(4):
        partial(at.x * 4 + m)
    normed_sum(0)
    normed_sum(1)
    sibling_part(0)
    gathered(1, 1, 1)
    gathered(1, 1, 3)
    turned(1, 1)
    normed_sum(2)
    sibling_part(1)
    result(0)
    normed_sum(3)
    sibling_part(2)
    sibling_part(3)
    result(1)
    c_swap.wait_recv()
    write(gin, de_ref)
    for copy in send.copies:
        copy.wait_send()
    for copy in outs:
        copy.wait()


BACKWARD_SENDS = 2 + 2 + 2 + 8 + 8 + 3 + 1 + 4 + 2 * 40


def backward(
    counts, queries, keys, values, d_context, w_key, w_value, normed, w_all, tokens, inverse, gain
):
    rows, width = queries.shape
    full = tokens.shape[1]
    vmem = pl.BlockSpec(memory_space=pltpu.VMEM)
    anywhere = pl.BlockSpec(memory_space=pl.ANY)

    def buffer(*shape, kind=BF16):
        return pltpu.VMEM(shape, kind)

    sizes = [size for group in range(2) for size in halves(group)]
    return pl.pallas_call(
        backward_kernel,
        in_specs=[pl.BlockSpec(memory_space=pltpu.SMEM)] + [anywhere] * 9 + [vmem, vmem],
        out_specs=[anywhere, vmem, anywhere, anywhere, vmem],
        out_shape=[
            jax.ShapeDtypeStruct((rows, width), BF16),
            jax.ShapeDtypeStruct((256, width), F32),
            jax.ShapeDtypeStruct((rows, full // 4), BF16),
            jax.ShapeDtypeStruct((KEYS, E), BF16),
            jax.ShapeDtypeStruct((1, rows), F32),
        ],
        scratch_shapes=[
            buffer(rows, width),
            buffer(rows, width),
            buffer(4, KEYS, width),
            buffer(4, KEYS, width),
            buffer(E, width),
            buffer(E, width),
            buffer(rows, width),
            buffer(6, BLOCK, KEYS, kind=F32),
            buffer(6, BLOCK, KEYS, kind=F32),
            buffer(6, BLOCK, KEYS),
            buffer(6, BLOCK, KEYS),
            buffer(rows, HD, kind=F32),
            buffer(512, 1024),
            buffer(1024, 512),
            buffer(16, 512, 256),
            buffer(16, 256, 1024),
            buffer(16, 1024, 256),
            buffer(768, 256, kind=F32),
            buffer(16, 512, 256),
            buffer(4, 2, 256, 256),
            buffer(4, 2, 512, 256),
            buffer(4, 256, 256),
            buffer(4, 256, 256),
            buffer(4, KEYS, E),
            buffer(2, 128, E),
            buffer(2, 256, E),
            buffer(2, 256, E),
            buffer(256, E),
            buffer(256, E),
            buffer(8, 256, kind=F32),
            buffer(3, 8, 256, kind=F32),
            buffer(8, 256, 256),
            buffer(256, 128, kind=F32),
        ]
        + [buffer(4, 2, size // 2, 256) for size in sizes]
        + [buffer(4, 2, size, 256) for size in sizes]
        + [buffer(2, size // 2, 256) for size in sizes]
        + [buffer(2, size, 256) for size in sizes]
        + [
            pltpu.SemaphoreType.DMA((LOADS,)),
            pltpu.SemaphoreType.DMA((10,)),
            pltpu.SemaphoreType.DMA((BACKWARD_SENDS,)),
            pltpu.SemaphoreType.DMA((BACKWARD_SENDS,)),
        ],
        compiler_params=pltpu.CompilerParams(
            collective_id=1, has_side_effects=True, vmem_limit_bytes=62 * 2**20
        ),
        cost_estimate=pl.CostEstimate(
            flops=12 * 2**30, bytes_accessed=30 * 2**20, transcendentals=0
        ),
    )(counts, queries, keys, values, d_context, w_key, w_value, normed, w_all, tokens, inverse, gain)


def shards(
    tokens,
    w_query,
    query_gain,
    state_kv,
    neighbours,
    enc_gain,
    enc_query,
    enc_out,
    w_key,
    w_value,
    counts,
    d_context,
):
    gain = query_gain.reshape(32, 1, 256)
    queries, w_part, normed, keys, values, inverse = forward(
        tokens, w_query, gain, state_kv, neighbours.reshape(KEYS, E), enc_gain.reshape(1, E),
        enc_query, enc_out, w_key, w_value,
    )
    context, d_query_weight, d_hidden, d_encoded, row_dots = backward(
        counts, queries, keys, values, d_context, w_key, w_value, normed, w_part, tokens, inverse,
        gain,
    )
    return (
        context,
        d_hidden,
        d_query_weight,
        d_encoded.reshape(1, 1, NBR, RLEN, E),
        row_dots[0],
    )


def solution(mesh):
    return jax.shard_map(
        shards,
        mesh=mesh,
        in_specs=(
            P(("section", "seq"), None),
            P(("section", "seq"), "tensor"),
            P(),
            P("tensor", None),
            P("section", ("seq", "tensor"), None, None, None),
            P(),
            P(),
            P(),
            P(None, "tensor"),
            P(None, "tensor"),
            P(("section", "seq")),
            P(("section", "seq"), "tensor"),
        ),
        out_specs=(
            P(("section", "seq"), "tensor"),
            P(("section", "seq"), "tensor"),
            P(("section", "seq"), "tensor"),
            P("section", ("seq", "tensor"), None, None, None),
            P(("section", "seq")),
        ),
        check_vma=False,
    )
```

```python
import functools
import math

import jax
import jax.numpy as jnp
from jax import lax
from jax.experimental import pallas as pl
from jax.experimental.pallas import tpu as pltpu
from jax.sharding import PartitionSpec as P

HD = 128
E = 896
EHD = 64
BLOCK = 64
NBR = 2
RLEN = 128
KEYS = NBR * RLEN

EPSILON = 1e-05
NEG_LARGE = -1e30
MESH = pl.DeviceIdType.MESH
F32 = jnp.float32
BF16 = jnp.bfloat16
LAST = (((1,), (1,)), ((), ()))
FIRST = (((0,), (0,)), ((), ()))


def dot(a, b, dims=(((1,), (0,)), ((), ()))):
    return lax.dot_general(a, b, dims, preferred_element_type=F32)


class Place:
    def __init__(self):
        self.section = lax.axis_index("section")
        seq = lax.axis_index("seq")
        self.x = lax.axis_index("tensor")
        self.core = seq % 2
        self.y = seq // 4
        self.z = 2 * ((seq // 2) % 2) + self.section

    def along(self, dim, off):
        if dim == "x":
            return (self.section, self.seq_of(self.y, self.z), (self.x + off) % 4)
        if dim == "y":
            return (self.section, self.seq_of((self.y + off) % 4, self.z), self.x)
        z = (self.z + off) % 4
        return (z % 2, self.seq_of(self.y, z), self.x)

    def seq_of(self, y, z):
        return y * 4 + (z // 2) * 2 + self.core

    def sibling(self):
        return (self.section, self.y * 4 + (self.z // 2) * 2 + 1 - self.core, self.x)

    def partner(self):
        return (1 - self.section, self.seq_of(self.y, self.z), self.x)

    def chunk(self, dy, dz):
        y, z = (self.y + dy) % 4, (self.z + dz) % 4
        return (z % 2) * 8 + y * 2 + z // 2


def greet(devices):
    barrier = pltpu.get_barrier_semaphore()
    for device in devices:
        pl.semaphore_signal(barrier, inc=1, device_id=device, device_id_type=MESH)
    pl.semaphore_wait(barrier, len(devices))


class Sender:
    def __init__(self, send_sem, recv_sem):
        self.send_sem, self.recv_sem, self.copies = send_sem, recv_sem, []

    def __call__(self, src, dst, device):
        index = len(self.copies)
        copy = pltpu.make_async_remote_copy(
            src_ref=src, dst_ref=dst, send_sem=self.send_sem.at[index],
            recv_sem=self.recv_sem.at[index], device_id=device, device_id_type=MESH,
        )
        copy.start()
        self.copies.append(copy)
        return copy


Y_FIRST = 96
CHUNK = 256


def wide(column):
    return jnp.concatenate([column, column], axis=1)


def forward_kernel(
    tokens_ref, w_ref, gain_ref, state_ref, near_ref, egain_ref, equery_ref, eout_ref, wk_ref, wv_ref,
    q_ref, w_out, nrm_out, k_out, v_out, inv_ref,
    tok, wc, nrm, theirs, skv, unit, acc, q_send, q_in,
    sp, sr1, sr2, enc_in, eq_s, ectx, escore, equery, eout, enc, wk, wv, ks, vs,
    load_sem, out_sem, send_sem, recv_sem,
):
    at = Place()
    share = tok.shape[1] // 4
    send = Sender(send_sem, recv_sem)
    me = at.chunk(0, 0)
    pairs = (
        (w_ref, wc.at[me]), (tokens_ref, tok), (state_ref, skv), (equery_ref, equery),
        (eout_ref, eout), (wk_ref, wk), (wv_ref, wv),
    )
    loads = [pltpu.make_async_copy(src, dst, load_sem.at[i]) for i, (src, dst) in enumerate(pairs)]
    for load in loads:
        load.start()
    greet(
        [at.along("x", 1), at.along("x", 3), at.along("y", 1), at.along("y", 3),
         at.along("z", 1), at.along("z", 3), at.sibling()]
    )

    dims = (("y", "z"), ("z", "y"))
    spans = ((0, Y_FIRST), (Y_FIRST, CHUNK))

    def piece(half, first, second, part=None):
        dy, dz = (first, second) if half == 0 else (second, first)
        low, high = spans[half]
        middle = (low + high) // 2
        low, high = (low, high) if part is None else ((low, middle), (middle, high))[part]
        return wc.at[at.chunk(dy, dz), low:high]

    def pass_on(ref, dim, off):
        return send(ref, ref, at.along(dim, off))

    near, relay, cross, last = {}, {}, {}, {}

    def across(half, line):
        dim = dims[half][1]
        block = piece(half, line, 0)
        cross[half, line] = (pass_on(block, dim, 1), pass_on(block, dim, 3))

    def relays(half):
        dim = dims[half][0]
        near[half][0].wait_recv()
        first = pass_on(piece(half, 3, 0, 0), dim, 1)
        near[half][1].wait_recv()
        relay[half] = (first, pass_on(piece(half, 1, 0, 1), dim, 3))

    def relayed(half):
        relay[half][0].wait_recv()
        relay[half][1].wait_recv()
        across(half, 2)

    def crossed(half, line):
        dim = dims[half][1]
        cross[half, line][0].wait_recv()
        first = pass_on(piece(half, line, 3, 0), dim, 1)
        cross[half, line][1].wait_recv()
        last[half, line] = (first, pass_on(piece(half, line, 1, 1), dim, 3))

    def landed(half, line):
        last[half, line][0].wait_recv()
        last[half, line][1].wait_recv()

    outs = []

    def write(src, dst):
        copy = pltpu.make_async_copy(src, dst, out_sem.at[len(outs)])
        copy.start()
        outs.append(copy)

    def accumulate(offsets, begin=False):
        chunks = [at.chunk(dy, dz) for dy, dz in offsets]
        for k in chunks:
            write(wc.at[k], w_out.at[k])

        @pl.loop(0, 4)
        def _(i):
            rows = pl.ds(pl.multiple_of((i // 2) * 256, 256), 256)
            cols = pl.ds(pl.multiple_of((i % 2) * 512, 512), 512)
            total = dot(nrm[chunks[0], rows, :], wc[chunks[0], :, cols])
            for k in chunks[1:]:
                total = total + dot(nrm[k, rows, :], wc[k, :, cols])
            acc[rows, cols] = total if begin else acc[rows, cols] + total

    loads[0].wait()
    for half in (0, 1):
        block = piece(half, 0, 0)
        near[half] = (pass_on(block, dims[half][0], 1), pass_on(block, dims[half][0], 3))
    c_near = send(near_ref, enc_in, at.partner())
    across(1, 0)

    loads[1].wait()

    @pl.loop(0, 16)
    def _(i):
        rows = pl.ds(pl.multiple_of(i * 16, 16), 16)
        values = tok[rows, :].astype(F32)
        square = jnp.sum(values * values, axis=-1, keepdims=True)
        inverse = lax.rsqrt(square * (1.0 / tok.shape[1]) + EPSILON)
        inv_ref[rows, :] = jnp.broadcast_to(inverse, (16, 128))

    @pl.loop(0, 8)
    def _(i):
        source = pl.ds(pl.multiple_of(at.x * share + i * 256, 256), 256)
        target = pl.ds(pl.multiple_of(i * 256, 256), 256)
        unit[:, target] = (tok[:, source].astype(F32) * wide(inv_ref[...])).astype(BF16)

    loads[2].wait()

    @pl.loop(0, 7)
    def _(i):
        cols = pl.ds(pl.multiple_of(i * 256, 256), 256)
        part = dot(unit[...], skv[:, cols]).astype(BF16)
        for j in range(4):
            sp[j, :, cols] = part[64 * j : 64 * j + 64]

    far, up, down = (at.x + 2) % 4, (at.x + 1) % 4, (at.x + 3) % 4
    c_s1 = (
        send(sp.at[far, 0:32], sr1.at[0], at.along("x", 1)),
        send(sp.at[far, 32:64], sr1.at[1], at.along("x", 3)),
    )
    relays(0)
    relays(1)
    across(1, 3)
    across(1, 1)
    for line in (0, 3, 1):
        across(0, line)

    @pl.loop(0, 16)
    def _(k):
        def chunk(g):
            cols = pl.ds(pl.multiple_of(g * CHUNK, CHUNK), CHUNK)
            return (tok[:, cols].astype(F32) * wide(inv_ref[...]) * gain_ref[g]).astype(BF16)

        nrm[k, 0:256] = chunk(2 * k + at.core)
        theirs[k] = chunk(2 * k + 1 - at.core)

    c_nrm = send(theirs, nrm.at[:, 256:512], at.sibling())

    for way, block in ((0, up), (1, down)):
        c_s1[way].wait_recv()
        rows = slice(32 * way, 32 * way + 32)
        sp[block, rows] = (sp[block, rows].astype(F32) + sr1[way].astype(F32)).astype(BF16)
    c_s2 = (
        send(sp.at[up], sr2.at[0], at.along("x", 1)),
        send(sp.at[down], sr2.at[1], at.along("x", 3)),
    )
    relayed(0)
    crossed(1, 0)

    loads[3].wait()
    c_near.wait_recv()
    enc_rows = enc_in[...].astype(F32)
    mean = jnp.sum(enc_rows * enc_rows, axis=-1, keepdims=True) * (1.0 / E)
    enc_normed = (enc_rows * lax.rsqrt(mean + EPSILON) * egain_ref[...].reshape(1, E)).astype(BF16)
    eq_s[...] = dot(enc_normed, equery[...]).astype(BF16)

    c_s2[0].wait_recv()
    c_s2[1].wait_recv()
    states = (sp[at.x].astype(F32) + sr2[0].astype(F32) + sr2[1].astype(F32)).astype(BF16)
    states = states.astype(F32)
    left = lax.broadcasted_iota(jnp.int32, (BLOCK, 128), 1) < EHD
    left_wide = lax.broadcasted_iota(jnp.int32, (KEYS, 128), 1) < EHD

    def doubled(cols):
        both = states[:, cols]
        return jnp.concatenate(
            [jnp.where(left, both, 0.0), jnp.where(left, 0.0, both)], axis=0
        ).astype(BF16)

    for j in range(7):
        keys = doubled(slice(128 * j, 128 * j + 128))
        escore[j] = dot(eq_s[:, 128 * j : 128 * j + 128], keys, LAST) * (1.0 / math.sqrt(EHD))
    for j in range(7):
        scores = escore[j]
        top_left = jnp.max(jnp.where(left_wide, scores, NEG_LARGE), axis=-1, keepdims=True)
        top_right = jnp.max(jnp.where(left_wide, NEG_LARGE, scores), axis=-1, keepdims=True)
        weights = jnp.exp(scores - jnp.where(left_wide, top_left, top_right))
        sum_left = jnp.sum(jnp.where(left_wide, weights, 0.0), axis=-1, keepdims=True)
        sum_right = jnp.sum(jnp.where(left_wide, 0.0, weights), axis=-1, keepdims=True)
        escore[j] = weights / jnp.where(left_wide, sum_left, sum_right)
    for j in range(7):
        values = doubled(slice(E + 128 * j, E + 128 * j + 128))
        ectx[:, 128 * j : 128 * j + 128] = dot(escore[j].astype(BF16), values).astype(BF16)
    loads[4].wait()
    enc[at.x] = (enc_in[...].astype(F32) + dot(ectx[...], eout[...])).astype(BF16)
    c_e1 = (
        send(enc.at[at.x], enc.at[at.x], at.along("x", 1)),
        send(enc.at[at.x], enc.at[at.x], at.along("x", 3)),
    )
    relayed(1)
    loads[5].wait()
    loads[6].wait()

    def project(block):
        @pl.loop(0, 4)
        def _(i):
            cols = pl.ds(pl.multiple_of(i * 256, 256), 256)
            ks[block, :, cols] = dot(enc[block], wk[:, cols]).astype(BF16)
            vs[block, :, cols] = dot(enc[block], wv[:, cols]).astype(BF16)

        write(ks.at[block], k_out.at[block])
        write(vs.at[block], v_out.at[block])

    c_nrm.wait_recv()
    write(nrm, nrm_out)
    crossed(0, 0)
    accumulate([(0, 0), (1, 0), (3, 0), (0, 1), (0, 3)], begin=True)
    crossed(1, 3)
    crossed(1, 1)
    project(at.x)
    crossed(0, 3)
    crossed(0, 1)
    c_e1[0].wait_recv()
    c_e2 = [send(enc.at[down, 0:128], enc.at[down, 0:128], at.along("x", 1))]
    c_e1[1].wait_recv()
    c_e2.append(send(enc.at[up, 128:256], enc.at[up, 128:256], at.along("x", 3)))
    project(down)
    project(up)
    accumulate([(1, 1), (1, 3), (3, 1), (3, 3)])
    crossed(1, 2)
    crossed(0, 2)
    landed(0, 0)
    landed(1, 0)
    accumulate([(2, 0), (0, 2)])
    c_e2[0].wait_recv()
    c_e2[1].wait_recv()
    project(far)
    for line in (3, 1):
        landed(0, line)
        landed(1, line)
    accumulate([(2, 1), (2, 3), (1, 2), (3, 2)])
    landed(0, 2)
    landed(1, 2)
    accumulate([(2, 2)])
    q_send[...] = acc[256:512].astype(BF16)
    c_q = send(q_send, q_in, at.sibling())
    c_q.wait_recv()
    q_ref[...] = (acc[0:256] + q_in[...].astype(F32)).astype(BF16)
    for copy in send.copies:
        copy.wait_send()
    for copy in outs:
        copy.wait()


FORWARD_SENDS = 4 + 1 + 4 + 2 * 6 + 2 * 2 + 16 + 2 + 2 + 1 + 2 + 2 + 1


def forward(tokens, w_query, gain, state_kv, near, enc_gain, enc_query, enc_out, w_key, w_value):
    rows, full = tokens.shape
    width = w_query.shape[1]
    vmem = pl.BlockSpec(memory_space=pltpu.VMEM)
    anywhere = pl.BlockSpec(memory_space=pl.ANY)

    def buffer(*shape, kind=BF16):
        return pltpu.VMEM(shape, kind)

    return pl.pallas_call(
        forward_kernel,
        in_specs=[anywhere, anywhere, vmem, anywhere, anywhere, vmem] + [anywhere] * 4,
        out_specs=[vmem] + [anywhere] * 4 + [vmem],
        out_shape=[
            jax.ShapeDtypeStruct((rows, width), BF16),
            jax.ShapeDtypeStruct((16, CHUNK, width), BF16),
            jax.ShapeDtypeStruct((16, 2 * rows, CHUNK), BF16),
            jax.ShapeDtypeStruct((4, KEYS, width), BF16),
            jax.ShapeDtypeStruct((4, KEYS, width), BF16),
            jax.ShapeDtypeStruct((rows, 128), F32),
        ],
        scratch_shapes=[
            buffer(rows, full),
            buffer(16, CHUNK, width),
            buffer(16, 2 * rows, CHUNK),
            buffer(16, rows, CHUNK),
            buffer(full // 4, 2 * E),
            buffer(rows, full // 4),
            buffer(2 * rows, width, kind=F32),
            buffer(rows, width),
            buffer(rows, width),
            buffer(4, BLOCK, 2 * E),
            buffer(2, BLOCK // 2, 2 * E),
            buffer(2, BLOCK, 2 * E),
            buffer(KEYS, E),
            buffer(KEYS, E),
            buffer(KEYS, E),
            buffer(7, KEYS, 128, kind=F32),
            buffer(E, E),
            buffer(E, E),
            buffer(4, KEYS, E),
            buffer(E, width),
            buffer(E, width),
            buffer(4, KEYS, width),
            buffer(4, KEYS, width),
            pltpu.SemaphoreType.DMA((7,)),
            pltpu.SemaphoreType.DMA((25,)),
            pltpu.SemaphoreType.DMA((FORWARD_SENDS,)),
            pltpu.SemaphoreType.DMA((FORWARD_SENDS,)),
        ],
        compiler_params=pltpu.CompilerParams(
            collective_id=2, has_side_effects=True, vmem_limit_bytes=60 * 2**20
        ),
        cost_estimate=pl.CostEstimate(
            flops=2 * 5400 * 2**20, bytes_accessed=40 * 2**20, transcendentals=0
        ),
    )(tokens, w_query, gain, state_kv, near, enc_gain, enc_query, enc_out, w_key, w_value)


LINES = (2, 1, 3, 0)
GROUPS = ((0, 256, 96), (256, 1024, 288))
LOADS = 16


def halves(group):
    first, stop, z_first = GROUPS[group]
    return z_first, stop - first - z_first


def backward_kernel(
    counts, q_ref, k_ref, v_ref, do_ref, wk_ref, wv_ref, nrm_ref, w_ref, tokens_ref,
    inverse_ref, gain_ref,
    ctx_ref, dw_ref, dh_ref, de_ref, dots_ref,
    qs, dos, ks, vs, wk, wv, ctx, score_s, dprob_s, weight_s, dscore_s, sum_s,
    dq2, dq_t, nrm, wc, prod, dw_t, part, rn1, rn2, out_sib, in_sib,
    grads, g1, gs, g2, gfin, gin, sums, sums_in, tok, column,
    ra1_00, ra1_01, ra1_10, ra1_11, ra2_00, ra2_01, ra2_10, ra2_11,
    rb1_00, rb1_01, rb1_10, rb1_11, rb2_00, rb2_01, rb2_10, rb2_11,
    load_sem, out_sem, send_sem, recv_sem,
):
    at = Place()
    width = tokens_ref.shape[1]
    share = width // 4
    ra1 = ((ra1_00, ra1_01), (ra1_10, ra1_11))
    ra2 = ((ra2_00, ra2_01), (ra2_10, ra2_11))
    rb1 = ((rb1_00, rb1_01), (rb1_10, rb1_11))
    rb2 = ((rb2_00, rb2_01), (rb2_10, rb2_11))
    pairs = [
        (q_ref, qs), (do_ref, dos), (k_ref, ks), (v_ref, vs), (wk_ref, wk), (wv_ref, wv),
        (nrm_ref, nrm), (w_ref, wc),
    ]
    for i in range(8):
        first = pl.multiple_of(at.x * share + i * 256, 256)
        pairs.append((tokens_ref.at[:, pl.ds(first, 256)], tok.at[i]))
    loads = [pltpu.make_async_copy(src, dst, load_sem.at[i]) for i, (src, dst) in enumerate(pairs)]
    for load in loads[:4]:
        load.start()
    barrier = pltpu.get_barrier_semaphore()
    friends = [at.along("x", 1), at.along("x", 2), at.along("x", 3), at.along("y", 1),
               at.along("y", 3), at.along("z", 1), at.along("z", 3), at.sibling()]
    for friend in friends:
        pl.semaphore_signal(barrier, inc=1, device_id=friend, device_id_type=MESH)

    send = Sender(send_sem, recv_sem)
    far, up, down = (at.x + 2) % 4, (at.x + 1) % 4, (at.x + 3) % 4
    scale = 1.0 / math.sqrt(HD)

    def added(dst, first, second):
        dst[...] = (first[...].astype(F32) + second[...].astype(F32)).astype(BF16)

    def both(dim, one, other):
        return send(*one, at.along(dim, 1)), send(*other, at.along(dim, 3))

    def attention(b, group):
        first, stop, _ = GROUPS[group]
        spans = [slice(low, low + HD) for low in range(first, stop, HD)]
        rows = pl.ds(pl.multiple_of(b * BLOCK, BLOCK), BLOCK)
        count = counts[b]
        valid = lax.broadcasted_iota(jnp.int32, (BLOCK, KEYS), 1) < count * RLEN
        empty = jnp.where(count == 0, 1.0, 0.0).astype(F32)
        for i, cols in enumerate(spans):
            score_s[i] = dot(qs[rows, cols], ks[b, :, cols], LAST) * scale
            dprob_s[i] = dot(dos[rows, cols], vs[b, :, cols], LAST)
        for i in range(len(spans)):
            scores = score_s[i]
            top = jnp.max(jnp.where(valid, scores, NEG_LARGE), axis=-1, keepdims=True)
            weights = jnp.where(valid, jnp.exp(scores - top), 0.0)
            probs = weights / (jnp.sum(weights, axis=-1, keepdims=True) + empty)
            weight_s[i] = probs.astype(BF16)
            d_probs = dprob_s[i]
            inner = jnp.sum(probs * d_probs, axis=-1, keepdims=True)
            dscore_s[i] = (probs * (d_probs - inner) * scale).astype(BF16)
        total = jnp.zeros((BLOCK, HD), F32)
        for i, cols in enumerate(spans):
            ctx[rows, cols] = dot(weight_s[i], vs[b, :, cols]).astype(BF16)
            dq = dot(dscore_s[i], ks[b, :, cols])
            dq2[rows, cols] = dq.astype(BF16)
            total = total + dq * qs[rows, cols].astype(F32)
            vs[b, :, cols] = dot(weight_s[i], dos[rows, cols], FIRST).astype(BF16)
            ks[b, :, cols] = dot(dscore_s[i], qs[rows, cols], FIRST).astype(BF16)
        sum_s[rows, :] = total if group == 0 else sum_s[rows, :] + total

    def encoded_grad(b):
        grad = dot(ks[b], wk[...], LAST) + dot(vs[b], wv[...], LAST)
        grads[b] = grad.astype(BF16)

    def share_dq(group):
        first, stop, _ = GROUPS[group]
        return send(dq2.at[0:256, first:stop], dq2.at[256:512, first:stop], at.sibling())

    def transposed(group, rows):
        first, stop, _ = GROUPS[group]
        for low in range(first, stop, 256):
            dq_t[low : low + 256, rows] = jnp.transpose(dq2[rows, low : low + 256])

    def product(group, dy, dz):
        k = at.chunk(dy, dz)
        first, stop, _ = GROUPS[group]
        prod[k, first:stop] = dot(dq_t[first:stop], nrm[k]).astype(BF16)

    dims = (("z", "y"), ("y", "z"))

    def block(group, half, line, off, part=None):
        dy, dz = (line, off) if half == 0 else (off, line)
        first, stop, z_first = GROUPS[group]
        low, high = ((first, first + z_first), (first + z_first, stop))[half]
        middle = (low + high) // 2
        low, high = (low, high) if part is None else ((low, middle), (middle, high))[part]
        return prod.at[at.chunk(dy, dz), low:high]

    c1, c2, d1, d2 = {}, {}, {}, {}

    def first_hop(group, half, line):
        slot = ra1[group][half].at[LINES.index(line)]
        c1[group, half, line] = both(
            dims[half][0],
            (block(group, half, line, 2, 0), slot.at[0]),
            (block(group, half, line, 2, 1), slot.at[1]),
        )

    def second_hop(group, half, line):
        for way, off in ((0, 1), (1, 3)):
            c1[group, half, line][way].wait_recv()
            piece = block(group, half, line, off, way)
            added(piece, piece, ra1[group][half].at[LINES.index(line), way])
        slot = ra2[group][half].at[LINES.index(line)]
        c2[group, half, line] = both(
            dims[half][0],
            (block(group, half, line, 1), slot.at[0]),
            (block(group, half, line, 3), slot.at[1]),
        )

    def gathered(group, half, line):
        for way in (0, 1):
            c2[group, half, line][way].wait_recv()
        slot = ra2[group][half].at[LINES.index(line)]
        piece = block(group, half, line, 0)
        total = piece[...].astype(F32) + slot[0].astype(F32) + slot[1].astype(F32)
        piece[...] = total.astype(BF16)

    def turn(group, half):
        d1[group, half] = both(
            dims[half][1],
            (block(group, half, 2, 0, 0), rb1[group][half].at[0]),
            (block(group, half, 2, 0, 1), rb1[group][half].at[1]),
        )

    def turned(group, half):
        for way, off in ((0, 1), (1, 3)):
            d1[group, half][way].wait_recv()
            piece = block(group, half, off, 0, way)
            added(piece, piece, rb1[group][half].at[way])
        d2[group, half] = both(
            dims[half][1],
            (block(group, half, 1, 0), rb2[group][half].at[0]),
            (block(group, half, 3, 0), rb2[group][half].at[1]),
        )

    def result(group):
        first, stop, _ = GROUPS[group]
        sizes = halves(group)
        for half in (0, 1):
            for way in (0, 1):
                c2[group, half, 0][way].wait_recv()
                d2[group, half][way].wait_recv()
            own = block(group, half, 0, 0)
            slot = ra2[group][half].at[LINES.index(0)]
            total = own[...].astype(F32) + slot[0].astype(F32) + slot[1].astype(F32)
            low = half * sizes[0]
            dw_t[low : low + sizes[half]] = (
                total + rb2[group][half][0].astype(F32) + rb2[group][half][1].astype(F32)
            )
        for low in range(0, stop - first, 128):
            dw_ref[:, first + low : first + low + 128] = jnp.transpose(dw_t[low : low + 128])

    def partial(k):
        part[k] = dot(dq2[...], wc[k], LAST).astype(BF16)

    n1, n2 = [], []

    def far_partial(m):
        partial(far * 4 + m)
        n1.append(
            both("x", (part.at[far * 4 + m, 0:256], rn1.at[m, 0]),
                 (part.at[far * 4 + m, 256:512], rn1.at[m, 1]))
        )

    def near_partial(m):
        n1[m][0].wait_recv()
        piece = part.at[up * 4 + m, 0:256]
        added(piece, piece, rn1.at[m, 0])
        n1[m][1].wait_recv()
        piece = part.at[down * 4 + m, 256:512]
        added(piece, piece, rn1.at[m, 1])
        n2.append(
            both("x", (part.at[up * 4 + m], rn2.at[m, 0]), (part.at[down * 4 + m], rn2.at[m, 1]))
        )

    outs = []

    def write(src, dst):
        copy = pltpu.make_async_copy(src, dst, out_sem.at[len(outs)])
        copy.start()
        outs.append(copy)

    def finish(i, d_normed):
        inverse = wide(inverse_ref[...])
        unit = tok[i].astype(F32) * inverse
        parts = d_normed * gain_ref[at.x * 8 + i]
        result = inverse * (parts - unit * (wide(column[...]) * (1.0 / width)))
        tok[i] = result.astype(BF16)
        first = pl.multiple_of(i * 256, 256)
        write(tok.at[i], dh_ref.at[:, pl.ds(first, 256)])

    c_sib = []

    def normed_sum(m):
        for copy in n2[m]:
            copy.wait_recv()

        def summed(low):
            rows = slice(low, low + 256)
            total = part[at.x * 4 + m, rows].astype(F32) + rn2[m, 0, rows].astype(F32)
            return total + rn2[m, 1, rows].astype(F32)

        out_sib[m] = summed(256).astype(BF16)
        c_sib.append(send(out_sib.at[m], in_sib.at[m], at.sibling()))
        finish(2 * m + at.core, summed(0))

    def sibling_part(m):
        c_sib[m].wait_recv()
        finish(2 * m + 1 - at.core, in_sib[m].astype(F32))

    for load in loads[:4]:
        load.wait()
    for load in loads[4:]:
        load.start()

    @pl.loop(0, 4)
    def _(b):
        attention(b, 0)

    pl.semaphore_wait(barrier, len(friends))
    c_dq = [share_dq(0)]
    own, other = slice(0, 256), slice(256, 512)
    transposed(0, own)
    for load in loads[4:8]:
        load.wait()
    attention(far, 1)
    encoded_grad(far)
    c_g1 = both("x", (grads.at[far, 0:128], g1.at[0]), (grads.at[far, 128:256], g1.at[1]))
    c_dq[0].wait_recv()
    transposed(0, other)
    product(0, 2, 2)
    first_hop(0, 1, 2)
    first_hop(0, 0, 2)
    for line in (1, 3, 0):
        product(0, 2, line)
        first_hop(0, 1, line)
        product(0, line, 2)
        first_hop(0, 0, line)
    attention(up, 1)
    second_hop(0, 1, 2)
    second_hop(0, 0, 2)
    corners = ((1, 1), (3, 1), (1, 3), (3, 3))
    rest = ((1, 0), (3, 0), (0, 1), (0, 3), (0, 0))
    for dy, dz in corners:
        product(0, dy, dz)
    for line in (1, 3):
        second_hop(0, 1, line)
        second_hop(0, 0, line)
    attention(down, 1)
    encoded_grad(up)
    encoded_grad(down)
    c_g1[0].wait_recv()
    c_g1[1].wait_recv()
    gs[0, 0:128] = (grads[up, 0:128].astype(F32) + g1[0].astype(F32)).astype(BF16)
    gs[0, 128:256] = grads[up, 128:256]
    gs[1, 0:128] = grads[down, 0:128]
    gs[1, 128:256] = (grads[down, 128:256].astype(F32) + g1[1].astype(F32)).astype(BF16)
    c_g2 = both("x", (gs.at[0], g2.at[0]), (gs.at[1], g2.at[1]))
    attention(at.x, 1)
    c_dq.append(share_dq(1))
    write(ctx, ctx_ref)
    for half in (0, 1):
        gathered(0, half, 2)
        turn(0, half)
    lanes = jnp.sum(jnp.transpose(sum_s[...]), axis=0, keepdims=True)
    sums[...] = jnp.broadcast_to(lanes, (8, 256))
    c_sums = [send(sums, sums_in.at[i], at.along("x", i + 1)) for i in range(3)]
    transposed(1, own)
    c_dq[1].wait_recv()
    transposed(1, other)
    product(1, 2, 2)
    first_hop(1, 1, 2)
    first_hop(1, 0, 2)
    for line in (1, 3, 0):
        product(1, 2, line)
        first_hop(1, 1, line)
        product(1, line, 2)
        first_hop(1, 0, line)
    for dy, dz in rest:
        product(0, dy, dz)
    for half in (0, 1):
        gathered(0, half, 1)
        gathered(0, half, 3)
        turned(0, half)
    second_hop(1, 0, 2)
    for m in range(4):
        far_partial(m)
    second_hop(1, 1, 2)
    for dy, dz in corners:
        product(1, dy, dz)
    for line in (1, 3):
        second_hop(1, 0, line)
        second_hop(1, 1, line)
    for m in range(4):
        partial(up * 4 + m)
        partial(down * 4 + m)
        near_partial(m)
    for dy, dz in rest:
        product(1, dy, dz)
    second_hop(0, 0, 0)
    second_hop(1, 0, 0)
    gathered(1, 0, 2)
    turn(1, 0)
    encoded_grad(at.x)
    for copy in c_g2:
        copy.wait_recv()
    gfin[...] = (grads[at.x].astype(F32) + g2[0].astype(F32) + g2[1].astype(F32)).astype(BF16)
    gathered(1, 1, 2)
    turn(1, 1)
    c_swap = send(gfin, gin, at.partner())
    second_hop(0, 1, 0)
    gathered(1, 0, 1)
    gathered(1, 0, 3)
    turned(1, 0)
    second_hop(1, 1, 0)

    for copy in c_sums:
        copy.wait_recv()
    whole = sums[...] + sums_in[0] + sums_in[1] + sums_in[2]
    dots_ref[...] = whole[0:1] * (1.0 / math.sqrt(width))
    column[...] = jnp.transpose(jnp.broadcast_to(whole[0:1], (128, 256)))
    for load in loads[8:]:
        load.wait()
    for m in range(4):
        partial(at.x * 4 + m)
    normed_sum(0)
    normed_sum(1)
    sibling_part(0)
    gathered(1, 1, 1)
    gathered(1, 1, 3)
    turned(1, 1)
    normed_sum(2)
    sibling_part(1)
    result(0)
    normed_sum(3)
    sibling_part(2)
    sibling_part(3)
    result(1)
    c_swap.wait_recv()
    write(gin, de_ref)
    for copy in send.copies:
        copy.wait_send()
    for copy in outs:
        copy.wait()


BACKWARD_SENDS = 2 + 2 + 2 + 8 + 8 + 3 + 1 + 4 + 2 * 40


def backward(
    counts, queries, keys, values, d_context, w_key, w_value, normed, w_all, tokens, inverse, gain
):
    rows, width = queries.shape
    full = tokens.shape[1]
    vmem = pl.BlockSpec(memory_space=pltpu.VMEM)
    anywhere = pl.BlockSpec(memory_space=pl.ANY)

    def buffer(*shape, kind=BF16):
        return pltpu.VMEM(shape, kind)

    sizes = [size for group in range(2) for size in halves(group)]
    return pl.pallas_call(
        backward_kernel,
        in_specs=[pl.BlockSpec(memory_space=pltpu.SMEM)] + [anywhere] * 9 + [vmem, vmem],
        out_specs=[anywhere, vmem, anywhere, anywhere, vmem],
        out_shape=[
            jax.ShapeDtypeStruct((rows, width), BF16),
            jax.ShapeDtypeStruct((256, width), F32),
            jax.ShapeDtypeStruct((rows, full // 4), BF16),
            jax.ShapeDtypeStruct((KEYS, E), BF16),
            jax.ShapeDtypeStruct((1, rows), F32),
        ],
        scratch_shapes=[
            buffer(rows, width),
            buffer(rows, width),
            buffer(4, KEYS, width),
            buffer(4, KEYS, width),
            buffer(E, width),
            buffer(E, width),
            buffer(rows, width),
            buffer(6, BLOCK, KEYS, kind=F32),
            buffer(6, BLOCK, KEYS, kind=F32),
            buffer(6, BLOCK, KEYS),
            buffer(6, BLOCK, KEYS),
            buffer(rows, HD, kind=F32),
            buffer(512, 1024),
            buffer(1024, 512),
            buffer(16, 512, 256),
            buffer(16, 256, 1024),
            buffer(16, 1024, 256),
            buffer(768, 256, kind=F32),
            buffer(16, 512, 256),
            buffer(4, 2, 256, 256),
            buffer(4, 2, 512, 256),
            buffer(4, 256, 256),
            buffer(4, 256, 256),
            buffer(4, KEYS, E),
            buffer(2, 128, E),
            buffer(2, 256, E),
            buffer(2, 256, E),
            buffer(256, E),
            buffer(256, E),
            buffer(8, 256, kind=F32),
            buffer(3, 8, 256, kind=F32),
            buffer(8, 256, 256),
            buffer(256, 128, kind=F32),
        ]
        + [buffer(4, 2, size // 2, 256) for size in sizes]
        + [buffer(4, 2, size, 256) for size in sizes]
        + [buffer(2, size // 2, 256) for size in sizes]
        + [buffer(2, size, 256) for size in sizes]
        + [
            pltpu.SemaphoreType.DMA((LOADS,)),
            pltpu.SemaphoreType.DMA((10,)),
            pltpu.SemaphoreType.DMA((BACKWARD_SENDS,)),
            pltpu.SemaphoreType.DMA((BACKWARD_SENDS,)),
        ],
        compiler_params=pltpu.CompilerParams(
            collective_id=1, has_side_effects=True, vmem_limit_bytes=62 * 2**20
        ),
        cost_estimate=pl.CostEstimate(
            flops=12 * 2**30, bytes_accessed=30 * 2**20, transcendentals=0
        ),
    )(counts, queries, keys, values, d_context, w_key, w_value, normed, w_all, tokens, inverse, gain)


def results_kernel(*refs):
    count = (len(refs) - 1) // 2
    sem = refs[-1]
    copies = []
    for source, target in zip(refs[:count], refs[count : 2 * count]):
        pieces = min(4, source.shape[0])
        rows = source.shape[0] // pieces
        for i in range(pieces):
            piece = pl.ds(i * rows, rows)
            copies.append(
                pltpu.make_async_copy(source.at[piece], target.at[piece], sem.at[len(copies)])
            )
    for copy in copies:
        copy.start()
    for copy in copies:
        copy.wait()


def results(*arrays):
    anywhere = pl.BlockSpec(memory_space=pl.ANY)
    return pl.pallas_call(
        results_kernel,
        in_specs=[anywhere] * len(arrays),
        out_specs=[anywhere] * len(arrays),
        out_shape=[jax.ShapeDtypeStruct(array.shape, array.dtype) for array in arrays],
        scratch_shapes=[pltpu.SemaphoreType.DMA((4 * len(arrays),))],
        compiler_params=pltpu.CompilerParams(vmem_limit_bytes=62 * 2**20),
    )(*arrays)


def shards(
    tokens,
    w_query,
    query_gain,
    state_kv,
    neighbours,
    enc_gain,
    enc_query,
    enc_out,
    w_key,
    w_value,
    counts,
    d_context,
):
    gain = query_gain.reshape(32, 1, 256)
    queries, w_part, normed, keys, values, inverse = forward(
        tokens, w_query, gain, state_kv, neighbours.reshape(KEYS, E), enc_gain,
        enc_query, enc_out, w_key, w_value,
    )
    context, d_query_weight, d_hidden, d_encoded, row_dots = backward(
        counts, queries, keys, values, d_context, w_key, w_value, normed, w_part, tokens, inverse,
        gain,
    )
    context, d_query_weight, d_hidden, d_encoded, row_dots = results(
        context, d_query_weight, d_hidden, d_encoded, row_dots
    )
    return (
        context,
        d_hidden,
        d_query_weight,
        d_encoded.reshape(1, 1, NBR, RLEN, E),
        row_dots[0],
    )


def solution(mesh):
    return jax.shard_map(
        shards,
        mesh=mesh,
        in_specs=(
            P(("section", "seq"), None),
            P(("section", "seq"), "tensor"),
            P(),
            P("tensor", None),
            P("section", ("seq", "tensor"), None, None, None),
            P(),
            P(),
            P(),
            P(None, "tensor"),
            P(None, "tensor"),
            P(("section", "seq")),
            P(("section", "seq"), "tensor"),
        ),
        out_specs=(
            P(("section", "seq"), "tensor"),
            P(("section", "seq"), "tensor"),
            P(("section", "seq"), "tensor"),
            P("section", ("seq", "tensor"), None, None, None),
            P(("section", "seq")),
        ),
        check_vma=False,
    )
```

```python
import functools
import math

import jax
import jax.numpy as jnp
from jax import lax
from jax.experimental import pallas as pl
from jax.experimental.pallas import tpu as pltpu
from jax.sharding import PartitionSpec as P

HD = 128
E = 896
EHD = 64
BLOCK = 64
NBR = 2
RLEN = 128
KEYS = NBR * RLEN

EPSILON = 1e-05
NEG_LARGE = -1e30
MESH = pl.DeviceIdType.MESH
F32 = jnp.float32
BF16 = jnp.bfloat16
LAST = (((1,), (1,)), ((), ()))
FIRST = (((0,), (0,)), ((), ()))


def dot(a, b, dims=(((1,), (0,)), ((), ()))):
    return lax.dot_general(a, b, dims, preferred_element_type=F32)


class Place:
    def __init__(self):
        self.section = lax.axis_index("section")
        seq = lax.axis_index("seq")
        self.x = lax.axis_index("tensor")
        self.core = seq % 2
        self.y = seq // 4
        self.z = 2 * ((seq // 2) % 2) + self.section

    def along(self, dim, off):
        if dim == "x":
            return (self.section, self.seq_of(self.y, self.z), (self.x + off) % 4)
        if dim == "y":
            return (self.section, self.seq_of((self.y + off) % 4, self.z), self.x)
        z = (self.z + off) % 4
        return (z % 2, self.seq_of(self.y, z), self.x)

    def seq_of(self, y, z):
        return y * 4 + (z // 2) * 2 + self.core

    def sibling(self):
        return (self.section, self.y * 4 + (self.z // 2) * 2 + 1 - self.core, self.x)

    def partner(self):
        return (1 - self.section, self.seq_of(self.y, self.z), self.x)

    def chunk(self, dy, dz):
        y, z = (self.y + dy) % 4, (self.z + dz) % 4
        return (z % 2) * 8 + y * 2 + z // 2


def greet(devices):
    barrier = pltpu.get_barrier_semaphore()
    for device in devices:
        pl.semaphore_signal(barrier, inc=1, device_id=device, device_id_type=MESH)
    pl.semaphore_wait(barrier, len(devices))


class Sender:
    def __init__(self, send_sem, recv_sem):
        self.send_sem, self.recv_sem, self.copies = send_sem, recv_sem, []

    def __call__(self, src, dst, device):
        index = len(self.copies)
        copy = pltpu.make_async_remote_copy(
            src_ref=src, dst_ref=dst, send_sem=self.send_sem.at[index],
            recv_sem=self.recv_sem.at[index], device_id=device, device_id_type=MESH,
        )
        copy.start()
        self.copies.append(copy)
        return copy


Y_FIRST = 96
CHUNK = 256


def wide(column):
    return jnp.concatenate([column, column], axis=1)


def forward_kernel(
    tokens_ref, w_ref, gain_ref, state_ref, near_ref, egain_ref, equery_ref, eout_ref, wk_ref, wv_ref,
    q_ref, w_out, nrm_out, k_out, v_out, inv_ref,
    tok, wc, nrm, theirs, skv, unit, acc, q_send, q_in,
    sp, sr1, sr2, enc_in, eq_s, ectx, escore, equery, eout, enc, wk, wv, ks, vs,
    load_sem, out_sem, send_sem, recv_sem,
):
    at = Place()
    share = tok.shape[1] // 4
    send = Sender(send_sem, recv_sem)
    me = at.chunk(0, 0)
    pairs = (
        (w_ref, wc.at[me]), (tokens_ref, tok), (state_ref, skv), (equery_ref, equery),
        (eout_ref, eout), (wk_ref, wk), (wv_ref, wv),
    )
    loads = [pltpu.make_async_copy(src, dst, load_sem.at[i]) for i, (src, dst) in enumerate(pairs)]
    for load in loads:
        load.start()
    greet(
        [at.along("x", 1), at.along("x", 3), at.along("y", 1), at.along("y", 3),
         at.along("z", 1), at.along("z", 3), at.sibling()]
    )

    dims = (("y", "z"), ("z", "y"))
    spans = ((0, Y_FIRST), (Y_FIRST, CHUNK))

    def piece(half, first, second, part=None):
        dy, dz = (first, second) if half == 0 else (second, first)
        low, high = spans[half]
        middle = (low + high) // 2
        low, high = (low, high) if part is None else ((low, middle), (middle, high))[part]
        return wc.at[at.chunk(dy, dz), low:high]

    def pass_on(ref, dim, off):
        return send(ref, ref, at.along(dim, off))

    near, relay, cross, last = {}, {}, {}, {}

    def across(half, line):
        dim = dims[half][1]
        block = piece(half, line, 0)
        cross[half, line] = (pass_on(block, dim, 1), pass_on(block, dim, 3))

    def relays(half):
        dim = dims[half][0]
        near[half][0].wait_recv()
        first = pass_on(piece(half, 3, 0, 0), dim, 1)
        near[half][1].wait_recv()
        relay[half] = (first, pass_on(piece(half, 1, 0, 1), dim, 3))

    def relayed(half):
        relay[half][0].wait_recv()
        relay[half][1].wait_recv()
        across(half, 2)

    def crossed(half, line):
        dim = dims[half][1]
        cross[half, line][0].wait_recv()
        first = pass_on(piece(half, line, 3, 0), dim, 1)
        cross[half, line][1].wait_recv()
        last[half, line] = (first, pass_on(piece(half, line, 1, 1), dim, 3))

    def landed(half, line):
        last[half, line][0].wait_recv()
        last[half, line][1].wait_recv()

    outs = []

    def write(src, dst):
        copy = pltpu.make_async_copy(src, dst, out_sem.at[len(outs)])
        copy.start()
        outs.append(copy)

    def accumulate(offsets, begin=False):
        chunks = [at.chunk(dy, dz) for dy, dz in offsets]
        for k in chunks:
            write(wc.at[k], w_out.at[k])

        @pl.loop(0, 4)
        def _(i):
            rows = pl.ds(pl.multiple_of((i // 2) * 256, 256), 256)
            cols = pl.ds(pl.multiple_of((i % 2) * 512, 512), 512)
            total = dot(nrm[chunks[0], rows, :], wc[chunks[0], :, cols])
            for k in chunks[1:]:
                total = total + dot(nrm[k, rows, :], wc[k, :, cols])
            acc[rows, cols] = total if begin else acc[rows, cols] + total

    loads[0].wait()
    for half in (0, 1):
        block = piece(half, 0, 0)
        near[half] = (pass_on(block, dims[half][0], 1), pass_on(block, dims[half][0], 3))
    c_near = send(near_ref, enc_in, at.partner())
    across(1, 0)

    loads[1].wait()

    @pl.loop(0, 16)
    def _(i):
        rows = pl.ds(pl.multiple_of(i * 16, 16), 16)
        values = tok[rows, :].astype(F32)
        square = jnp.sum(values * values, axis=-1, keepdims=True)
        inverse = lax.rsqrt(square * (1.0 / tok.shape[1]) + EPSILON)
        inv_ref[rows, :] = jnp.broadcast_to(inverse, (16, 128))

    @pl.loop(0, 8)
    def _(i):
        source = pl.ds(pl.multiple_of(at.x * share + i * 256, 256), 256)
        target = pl.ds(pl.multiple_of(i * 256, 256), 256)
        unit[:, target] = (tok[:, source].astype(F32) * wide(inv_ref[...])).astype(BF16)

    loads[2].wait()

    @pl.loop(0, 7)
    def _(i):
        cols = pl.ds(pl.multiple_of(i * 256, 256), 256)
        part = dot(unit[...], skv[:, cols]).astype(BF16)
        for j in range(4):
            sp[j, :, cols] = part[64 * j : 64 * j + 64]

    far, up, down = (at.x + 2) % 4, (at.x + 1) % 4, (at.x + 3) % 4
    c_s1 = (
        send(sp.at[far, 0:32], sr1.at[0], at.along("x", 1)),
        send(sp.at[far, 32:64], sr1.at[1], at.along("x", 3)),
    )
    relays(0)
    relays(1)
    across(1, 3)
    across(1, 1)
    for line in (0, 3, 1):
        across(0, line)

    @pl.loop(0, 16)
    def _(k):
        def chunk(g):
            cols = pl.ds(pl.multiple_of(g * CHUNK, CHUNK), CHUNK)
            return (tok[:, cols].astype(F32) * wide(inv_ref[...]) * gain_ref[g]).astype(BF16)

        nrm[k, 0:256] = chunk(2 * k + at.core)
        theirs[k] = chunk(2 * k + 1 - at.core)

    c_nrm = send(theirs, nrm.at[:, 256:512], at.sibling())

    for way, block in ((0, up), (1, down)):
        c_s1[way].wait_recv()
        rows = slice(32 * way, 32 * way + 32)
        sp[block, rows] = (sp[block, rows].astype(F32) + sr1[way].astype(F32)).astype(BF16)
    c_s2 = (
        send(sp.at[up], sr2.at[0], at.along("x", 1)),
        send(sp.at[down], sr2.at[1], at.along("x", 3)),
    )
    relayed(0)
    crossed(1, 0)

    loads[3].wait()
    c_near.wait_recv()
    enc_rows = enc_in[...].astype(F32)
    mean = jnp.sum(enc_rows * enc_rows, axis=-1, keepdims=True) * (1.0 / E)
    enc_normed = (enc_rows * lax.rsqrt(mean + EPSILON) * egain_ref[...].reshape(1, E)).astype(BF16)
    eq_s[...] = dot(enc_normed, equery[...]).astype(BF16)

    c_s2[0].wait_recv()
    c_s2[1].wait_recv()
    states = (sp[at.x].astype(F32) + sr2[0].astype(F32) + sr2[1].astype(F32)).astype(BF16)
    states = states.astype(F32)
    left = lax.broadcasted_iota(jnp.int32, (BLOCK, 128), 1) < EHD
    left_wide = lax.broadcasted_iota(jnp.int32, (KEYS, 128), 1) < EHD

    def doubled(cols):
        both = states[:, cols]
        return jnp.concatenate(
            [jnp.where(left, both, 0.0), jnp.where(left, 0.0, both)], axis=0
        ).astype(BF16)

    for j in range(7):
        keys = doubled(slice(128 * j, 128 * j + 128))
        escore[j] = dot(eq_s[:, 128 * j : 128 * j + 128], keys, LAST) * (1.0 / math.sqrt(EHD))
    for j in range(7):
        scores = escore[j]
        top_left = jnp.max(jnp.where(left_wide, scores, NEG_LARGE), axis=-1, keepdims=True)
        top_right = jnp.max(jnp.where(left_wide, NEG_LARGE, scores), axis=-1, keepdims=True)
        weights = jnp.exp(scores - jnp.where(left_wide, top_left, top_right))
        sum_left = jnp.sum(jnp.where(left_wide, weights, 0.0), axis=-1, keepdims=True)
        sum_right = jnp.sum(jnp.where(left_wide, 0.0, weights), axis=-1, keepdims=True)
        escore[j] = weights / jnp.where(left_wide, sum_left, sum_right)
    for j in range(7):
        values = doubled(slice(E + 128 * j, E + 128 * j + 128))
        ectx[:, 128 * j : 128 * j + 128] = dot(escore[j].astype(BF16), values).astype(BF16)
    loads[4].wait()
    enc[at.x] = (enc_in[...].astype(F32) + dot(ectx[...], eout[...])).astype(BF16)
    c_e1 = (
        send(enc.at[at.x], enc.at[at.x], at.along("x", 1)),
        send(enc.at[at.x], enc.at[at.x], at.along("x", 3)),
    )
    relayed(1)
    loads[5].wait()
    loads[6].wait()

    def project(block):
        @pl.loop(0, 4)
        def _(i):
            cols = pl.ds(pl.multiple_of(i * 256, 256), 256)
            ks[block, :, cols] = dot(enc[block], wk[:, cols]).astype(BF16)
            vs[block, :, cols] = dot(enc[block], wv[:, cols]).astype(BF16)

        write(ks.at[block], k_out.at[block])
        write(vs.at[block], v_out.at[block])

    c_nrm.wait_recv()
    write(nrm, nrm_out)
    crossed(0, 0)
    accumulate([(0, 0), (1, 0), (3, 0), (0, 1), (0, 3)], begin=True)
    crossed(1, 3)
    crossed(1, 1)
    project(at.x)
    crossed(0, 3)
    crossed(0, 1)
    c_e1[0].wait_recv()
    c_e2 = [send(enc.at[down, 0:128], enc.at[down, 0:128], at.along("x", 1))]
    c_e1[1].wait_recv()
    c_e2.append(send(enc.at[up, 128:256], enc.at[up, 128:256], at.along("x", 3)))
    project(down)
    project(up)
    accumulate([(1, 1), (1, 3), (3, 1), (3, 3)])
    crossed(1, 2)
    crossed(0, 2)
    landed(0, 0)
    landed(1, 0)
    accumulate([(2, 0), (0, 2)])
    c_e2[0].wait_recv()
    c_e2[1].wait_recv()
    project(far)
    for line in (3, 1):
        landed(0, line)
        landed(1, line)
    accumulate([(2, 1), (2, 3), (1, 2), (3, 2)])
    landed(0, 2)
    landed(1, 2)
    accumulate([(2, 2)])
    q_send[...] = acc[256:512].astype(BF16)
    c_q = send(q_send, q_in, at.sibling())
    c_q.wait_recv()
    q_ref[...] = (acc[0:256] + q_in[...].astype(F32)).astype(BF16)
    for copy in send.copies:
        copy.wait_send()
    for copy in outs:
        copy.wait()


FORWARD_SENDS = 4 + 1 + 4 + 2 * 6 + 2 * 2 + 16 + 2 + 2 + 1 + 2 + 2 + 1


def forward(tokens, w_query, gain, state_kv, near, enc_gain, enc_query, enc_out, w_key, w_value):
    rows, full = tokens.shape
    width = w_query.shape[1]
    vmem = pl.BlockSpec(memory_space=pltpu.VMEM)
    anywhere = pl.BlockSpec(memory_space=pl.ANY)

    def buffer(*shape, kind=BF16):
        return pltpu.VMEM(shape, kind)

    return pl.pallas_call(
        forward_kernel,
        in_specs=[anywhere, anywhere, vmem, anywhere, anywhere, vmem] + [anywhere] * 4,
        out_specs=[vmem] + [anywhere] * 4 + [vmem],
        out_shape=[
            jax.ShapeDtypeStruct((rows, width), BF16),
            jax.ShapeDtypeStruct((16, CHUNK, width), BF16),
            jax.ShapeDtypeStruct((16, 2 * rows, CHUNK), BF16),
            jax.ShapeDtypeStruct((4, KEYS, width), BF16),
            jax.ShapeDtypeStruct((4, KEYS, width), BF16),
            jax.ShapeDtypeStruct((rows, 128), F32),
        ],
        scratch_shapes=[
            buffer(rows, full),
            buffer(16, CHUNK, width),
            buffer(16, 2 * rows, CHUNK),
            buffer(16, rows, CHUNK),
            buffer(full // 4, 2 * E),
            buffer(rows, full // 4),
            buffer(2 * rows, width, kind=F32),
            buffer(rows, width),
            buffer(rows, width),
            buffer(4, BLOCK, 2 * E),
            buffer(2, BLOCK // 2, 2 * E),
            buffer(2, BLOCK, 2 * E),
            buffer(KEYS, E),
            buffer(KEYS, E),
            buffer(KEYS, E),
            buffer(7, KEYS, 128, kind=F32),
            buffer(E, E),
            buffer(E, E),
            buffer(4, KEYS, E),
            buffer(E, width),
            buffer(E, width),
            buffer(4, KEYS, width),
            buffer(4, KEYS, width),
            pltpu.SemaphoreType.DMA((7,)),
            pltpu.SemaphoreType.DMA((25,)),
            pltpu.SemaphoreType.DMA((FORWARD_SENDS,)),
            pltpu.SemaphoreType.DMA((FORWARD_SENDS,)),
        ],
        compiler_params=pltpu.CompilerParams(
            collective_id=2, has_side_effects=True, vmem_limit_bytes=60 * 2**20
        ),
        cost_estimate=pl.CostEstimate(
            flops=2 * 5400 * 2**20, bytes_accessed=40 * 2**20, transcendentals=0
        ),
    )(tokens, w_query, gain, state_kv, near, enc_gain, enc_query, enc_out, w_key, w_value)


LINES = (2, 1, 3, 0)
GROUPS = ((0, 384, 160), (384, 1024, 224))
LOADS = 16


def halves(group):
    first, stop, z_first = GROUPS[group]
    return z_first, stop - first - z_first


def backward_kernel(
    counts, q_ref, k_ref, v_ref, do_ref, wk_ref, wv_ref, nrm_ref, w_ref, tokens_ref,
    inverse_ref, gain_ref,
    ctx_ref, dw_ref, dh_ref, de_ref, dots_ref,
    qs, dos, ks, vs, wk, wv, ctx, score_s, dprob_s, weight_s, dscore_s, sum_s,
    dq2, dq_t, nrm, wc, prod, dw_t, part, rn1, rn2, out_sib, in_sib,
    grads, g1, gs, g2, gfin, gin, sums, sums_in, tok, column,
    ra1_00, ra1_01, ra1_10, ra1_11, ra2_00, ra2_01, ra2_10, ra2_11,
    rb1_00, rb1_01, rb1_10, rb1_11, rb2_00, rb2_01, rb2_10, rb2_11,
    load_sem, out_sem, send_sem, recv_sem,
):
    at = Place()
    width = tokens_ref.shape[1]
    share = width // 4
    ra1 = ((ra1_00, ra1_01), (ra1_10, ra1_11))
    ra2 = ((ra2_00, ra2_01), (ra2_10, ra2_11))
    rb1 = ((rb1_00, rb1_01), (rb1_10, rb1_11))
    rb2 = ((rb2_00, rb2_01), (rb2_10, rb2_11))
    pairs = [
        (q_ref, qs), (do_ref, dos), (k_ref, ks), (v_ref, vs), (wk_ref, wk), (wv_ref, wv),
        (nrm_ref, nrm), (w_ref, wc),
    ]
    for i in range(8):
        first = pl.multiple_of(at.x * share + i * 256, 256)
        pairs.append((tokens_ref.at[:, pl.ds(first, 256)], tok.at[i]))
    loads = [pltpu.make_async_copy(src, dst, load_sem.at[i]) for i, (src, dst) in enumerate(pairs)]
    for load in loads[:4]:
        load.start()
    barrier = pltpu.get_barrier_semaphore()
    friends = [at.along("x", 1), at.along("x", 2), at.along("x", 3), at.along("y", 1),
               at.along("y", 3), at.along("z", 1), at.along("z", 3), at.sibling()]
    for friend in friends:
        pl.semaphore_signal(barrier, inc=1, device_id=friend, device_id_type=MESH)

    send = Sender(send_sem, recv_sem)
    far, up, down = (at.x + 2) % 4, (at.x + 1) % 4, (at.x + 3) % 4
    scale = 1.0 / math.sqrt(HD)

    def added(dst, first, second):
        dst[...] = (first[...].astype(F32) + second[...].astype(F32)).astype(BF16)

    def both(dim, one, other):
        return send(*one, at.along(dim, 1)), send(*other, at.along(dim, 3))

    def attention(b, group):
        first, stop, _ = GROUPS[group]
        spans = [slice(low, low + HD) for low in range(first, stop, HD)]
        rows = pl.ds(pl.multiple_of(b * BLOCK, BLOCK), BLOCK)
        count = counts[b]
        valid = lax.broadcasted_iota(jnp.int32, (BLOCK, KEYS), 1) < count * RLEN
        empty = jnp.where(count == 0, 1.0, 0.0).astype(F32)
        for i, cols in enumerate(spans):
            score_s[i] = dot(qs[rows, cols], ks[b, :, cols], LAST) * scale
            dprob_s[i] = dot(dos[rows, cols], vs[b, :, cols], LAST)
        for i in range(len(spans)):
            scores = score_s[i]
            top = jnp.max(jnp.where(valid, scores, NEG_LARGE), axis=-1, keepdims=True)
            weights = jnp.where(valid, jnp.exp(scores - top), 0.0)
            probs = weights / (jnp.sum(weights, axis=-1, keepdims=True) + empty)
            weight_s[i] = probs.astype(BF16)
            d_probs = dprob_s[i]
            inner = jnp.sum(probs * d_probs, axis=-1, keepdims=True)
            dscore_s[i] = (probs * (d_probs - inner) * scale).astype(BF16)
        total = jnp.zeros((BLOCK, HD), F32)
        for i, cols in enumerate(spans):
            ctx[rows, cols] = dot(weight_s[i], vs[b, :, cols]).astype(BF16)
            dq = dot(dscore_s[i], ks[b, :, cols])
            dq2[rows, cols] = dq.astype(BF16)
            total = total + dq * qs[rows, cols].astype(F32)
            vs[b, :, cols] = dot(weight_s[i], dos[rows, cols], FIRST).astype(BF16)
            ks[b, :, cols] = dot(dscore_s[i], qs[rows, cols], FIRST).astype(BF16)
        sum_s[rows, :] = total if group == 0 else sum_s[rows, :] + total

    def encoded_grad(b):
        grad = dot(ks[b], wk[...], LAST) + dot(vs[b], wv[...], LAST)
        grads[b] = grad.astype(BF16)

    def share_dq(group):
        first, stop, _ = GROUPS[group]
        return send(dq2.at[0:256, first:stop], dq2.at[256:512, first:stop], at.sibling())

    def transposed(group, rows):
        first, stop, _ = GROUPS[group]
        for low in range(first, stop, 128):
            dq_t[low : low + 128, rows] = jnp.transpose(dq2[rows, low : low + 128])

    def product(group, dy, dz):
        k = at.chunk(dy, dz)
        first, stop, _ = GROUPS[group]
        prod[k, first:stop] = dot(dq_t[first:stop], nrm[k]).astype(BF16)

    dims = (("z", "y"), ("y", "z"))

    def block(group, half, line, off, part=None):
        dy, dz = (line, off) if half == 0 else (off, line)
        first, stop, z_first = GROUPS[group]
        low, high = ((first, first + z_first), (first + z_first, stop))[half]
        middle = (low + high) // 2
        low, high = (low, high) if part is None else ((low, middle), (middle, high))[part]
        return prod.at[at.chunk(dy, dz), low:high]

    c1, c2, d1, d2 = {}, {}, {}, {}

    def first_hop(group, half, line):
        slot = ra1[group][half].at[LINES.index(line)]
        c1[group, half, line] = both(
            dims[half][0],
            (block(group, half, line, 2, 0), slot.at[0]),
            (block(group, half, line, 2, 1), slot.at[1]),
        )

    def second_hop(group, half, line):
        for way, off in ((0, 1), (1, 3)):
            c1[group, half, line][way].wait_recv()
            piece = block(group, half, line, off, way)
            added(piece, piece, ra1[group][half].at[LINES.index(line), way])
        slot = ra2[group][half].at[LINES.index(line)]
        c2[group, half, line] = both(
            dims[half][0],
            (block(group, half, line, 1), slot.at[0]),
            (block(group, half, line, 3), slot.at[1]),
        )

    def gathered(group, half, line):
        for way in (0, 1):
            c2[group, half, line][way].wait_recv()
        slot = ra2[group][half].at[LINES.index(line)]
        piece = block(group, half, line, 0)
        total = piece[...].astype(F32) + slot[0].astype(F32) + slot[1].astype(F32)
        piece[...] = total.astype(BF16)

    def turn(group, half):
        d1[group, half] = both(
            dims[half][1],
            (block(group, half, 2, 0, 0), rb1[group][half].at[0]),
            (block(group, half, 2, 0, 1), rb1[group][half].at[1]),
        )

    def turned(group, half):
        for way, off in ((0, 1), (1, 3)):
            d1[group, half][way].wait_recv()
            piece = block(group, half, off, 0, way)
            added(piece, piece, rb1[group][half].at[way])
        d2[group, half] = both(
            dims[half][1],
            (block(group, half, 1, 0), rb2[group][half].at[0]),
            (block(group, half, 3, 0), rb2[group][half].at[1]),
        )

    def result(group):
        first, stop, _ = GROUPS[group]
        sizes = halves(group)
        for half in (0, 1):
            for way in (0, 1):
                c2[group, half, 0][way].wait_recv()
                d2[group, half][way].wait_recv()
            own = block(group, half, 0, 0)
            slot = ra2[group][half].at[LINES.index(0)]
            total = own[...].astype(F32) + slot[0].astype(F32) + slot[1].astype(F32)
            low = half * sizes[0]
            dw_t[low : low + sizes[half]] = (
                total + rb2[group][half][0].astype(F32) + rb2[group][half][1].astype(F32)
            )
        for low in range(0, stop - first, 128):
            dw_ref[:, first + low : first + low + 128] = jnp.transpose(dw_t[low : low + 128])

    def partial(k):
        part[k] = dot(dq2[...], wc[k], LAST).astype(BF16)

    n1, n2 = [], []

    def far_partial(m):
        partial(far * 4 + m)
        n1.append(
            both("x", (part.at[far * 4 + m, 0:256], rn1.at[m, 0]),
                 (part.at[far * 4 + m, 256:512], rn1.at[m, 1]))
        )

    def near_partial(m):
        n1[m][0].wait_recv()
        piece = part.at[up * 4 + m, 0:256]
        added(piece, piece, rn1.at[m, 0])
        n1[m][1].wait_recv()
        piece = part.at[down * 4 + m, 256:512]
        added(piece, piece, rn1.at[m, 1])
        n2.append(
            both("x", (part.at[up * 4 + m], rn2.at[m, 0]), (part.at[down * 4 + m], rn2.at[m, 1]))
        )

    outs = []

    def write(src, dst):
        copy = pltpu.make_async_copy(src, dst, out_sem.at[len(outs)])
        copy.start()
        outs.append(copy)

    def finish(i, d_normed):
        inverse = wide(inverse_ref[...])
        unit = tok[i].astype(F32) * inverse
        parts = d_normed * gain_ref[at.x * 8 + i]
        result = inverse * (parts - unit * (wide(column[...]) * (1.0 / width)))
        tok[i] = result.astype(BF16)
        first = pl.multiple_of(i * 256, 256)
        write(tok.at[i], dh_ref.at[:, pl.ds(first, 256)])

    c_sib = []

    def normed_sum(m):
        for copy in n2[m]:
            copy.wait_recv()

        def summed(low):
            rows = slice(low, low + 256)
            total = part[at.x * 4 + m, rows].astype(F32) + rn2[m, 0, rows].astype(F32)
            return total + rn2[m, 1, rows].astype(F32)

        out_sib[m] = summed(256).astype(BF16)
        c_sib.append(send(out_sib.at[m], in_sib.at[m], at.sibling()))
        finish(2 * m + at.core, summed(0))

    def sibling_part(m):
        c_sib[m].wait_recv()
        finish(2 * m + 1 - at.core, in_sib[m].astype(F32))

    for load in loads[:4]:
        load.wait()
    for load in loads[4:]:
        load.start()

    @pl.loop(0, 4)
    def _(b):
        attention(b, 0)

    pl.semaphore_wait(barrier, len(friends))
    c_dq = [share_dq(0)]
    own, other = slice(0, 256), slice(256, 512)
    transposed(0, own)
    for load in loads[4:8]:
        load.wait()
    attention(far, 1)
    encoded_grad(far)
    c_g1 = both("x", (grads.at[far, 0:128], g1.at[0]), (grads.at[far, 128:256], g1.at[1]))
    c_dq[0].wait_recv()
    transposed(0, other)
    product(0, 2, 2)
    first_hop(0, 1, 2)
    first_hop(0, 0, 2)
    for line in (1, 3, 0):
        product(0, 2, line)
        first_hop(0, 1, line)
        product(0, line, 2)
        first_hop(0, 0, line)
    attention(up, 1)
    attention(down, 1)
    encoded_grad(up)
    encoded_grad(down)
    c_g1[0].wait_recv()
    c_g1[1].wait_recv()
    gs[0, 0:128] = (grads[up, 0:128].astype(F32) + g1[0].astype(F32)).astype(BF16)
    gs[0, 128:256] = grads[up, 128:256]
    gs[1, 0:128] = grads[down, 0:128]
    gs[1, 128:256] = (grads[down, 128:256].astype(F32) + g1[1].astype(F32)).astype(BF16)
    c_g2 = both("x", (gs.at[0], g2.at[0]), (gs.at[1], g2.at[1]))
    second_hop(0, 1, 2)
    second_hop(0, 0, 2)
    attention(at.x, 1)
    c_dq.append(share_dq(1))
    write(ctx, ctx_ref)
    corners = ((1, 1), (3, 1), (1, 3), (3, 3))
    rest = ((1, 0), (3, 0), (0, 1), (0, 3), (0, 0))
    for dy, dz in corners:
        product(0, dy, dz)
    for line in (1, 3):
        second_hop(0, 1, line)
        second_hop(0, 0, line)
    for half in (0, 1):
        gathered(0, half, 2)
        turn(0, half)
    lanes = jnp.sum(jnp.transpose(sum_s[...]), axis=0, keepdims=True)
    sums[...] = jnp.broadcast_to(lanes, (8, 256))
    c_sums = [send(sums, sums_in.at[i], at.along("x", i + 1)) for i in range(3)]
    transposed(1, own)
    c_dq[1].wait_recv()
    transposed(1, other)
    product(1, 2, 2)
    first_hop(1, 1, 2)
    first_hop(1, 0, 2)
    for m, line in enumerate((1, 3, 0)):
        product(1, 2, line)
        first_hop(1, 1, line)
        product(1, line, 2)
        first_hop(1, 0, line)
        far_partial(m)
    far_partial(3)
    for dy, dz in rest:
        product(0, dy, dz)
    for half in (0, 1):
        gathered(0, half, 1)
        gathered(0, half, 3)
        turned(0, half)
    second_hop(1, 0, 2)
    second_hop(1, 1, 2)
    for dy, dz in corners:
        product(1, dy, dz)
    for line in (1, 3):
        second_hop(1, 0, line)
        second_hop(1, 1, line)
    encoded_grad(at.x)
    for copy in c_g2:
        copy.wait_recv()
    gfin[...] = (grads[at.x].astype(F32) + g2[0].astype(F32) + g2[1].astype(F32)).astype(BF16)
    c_swap = send(gfin, gin, at.partner())
    for m in range(4):
        partial(up * 4 + m)
        partial(down * 4 + m)
        near_partial(m)
    for dy, dz in rest:
        product(1, dy, dz)
    second_hop(0, 0, 0)
    second_hop(1, 0, 0)
    gathered(1, 0, 2)
    turn(1, 0)
    gathered(1, 1, 2)
    turn(1, 1)
    second_hop(0, 1, 0)
    gathered(1, 0, 1)
    gathered(1, 0, 3)
    turned(1, 0)
    second_hop(1, 1, 0)

    for copy in c_sums:
        copy.wait_recv()
    whole = sums[...] + sums_in[0] + sums_in[1] + sums_in[2]
    dots_ref[...] = whole[0:1] * (1.0 / math.sqrt(width))
    column[...] = jnp.transpose(jnp.broadcast_to(whole[0:1], (128, 256)))
    for load in loads[8:]:
        load.wait()
    for m in range(4):
        partial(at.x * 4 + m)
    normed_sum(0)
    normed_sum(1)
    sibling_part(0)
    gathered(1, 1, 1)
    gathered(1, 1, 3)
    turned(1, 1)
    normed_sum(2)
    sibling_part(1)
    result(0)
    normed_sum(3)
    sibling_part(2)
    sibling_part(3)
    result(1)
    c_swap.wait_recv()
    write(gin, de_ref)
    for copy in send.copies:
        copy.wait_send()
    for copy in outs:
        copy.wait()


BACKWARD_SENDS = 2 + 2 + 2 + 8 + 8 + 3 + 1 + 4 + 2 * 40


def backward(
    counts, queries, keys, values, d_context, w_key, w_value, normed, w_all, tokens, inverse, gain
):
    rows, width = queries.shape
    full = tokens.shape[1]
    vmem = pl.BlockSpec(memory_space=pltpu.VMEM)
    anywhere = pl.BlockSpec(memory_space=pl.ANY)

    def buffer(*shape, kind=BF16):
        return pltpu.VMEM(shape, kind)

    sizes = [size for group in range(2) for size in halves(group)]
    return pl.pallas_call(
        backward_kernel,
        in_specs=[pl.BlockSpec(memory_space=pltpu.SMEM)] + [anywhere] * 9 + [vmem, vmem],
        out_specs=[anywhere, vmem, anywhere, anywhere, vmem],
        out_shape=[
            jax.ShapeDtypeStruct((rows, width), BF16),
            jax.ShapeDtypeStruct((256, width), F32),
            jax.ShapeDtypeStruct((rows, full // 4), BF16),
            jax.ShapeDtypeStruct((KEYS, E), BF16),
            jax.ShapeDtypeStruct((1, rows), F32),
        ],
        scratch_shapes=[
            buffer(rows, width),
            buffer(rows, width),
            buffer(4, KEYS, width),
            buffer(4, KEYS, width),
            buffer(E, width),
            buffer(E, width),
            buffer(rows, width),
            buffer(6, BLOCK, KEYS, kind=F32),
            buffer(6, BLOCK, KEYS, kind=F32),
            buffer(6, BLOCK, KEYS),
            buffer(6, BLOCK, KEYS),
            buffer(rows, HD, kind=F32),
            buffer(512, 1024),
            buffer(1024, 512),
            buffer(16, 512, 256),
            buffer(16, 256, 1024),
            buffer(16, 1024, 256),
            buffer(768, 256, kind=F32),
            buffer(16, 512, 256),
            buffer(4, 2, 256, 256),
            buffer(4, 2, 512, 256),
            buffer(4, 256, 256),
            buffer(4, 256, 256),
            buffer(4, KEYS, E),
            buffer(2, 128, E),
            buffer(2, 256, E),
            buffer(2, 256, E),
            buffer(256, E),
            buffer(256, E),
            buffer(8, 256, kind=F32),
            buffer(3, 8, 256, kind=F32),
            buffer(8, 256, 256),
            buffer(256, 128, kind=F32),
        ]
        + [buffer(4, 2, size // 2, 256) for size in sizes]
        + [buffer(4, 2, size, 256) for size in sizes]
        + [buffer(2, size // 2, 256) for size in sizes]
        + [buffer(2, size, 256) for size in sizes]
        + [
            pltpu.SemaphoreType.DMA((LOADS,)),
            pltpu.SemaphoreType.DMA((10,)),
            pltpu.SemaphoreType.DMA((BACKWARD_SENDS,)),
            pltpu.SemaphoreType.DMA((BACKWARD_SENDS,)),
        ],
        compiler_params=pltpu.CompilerParams(
            collective_id=1, has_side_effects=True, vmem_limit_bytes=62 * 2**20
        ),
        cost_estimate=pl.CostEstimate(
            flops=12 * 2**30, bytes_accessed=30 * 2**20, transcendentals=0
        ),
    )(counts, queries, keys, values, d_context, w_key, w_value, normed, w_all, tokens, inverse, gain)


def results_kernel(*refs):
    count = len(refs) // 2
    for source, target in zip(refs[:count], refs[count:]):
        target[...] = source[...]


def results(*arrays):
    steps = 4
    specs = [
        pl.BlockSpec((array.shape[0] // steps, array.shape[1]), lambda i: (i, 0))
        for array in arrays
    ]
    return pl.pallas_call(
        results_kernel,
        grid=(steps,),
        in_specs=specs,
        out_specs=specs,
        out_shape=[jax.ShapeDtypeStruct(array.shape, array.dtype) for array in arrays],
        compiler_params=pltpu.CompilerParams(vmem_limit_bytes=62 * 2**20),
    )(*arrays)


def shards(
    tokens,
    w_query,
    query_gain,
    state_kv,
    neighbours,
    enc_gain,
    enc_query,
    enc_out,
    w_key,
    w_value,
    counts,
    d_context,
):
    gain = query_gain.reshape(32, 1, 256)
    queries, w_part, normed, keys, values, inverse = forward(
        tokens, w_query, gain, state_kv, neighbours.reshape(KEYS, E), enc_gain,
        enc_query, enc_out, w_key, w_value,
    )
    context, d_query_weight, d_hidden, d_encoded, row_dots = backward(
        counts, queries, keys, values, d_context, w_key, w_value, normed, w_part, tokens, inverse,
        gain,
    )
    context, d_query_weight, d_hidden, d_encoded = results(
        context, d_query_weight, d_hidden, d_encoded
    )
    return (
        context,
        d_hidden,
        d_query_weight,
        d_encoded.reshape(1, 1, NBR, RLEN, E),
        row_dots[0],
    )


def solution(mesh):
    return jax.shard_map(
        shards,
        mesh=mesh,
        in_specs=(
            P(("section", "seq"), None),
            P(("section", "seq"), "tensor"),
            P(),
            P("tensor", None),
            P("section", ("seq", "tensor"), None, None, None),
            P(),
            P(),
            P(),
            P(None, "tensor"),
            P(None, "tensor"),
            P(("section", "seq")),
            P(("section", "seq"), "tensor"),
        ),
        out_specs=(
            P(("section", "seq"), "tensor"),
            P(("section", "seq"), "tensor"),
            P(("section", "seq"), "tensor"),
            P("section", ("seq", "tensor"), None, None, None),
            P(("section", "seq")),
        ),
        check_vma=False,
    )
```

```python
import functools
import math

import jax
import jax.numpy as jnp
from jax import lax
from jax.experimental import pallas as pl
from jax.experimental.pallas import tpu as pltpu
from jax.sharding import PartitionSpec as P

HD = 128
E = 896
EHD = 64
BLOCK = 64
NBR = 2
RLEN = 128
KEYS = NBR * RLEN

EPSILON = 1e-05
NEG_LARGE = -1e30
MESH = pl.DeviceIdType.MESH
F32 = jnp.float32
BF16 = jnp.bfloat16
LAST = (((1,), (1,)), ((), ()))
FIRST = (((0,), (0,)), ((), ()))


def dot(a, b, dims=(((1,), (0,)), ((), ()))):
    return lax.dot_general(a, b, dims, preferred_element_type=F32)


class Place:
    def __init__(self):
        self.section = lax.axis_index("section")
        seq = lax.axis_index("seq")
        self.x = lax.axis_index("tensor")
        self.core = seq % 2
        self.y = seq // 4
        self.z = 2 * ((seq // 2) % 2) + self.section

    def along(self, dim, off):
        if dim == "x":
            return (self.section, self.seq_of(self.y, self.z), (self.x + off) % 4)
        if dim == "y":
            return (self.section, self.seq_of((self.y + off) % 4, self.z), self.x)
        z = (self.z + off) % 4
        return (z % 2, self.seq_of(self.y, z), self.x)

    def seq_of(self, y, z):
        return y * 4 + (z // 2) * 2 + self.core

    def sibling(self):
        return (self.section, self.y * 4 + (self.z // 2) * 2 + 1 - self.core, self.x)

    def partner(self):
        return (1 - self.section, self.seq_of(self.y, self.z), self.x)

    def chunk(self, dy, dz):
        y, z = (self.y + dy) % 4, (self.z + dz) % 4
        return (z % 2) * 8 + y * 2 + z // 2


def greet(devices):
    barrier = pltpu.get_barrier_semaphore()
    for device in devices:
        pl.semaphore_signal(barrier, inc=1, device_id=device, device_id_type=MESH)
    pl.semaphore_wait(barrier, len(devices))


class Sender:
    def __init__(self, send_sem, recv_sem):
        self.send_sem, self.recv_sem, self.copies = send_sem, recv_sem, []

    def __call__(self, src, dst, device):
        index = len(self.copies)
        copy = pltpu.make_async_remote_copy(
            src_ref=src, dst_ref=dst, send_sem=self.send_sem.at[index],
            recv_sem=self.recv_sem.at[index], device_id=device, device_id_type=MESH,
        )
        copy.start()
        self.copies.append(copy)
        return copy


Y_FIRST = 96
CHUNK = 256


def wide(column):
    return jnp.concatenate([column, column], axis=1)


def forward_kernel(
    tokens_ref, w_ref, gain_ref, state_ref, near_ref, egain_ref, equery_ref, eout_ref, wk_ref, wv_ref,
    q_ref, w_out, nrm_out, k_out, v_out, inv_ref,
    tok, wc, nrm, theirs, skv, unit, acc, q_send, q_in,
    sp, sr1, sr2, enc_in, eq_s, ectx, escore, equery, eout, enc, wk, wv, ks, vs,
    load_sem, out_sem, send_sem, recv_sem,
):
    at = Place()
    share = tok.shape[1] // 4
    send = Sender(send_sem, recv_sem)
    me = at.chunk(0, 0)
    pairs = (
        (w_ref, wc.at[me]), (tokens_ref, tok), (state_ref, skv), (equery_ref, equery),
        (eout_ref, eout), (wk_ref, wk), (wv_ref, wv),
    )
    loads = [pltpu.make_async_copy(src, dst, load_sem.at[i]) for i, (src, dst) in enumerate(pairs)]
    for load in loads:
        load.start()
    greet(
        [at.along("x", 1), at.along("x", 3), at.along("y", 1), at.along("y", 3),
         at.along("z", 1), at.along("z", 3), at.sibling()]
    )

    dims = (("y", "z"), ("z", "y"))
    spans = ((0, Y_FIRST), (Y_FIRST, CHUNK))

    def piece(half, first, second, part=None):
        dy, dz = (first, second) if half == 0 else (second, first)
        low, high = spans[half]
        middle = (low + high) // 2
        low, high = (low, high) if part is None else ((low, middle), (middle, high))[part]
        return wc.at[at.chunk(dy, dz), low:high]

    def pass_on(ref, dim, off):
        return send(ref, ref, at.along(dim, off))

    near, relay, cross, last = {}, {}, {}, {}

    def across(half, line):
        dim = dims[half][1]
        block = piece(half, line, 0)
        cross[half, line] = (pass_on(block, dim, 1), pass_on(block, dim, 3))

    def relays(half):
        dim = dims[half][0]
        near[half][0].wait_recv()
        first = pass_on(piece(half, 3, 0, 0), dim, 1)
        near[half][1].wait_recv()
        relay[half] = (first, pass_on(piece(half, 1, 0, 1), dim, 3))

    def relayed(half):
        relay[half][0].wait_recv()
        relay[half][1].wait_recv()
        across(half, 2)

    def crossed(half, line):
        dim = dims[half][1]
        cross[half, line][0].wait_recv()
        first = pass_on(piece(half, line, 3, 0), dim, 1)
        cross[half, line][1].wait_recv()
        last[half, line] = (first, pass_on(piece(half, line, 1, 1), dim, 3))

    def landed(half, line):
        last[half, line][0].wait_recv()
        last[half, line][1].wait_recv()

    outs = []

    def write(src, dst):
        copy = pltpu.make_async_copy(src, dst, out_sem.at[len(outs)])
        copy.start()
        outs.append(copy)

    def accumulate(offsets, begin=False):
        chunks = [at.chunk(dy, dz) for dy, dz in offsets]
        for k in chunks:
            write(wc.at[k], w_out.at[k])

        @pl.loop(0, 4)
        def _(i):
            rows = pl.ds(pl.multiple_of((i // 2) * 256, 256), 256)
            cols = pl.ds(pl.multiple_of((i % 2) * 512, 512), 512)
            total = dot(nrm[chunks[0], rows, :], wc[chunks[0], :, cols])
            for k in chunks[1:]:
                total = total + dot(nrm[k, rows, :], wc[k, :, cols])
            acc[rows, cols] = total if begin else acc[rows, cols] + total

    loads[0].wait()
    for half in (0, 1):
        block = piece(half, 0, 0)
        near[half] = (pass_on(block, dims[half][0], 1), pass_on(block, dims[half][0], 3))
    c_near = send(near_ref, enc_in, at.partner())
    across(1, 0)

    loads[1].wait()

    @pl.loop(0, 16)
    def _(i):
        rows = pl.ds(pl.multiple_of(i * 16, 16), 16)
        values = tok[rows, :].astype(F32)
        square = jnp.sum(values * values, axis=-1, keepdims=True)
        inverse = lax.rsqrt(square * (1.0 / tok.shape[1]) + EPSILON)
        inv_ref[rows, :] = jnp.broadcast_to(inverse, (16, 128))

    @pl.loop(0, 8)
    def _(i):
        source = pl.ds(pl.multiple_of(at.x * share + i * 256, 256), 256)
        target = pl.ds(pl.multiple_of(i * 256, 256), 256)
        unit[:, target] = (tok[:, source].astype(F32) * wide(inv_ref[...])).astype(BF16)

    loads[2].wait()

    @pl.loop(0, 7)
    def _(i):
        cols = pl.ds(pl.multiple_of(i * 256, 256), 256)
        part = dot(unit[...], skv[:, cols]).astype(BF16)
        for j in range(4):
            sp[j, :, cols] = part[64 * j : 64 * j + 64]

    far, up, down = (at.x + 2) % 4, (at.x + 1) % 4, (at.x + 3) % 4
    c_s1 = (
        send(sp.at[far, 0:32], sr1.at[0], at.along("x", 1)),
        send(sp.at[far, 32:64], sr1.at[1], at.along("x", 3)),
    )
    relays(0)
    relays(1)
    across(1, 3)
    across(1, 1)
    for line in (0, 3, 1):
        across(0, line)

    @pl.loop(0, 16)
    def _(k):
        def chunk(g):
            cols = pl.ds(pl.multiple_of(g * CHUNK, CHUNK), CHUNK)
            return (tok[:, cols].astype(F32) * wide(inv_ref[...]) * gain_ref[g]).astype(BF16)

        nrm[k, 0:256] = chunk(2 * k + at.core)
        theirs[k] = chunk(2 * k + 1 - at.core)

    c_nrm = send(theirs, nrm.at[:, 256:512], at.sibling())

    for way, block in ((0, up), (1, down)):
        c_s1[way].wait_recv()
        rows = slice(32 * way, 32 * way + 32)
        sp[block, rows] = (sp[block, rows].astype(F32) + sr1[way].astype(F32)).astype(BF16)
    c_s2 = (
        send(sp.at[up], sr2.at[0], at.along("x", 1)),
        send(sp.at[down], sr2.at[1], at.along("x", 3)),
    )
    relayed(0)
    crossed(1, 0)

    loads[3].wait()
    c_near.wait_recv()
    enc_rows = enc_in[...].astype(F32)
    mean = jnp.sum(enc_rows * enc_rows, axis=-1, keepdims=True) * (1.0 / E)
    enc_normed = (enc_rows * lax.rsqrt(mean + EPSILON) * egain_ref[...].reshape(1, E)).astype(BF16)
    eq_s[...] = dot(enc_normed, equery[...]).astype(BF16)

    c_s2[0].wait_recv()
    c_s2[1].wait_recv()
    states = (sp[at.x].astype(F32) + sr2[0].astype(F32) + sr2[1].astype(F32)).astype(BF16)
    states = states.astype(F32)
    left = lax.broadcasted_iota(jnp.int32, (BLOCK, 128), 1) < EHD
    left_wide = lax.broadcasted_iota(jnp.int32, (KEYS, 128), 1) < EHD

    def doubled(cols):
        both = states[:, cols]
        return jnp.concatenate(
            [jnp.where(left, both, 0.0), jnp.where(left, 0.0, both)], axis=0
        ).astype(BF16)

    for j in range(7):
        keys = doubled(slice(128 * j, 128 * j + 128))
        escore[j] = dot(eq_s[:, 128 * j : 128 * j + 128], keys, LAST) * (1.0 / math.sqrt(EHD))
    for j in range(7):
        scores = escore[j]
        top_left = jnp.max(jnp.where(left_wide, scores, NEG_LARGE), axis=-1, keepdims=True)
        top_right = jnp.max(jnp.where(left_wide, NEG_LARGE, scores), axis=-1, keepdims=True)
        weights = jnp.exp(scores - jnp.where(left_wide, top_left, top_right))
        sum_left = jnp.sum(jnp.where(left_wide, weights, 0.0), axis=-1, keepdims=True)
        sum_right = jnp.sum(jnp.where(left_wide, 0.0, weights), axis=-1, keepdims=True)
        escore[j] = weights / jnp.where(left_wide, sum_left, sum_right)
    for j in range(7):
        values = doubled(slice(E + 128 * j, E + 128 * j + 128))
        ectx[:, 128 * j : 128 * j + 128] = dot(escore[j].astype(BF16), values).astype(BF16)
    loads[4].wait()
    enc[at.x] = (enc_in[...].astype(F32) + dot(ectx[...], eout[...])).astype(BF16)
    c_e1 = (
        send(enc.at[at.x], enc.at[at.x], at.along("x", 1)),
        send(enc.at[at.x], enc.at[at.x], at.along("x", 3)),
    )
    relayed(1)
    loads[5].wait()
    loads[6].wait()

    def project(block):
        @pl.loop(0, 4)
        def _(i):
            cols = pl.ds(pl.multiple_of(i * 256, 256), 256)
            ks[block, :, cols] = dot(enc[block], wk[:, cols]).astype(BF16)
            vs[block, :, cols] = dot(enc[block], wv[:, cols]).astype(BF16)

        write(ks.at[block], k_out.at[block])
        write(vs.at[block], v_out.at[block])

    c_nrm.wait_recv()
    write(nrm, nrm_out)
    crossed(0, 0)
    accumulate([(0, 0), (1, 0), (3, 0), (0, 1), (0, 3)], begin=True)
    crossed(1, 3)
    crossed(1, 1)
    project(at.x)
    crossed(0, 3)
    crossed(0, 1)
    c_e1[0].wait_recv()
    c_e2 = [send(enc.at[down, 0:128], enc.at[down, 0:128], at.along("x", 1))]
    c_e1[1].wait_recv()
    c_e2.append(send(enc.at[up, 128:256], enc.at[up, 128:256], at.along("x", 3)))
    project(down)
    project(up)
    accumulate([(1, 1), (1, 3), (3, 1), (3, 3)])
    crossed(1, 2)
    crossed(0, 2)
    landed(0, 0)
    landed(1, 0)
    accumulate([(2, 0), (0, 2)])
    c_e2[0].wait_recv()
    c_e2[1].wait_recv()
    project(far)
    for line in (3, 1):
        landed(0, line)
        landed(1, line)
    accumulate([(2, 1), (2, 3), (1, 2), (3, 2)])
    landed(0, 2)
    landed(1, 2)
    accumulate([(2, 2)])
    q_send[...] = acc[256:512].astype(BF16)
    c_q = send(q_send, q_in, at.sibling())
    c_q.wait_recv()
    q_ref[...] = (acc[0:256] + q_in[...].astype(F32)).astype(BF16)
    for copy in send.copies:
        copy.wait_send()
    for copy in outs:
        copy.wait()


FORWARD_SENDS = 4 + 1 + 4 + 2 * 6 + 2 * 2 + 16 + 2 + 2 + 1 + 2 + 2 + 1


def forward(tokens, w_query, gain, state_kv, near, enc_gain, enc_query, enc_out, w_key, w_value):
    rows, full = tokens.shape
    width = w_query.shape[1]
    vmem = pl.BlockSpec(memory_space=pltpu.VMEM)
    anywhere = pl.BlockSpec(memory_space=pl.ANY)

    def buffer(*shape, kind=BF16):
        return pltpu.VMEM(shape, kind)

    return pl.pallas_call(
        forward_kernel,
        in_specs=[anywhere, anywhere, vmem, anywhere, anywhere, vmem] + [anywhere] * 4,
        out_specs=[vmem] + [anywhere] * 4 + [vmem],
        out_shape=[
            jax.ShapeDtypeStruct((rows, width), BF16),
            jax.ShapeDtypeStruct((16, CHUNK, width), BF16),
            jax.ShapeDtypeStruct((16, 2 * rows, CHUNK), BF16),
            jax.ShapeDtypeStruct((4, KEYS, width), BF16),
            jax.ShapeDtypeStruct((4, KEYS, width), BF16),
            jax.ShapeDtypeStruct((rows, 128), F32),
        ],
        scratch_shapes=[
            buffer(rows, full),
            buffer(16, CHUNK, width),
            buffer(16, 2 * rows, CHUNK),
            buffer(16, rows, CHUNK),
            buffer(full // 4, 2 * E),
            buffer(rows, full // 4),
            buffer(2 * rows, width, kind=F32),
            buffer(rows, width),
            buffer(rows, width),
            buffer(4, BLOCK, 2 * E),
            buffer(2, BLOCK // 2, 2 * E),
            buffer(2, BLOCK, 2 * E),
            buffer(KEYS, E),
            buffer(KEYS, E),
            buffer(KEYS, E),
            buffer(7, KEYS, 128, kind=F32),
            buffer(E, E),
            buffer(E, E),
            buffer(4, KEYS, E),
            buffer(E, width),
            buffer(E, width),
            buffer(4, KEYS, width),
            buffer(4, KEYS, width),
            pltpu.SemaphoreType.DMA((7,)),
            pltpu.SemaphoreType.DMA((25,)),
            pltpu.SemaphoreType.DMA((FORWARD_SENDS,)),
            pltpu.SemaphoreType.DMA((FORWARD_SENDS,)),
        ],
        compiler_params=pltpu.CompilerParams(
            collective_id=2, has_side_effects=True, vmem_limit_bytes=60 * 2**20
        ),
        cost_estimate=pl.CostEstimate(
            flops=2 * 5400 * 2**20, bytes_accessed=40 * 2**20, transcendentals=0
        ),
    )(tokens, w_query, gain, state_kv, near, enc_gain, enc_query, enc_out, w_key, w_value)


LINES = (2, 1, 3, 0)
GROUPS = ((0, 384, 160), (384, 1024, 224))
LOADS = 16


def halves(group):
    first, stop, z_first = GROUPS[group]
    return z_first, stop - first - z_first


def backward_kernel(
    counts, q_ref, k_ref, v_ref, do_ref, wk_ref, wv_ref, nrm_ref, w_ref, tokens_ref,
    inverse_ref, gain_ref,
    ctx_ref, dw_ref, dh_ref, de_ref, dots_ref,
    qs, dos, ks, vs, wk, wv, ctx, score_s, dprob_s, weight_s, dscore_s, sum_s,
    dq2, dq_t, nrm, wc, prod, dw_t, dw_s, part, rn1, rn2, out_sib, in_sib,
    grads, g1, gs, g2, gfin, gin, sums, sums_in, tok, column,
    ra1_00, ra1_01, ra1_10, ra1_11, ra2_00, ra2_01, ra2_10, ra2_11,
    rb1_00, rb1_01, rb1_10, rb1_11, rb2_00, rb2_01, rb2_10, rb2_11,
    load_sem, out_sem, send_sem, recv_sem,
):
    at = Place()
    width = tokens_ref.shape[1]
    share = width // 4
    ra1 = ((ra1_00, ra1_01), (ra1_10, ra1_11))
    ra2 = ((ra2_00, ra2_01), (ra2_10, ra2_11))
    rb1 = ((rb1_00, rb1_01), (rb1_10, rb1_11))
    rb2 = ((rb2_00, rb2_01), (rb2_10, rb2_11))
    pairs = [
        (q_ref, qs), (do_ref, dos), (k_ref, ks), (v_ref, vs), (wk_ref, wk), (wv_ref, wv),
        (nrm_ref, nrm), (w_ref, wc),
    ]
    for i in range(8):
        first = pl.multiple_of(at.x * share + i * 256, 256)
        pairs.append((tokens_ref.at[:, pl.ds(first, 256)], tok.at[i]))
    loads = [pltpu.make_async_copy(src, dst, load_sem.at[i]) for i, (src, dst) in enumerate(pairs)]
    for load in loads[:4]:
        load.start()
    barrier = pltpu.get_barrier_semaphore()
    friends = [at.along("x", 1), at.along("x", 2), at.along("x", 3), at.along("y", 1),
               at.along("y", 3), at.along("z", 1), at.along("z", 3), at.sibling()]
    for friend in friends:
        pl.semaphore_signal(barrier, inc=1, device_id=friend, device_id_type=MESH)

    send = Sender(send_sem, recv_sem)
    far, up, down = (at.x + 2) % 4, (at.x + 1) % 4, (at.x + 3) % 4
    scale = 1.0 / math.sqrt(HD)

    def added(dst, first, second):
        dst[...] = (first[...].astype(F32) + second[...].astype(F32)).astype(BF16)

    def both(dim, one, other):
        return send(*one, at.along(dim, 1)), send(*other, at.along(dim, 3))

    def attention(b, group):
        first, stop, _ = GROUPS[group]
        spans = [slice(low, low + HD) for low in range(first, stop, HD)]
        rows = pl.ds(pl.multiple_of(b * BLOCK, BLOCK), BLOCK)
        count = counts[b]
        valid = lax.broadcasted_iota(jnp.int32, (BLOCK, KEYS), 1) < count * RLEN
        empty = jnp.where(count == 0, 1.0, 0.0).astype(F32)
        for i, cols in enumerate(spans):
            score_s[i] = dot(qs[rows, cols], ks[b, :, cols], LAST) * scale
            dprob_s[i] = dot(dos[rows, cols], vs[b, :, cols], LAST)
        for i in range(len(spans)):
            scores = score_s[i]
            top = jnp.max(jnp.where(valid, scores, NEG_LARGE), axis=-1, keepdims=True)
            weights = jnp.where(valid, jnp.exp(scores - top), 0.0)
            probs = weights / (jnp.sum(weights, axis=-1, keepdims=True) + empty)
            weight_s[i] = probs.astype(BF16)
            d_probs = dprob_s[i]
            inner = jnp.sum(probs * d_probs, axis=-1, keepdims=True)
            dscore_s[i] = (probs * (d_probs - inner) * scale).astype(BF16)
        total = jnp.zeros((BLOCK, HD), F32)
        for i, cols in enumerate(spans):
            ctx[rows, cols] = dot(weight_s[i], vs[b, :, cols]).astype(BF16)
            dq = dot(dscore_s[i], ks[b, :, cols])
            dq2[rows, cols] = dq.astype(BF16)
            total = total + dq * qs[rows, cols].astype(F32)
            vs[b, :, cols] = dot(weight_s[i], dos[rows, cols], FIRST).astype(BF16)
            ks[b, :, cols] = dot(dscore_s[i], qs[rows, cols], FIRST).astype(BF16)
        sum_s[rows, :] = total if group == 0 else sum_s[rows, :] + total

    def encoded_grad(b):
        grad = dot(ks[b], wk[...], LAST) + dot(vs[b], wv[...], LAST)
        grads[b] = grad.astype(BF16)

    def share_dq(group):
        first, stop, _ = GROUPS[group]
        return send(dq2.at[0:256, first:stop], dq2.at[256:512, first:stop], at.sibling())

    def transposed(group, rows):
        first, stop, _ = GROUPS[group]
        for low in range(first, stop, 128):
            dq_t[low : low + 128, rows] = jnp.transpose(dq2[rows, low : low + 128])

    def product(group, dy, dz):
        k = at.chunk(dy, dz)
        first, stop, _ = GROUPS[group]
        prod[k, first:stop] = dot(dq_t[first:stop], nrm[k]).astype(BF16)

    dims = (("z", "y"), ("y", "z"))

    def block(group, half, line, off, part=None):
        dy, dz = (line, off) if half == 0 else (off, line)
        first, stop, z_first = GROUPS[group]
        low, high = ((first, first + z_first), (first + z_first, stop))[half]
        middle = (low + high) // 2
        low, high = (low, high) if part is None else ((low, middle), (middle, high))[part]
        return prod.at[at.chunk(dy, dz), low:high]

    c1, c2, d1, d2 = {}, {}, {}, {}

    def first_hop(group, half, line):
        slot = ra1[group][half].at[LINES.index(line)]
        c1[group, half, line] = both(
            dims[half][0],
            (block(group, half, line, 2, 0), slot.at[0]),
            (block(group, half, line, 2, 1), slot.at[1]),
        )

    def second_hop(group, half, line):
        for way, off in ((0, 1), (1, 3)):
            c1[group, half, line][way].wait_recv()
            piece = block(group, half, line, off, way)
            added(piece, piece, ra1[group][half].at[LINES.index(line), way])
        slot = ra2[group][half].at[LINES.index(line)]
        c2[group, half, line] = both(
            dims[half][0],
            (block(group, half, line, 1), slot.at[0]),
            (block(group, half, line, 3), slot.at[1]),
        )

    def gathered(group, half, line):
        for way in (0, 1):
            c2[group, half, line][way].wait_recv()
        slot = ra2[group][half].at[LINES.index(line)]
        piece = block(group, half, line, 0)
        total = piece[...].astype(F32) + slot[0].astype(F32) + slot[1].astype(F32)
        piece[...] = total.astype(BF16)

    def turn(group, half):
        d1[group, half] = both(
            dims[half][1],
            (block(group, half, 2, 0, 0), rb1[group][half].at[0]),
            (block(group, half, 2, 0, 1), rb1[group][half].at[1]),
        )

    def turned(group, half):
        for way, off in ((0, 1), (1, 3)):
            d1[group, half][way].wait_recv()
            piece = block(group, half, off, 0, way)
            added(piece, piece, rb1[group][half].at[way])
        d2[group, half] = both(
            dims[half][1],
            (block(group, half, 1, 0), rb2[group][half].at[0]),
            (block(group, half, 3, 0), rb2[group][half].at[1]),
        )

    def result(group):
        first, stop, _ = GROUPS[group]
        sizes = halves(group)
        for half in (0, 1):
            for way in (0, 1):
                c2[group, half, 0][way].wait_recv()
                d2[group, half][way].wait_recv()
            own = block(group, half, 0, 0)
            slot = ra2[group][half].at[LINES.index(0)]
            total = own[...].astype(F32) + slot[0].astype(F32) + slot[1].astype(F32)
            low = half * sizes[0]
            dw_t[low : low + sizes[half]] = (
                total + rb2[group][half][0].astype(F32) + rb2[group][half][1].astype(F32)
            )
        for low in range(0, stop - first, 128):
            dw_s[:, first + low : first + low + 128] = jnp.transpose(dw_t[low : low + 128])
        write(dw_s.at[:, first:stop], dw_ref.at[:, first:stop])

    def partial(k):
        part[k] = dot(dq2[...], wc[k], LAST).astype(BF16)

    n1, n2 = [], []

    def far_partial(m):
        partial(far * 4 + m)
        n1.append(
            both("x", (part.at[far * 4 + m, 0:256], rn1.at[m, 0]),
                 (part.at[far * 4 + m, 256:512], rn1.at[m, 1]))
        )

    def summed_partial(m):
        partial(up * 4 + m)
        partial(down * 4 + m)
        n1[m][0].wait_recv()
        piece = part.at[up * 4 + m, 0:256]
        added(piece, piece, rn1.at[m, 0])
        n1[m][1].wait_recv()
        piece = part.at[down * 4 + m, 256:512]
        added(piece, piece, rn1.at[m, 1])
        n2.append(
            both("x", (part.at[up * 4 + m], rn2.at[m, 0]), (part.at[down * 4 + m], rn2.at[m, 1]))
        )

    outs = []

    def write(src, dst):
        copy = pltpu.make_async_copy(src, dst, out_sem.at[len(outs)])
        copy.start()
        outs.append(copy)

    def finish(i, d_normed):
        inverse = wide(inverse_ref[...])
        unit = tok[i].astype(F32) * inverse
        parts = d_normed * gain_ref[at.x * 8 + i]
        result = inverse * (parts - unit * (wide(column[...]) * (1.0 / width)))
        tok[i] = result.astype(BF16)
        first = pl.multiple_of(i * 256, 256)
        write(tok.at[i], dh_ref.at[:, pl.ds(first, 256)])

    c_sib = []

    def normed_sum(m):
        for copy in n2[m]:
            copy.wait_recv()

        def summed(low):
            rows = slice(low, low + 256)
            total = part[at.x * 4 + m, rows].astype(F32) + rn2[m, 0, rows].astype(F32)
            return total + rn2[m, 1, rows].astype(F32)

        out_sib[m] = summed(256).astype(BF16)
        c_sib.append(send(out_sib.at[m], in_sib.at[m], at.sibling()))
        finish(2 * m + at.core, summed(0))

    def sibling_part(m):
        c_sib[m].wait_recv()
        finish(2 * m + 1 - at.core, in_sib[m].astype(F32))

    for load in loads[:4]:
        load.wait()
    for load in loads[4:]:
        load.start()

    @pl.loop(0, 4)
    def _(b):
        attention(b, 0)

    pl.semaphore_wait(barrier, len(friends))
    c_dq = [share_dq(0)]
    own, other = slice(0, 256), slice(256, 512)
    transposed(0, own)
    for load in loads[4:8]:
        load.wait()
    attention(far, 1)
    encoded_grad(far)
    c_g1 = both("x", (grads.at[far, 0:128], g1.at[0]), (grads.at[far, 128:256], g1.at[1]))
    c_dq[0].wait_recv()
    transposed(0, other)
    product(0, 2, 2)
    first_hop(0, 1, 2)
    first_hop(0, 0, 2)

    def leading(line):
        product(0, 2, line)
        first_hop(0, 1, line)
        product(0, line, 2)
        first_hop(0, 0, line)

    leading(1)
    attention(up, 1)
    attention(down, 1)
    encoded_grad(up)
    encoded_grad(down)
    c_g1[0].wait_recv()
    c_g1[1].wait_recv()
    gs[0, 0:128] = (grads[up, 0:128].astype(F32) + g1[0].astype(F32)).astype(BF16)
    gs[0, 128:256] = grads[up, 128:256]
    gs[1, 0:128] = grads[down, 0:128]
    gs[1, 128:256] = (grads[down, 128:256].astype(F32) + g1[1].astype(F32)).astype(BF16)
    c_g2 = both("x", (gs.at[0], g2.at[0]), (gs.at[1], g2.at[1]))
    leading(3)
    leading(0)
    second_hop(0, 1, 2)
    second_hop(0, 0, 2)
    attention(at.x, 1)
    c_dq.append(share_dq(1))
    write(ctx, ctx_ref)
    corners = ((1, 1), (3, 1), (1, 3), (3, 3))
    rest = ((1, 0), (3, 0), (0, 1), (0, 3), (0, 0))
    for dy, dz in corners:
        product(0, dy, dz)
    for line in (1, 3):
        second_hop(0, 1, line)
        second_hop(0, 0, line)
    for half in (0, 1):
        gathered(0, half, 2)
        turn(0, half)
    lanes = jnp.sum(jnp.transpose(sum_s[...]), axis=0, keepdims=True)
    sums[...] = jnp.broadcast_to(lanes, (8, 256))
    c_sums = [send(sums, sums_in.at[i], at.along("x", i + 1)) for i in range(3)]
    transposed(1, own)
    c_dq[1].wait_recv()
    transposed(1, other)
    product(1, 2, 2)
    first_hop(1, 1, 2)
    first_hop(1, 0, 2)
    for m, line in enumerate((1, 3, 0)):
        product(1, 2, line)
        first_hop(1, 1, line)
        product(1, line, 2)
        first_hop(1, 0, line)
        far_partial(m)
    far_partial(3)
    for dy, dz in rest:
        product(0, dy, dz)
    for half in (0, 1):
        gathered(0, half, 1)
        gathered(0, half, 3)
        turned(0, half)
    second_hop(1, 0, 2)
    second_hop(1, 1, 2)
    for dy, dz in corners:
        product(1, dy, dz)
    for line in (1, 3):
        second_hop(1, 0, line)
        second_hop(1, 1, line)
    summed_partial(0)
    encoded_grad(at.x)
    for copy in c_g2:
        copy.wait_recv()
    gfin[...] = (grads[at.x].astype(F32) + g2[0].astype(F32) + g2[1].astype(F32)).astype(BF16)
    c_swap = send(gfin, gin, at.partner())
    for m in range(1, 4):
        summed_partial(m)
    for dy, dz in rest:
        product(1, dy, dz)
    gathered(1, 0, 2)
    turn(1, 0)
    gathered(1, 1, 2)
    turn(1, 1)
    second_hop(0, 0, 0)
    second_hop(0, 1, 0)

    for copy in c_sums:
        copy.wait_recv()
    whole = sums[...] + sums_in[0] + sums_in[1] + sums_in[2]
    dots_ref[...] = whole[0:1] * (1.0 / math.sqrt(width))
    column[...] = jnp.transpose(jnp.broadcast_to(whole[0:1], (128, 256)))
    for load in loads[8:]:
        load.wait()
    for m in range(4):
        partial(at.x * 4 + m)
    normed_sum(0)
    gathered(1, 0, 1)
    gathered(1, 0, 3)
    turned(1, 0)
    second_hop(1, 1, 0)
    gathered(1, 1, 1)
    gathered(1, 1, 3)
    turned(1, 1)
    second_hop(1, 0, 0)
    normed_sum(1)
    sibling_part(0)
    normed_sum(2)
    sibling_part(1)
    result(0)
    c_swap.wait_recv()
    write(gin, de_ref)
    sibling_part(2)
    normed_sum(3)
    result(1)
    sibling_part(3)
    for copy in send.copies:
        copy.wait_send()
    for copy in outs:
        copy.wait()


BACKWARD_SENDS = 2 + 2 + 2 + 8 + 8 + 3 + 1 + 4 + 2 * 40


def backward(
    counts, queries, keys, values, d_context, w_key, w_value, normed, w_all, tokens, inverse, gain
):
    rows, width = queries.shape
    full = tokens.shape[1]
    vmem = pl.BlockSpec(memory_space=pltpu.VMEM)
    anywhere = pl.BlockSpec(memory_space=pl.ANY)

    def buffer(*shape, kind=BF16):
        return pltpu.VMEM(shape, kind)

    sizes = [size for group in range(2) for size in halves(group)]
    return pl.pallas_call(
        backward_kernel,
        in_specs=[pl.BlockSpec(memory_space=pltpu.SMEM)] + [anywhere] * 9 + [vmem, vmem],
        out_specs=[anywhere] * 4 + [vmem],
        out_shape=[
            jax.ShapeDtypeStruct((rows, width), BF16),
            jax.ShapeDtypeStruct((256, width), F32),
            jax.ShapeDtypeStruct((rows, full // 4), BF16),
            jax.ShapeDtypeStruct((KEYS, E), BF16),
            jax.ShapeDtypeStruct((1, rows), F32),
        ],
        scratch_shapes=[
            buffer(rows, width),
            buffer(rows, width),
            buffer(4, KEYS, width),
            buffer(4, KEYS, width),
            buffer(E, width),
            buffer(E, width),
            buffer(rows, width),
            buffer(6, BLOCK, KEYS, kind=F32),
            buffer(6, BLOCK, KEYS, kind=F32),
            buffer(6, BLOCK, KEYS),
            buffer(6, BLOCK, KEYS),
            buffer(rows, HD, kind=F32),
            buffer(512, 1024),
            buffer(1024, 512),
            buffer(16, 512, 256),
            buffer(16, 256, 1024),
            buffer(16, 1024, 256),
            buffer(768, 256, kind=F32),
            buffer(256, width, kind=F32),
            buffer(16, 512, 256),
            buffer(4, 2, 256, 256),
            buffer(4, 2, 512, 256),
            buffer(4, 256, 256),
            buffer(4, 256, 256),
            buffer(4, KEYS, E),
            buffer(2, 128, E),
            buffer(2, 256, E),
            buffer(2, 256, E),
            buffer(256, E),
            buffer(256, E),
            buffer(8, 256, kind=F32),
            buffer(3, 8, 256, kind=F32),
            buffer(8, 256, 256),
            buffer(256, 128, kind=F32),
        ]
        + [buffer(4, 2, size // 2, 256) for size in sizes]
        + [buffer(4, 2, size, 256) for size in sizes]
        + [buffer(2, size // 2, 256) for size in sizes]
        + [buffer(2, size, 256) for size in sizes]
        + [
            pltpu.SemaphoreType.DMA((LOADS,)),
            pltpu.SemaphoreType.DMA((12,)),
            pltpu.SemaphoreType.DMA((BACKWARD_SENDS,)),
            pltpu.SemaphoreType.DMA((BACKWARD_SENDS,)),
        ],
        compiler_params=pltpu.CompilerParams(
            collective_id=1, has_side_effects=True, vmem_limit_bytes=62 * 2**20
        ),
        cost_estimate=pl.CostEstimate(
            flops=12 * 2**30, bytes_accessed=30 * 2**20, transcendentals=0
        ),
    )(counts, queries, keys, values, d_context, w_key, w_value, normed, w_all, tokens, inverse, gain)


def results_kernel(*refs):
    count = (len(refs) - 2) // 3
    in_sem, out_sem = refs[-2:]
    coming, going = [], []
    for source, target, held in zip(refs, refs[count:], refs[2 * count : 3 * count]):
        pieces = min(2, source.shape[0])
        rows = source.shape[0] // pieces
        for i in range(pieces):
            piece, index = pl.ds(i * rows, rows), len(coming)
            coming.append(
                pltpu.make_async_copy(source.at[piece], held.at[piece], in_sem.at[index])
            )
            going.append(
                pltpu.make_async_copy(held.at[piece], target.at[piece], out_sem.at[index])
            )
    for copy in coming:
        copy.start()
    for arrived, copy in zip(coming, going):
        arrived.wait()
        copy.start()
    for copy in going:
        copy.wait()


def results(*arrays):
    anywhere = pl.BlockSpec(memory_space=pl.ANY)
    return pl.pallas_call(
        results_kernel,
        in_specs=[anywhere] * len(arrays),
        out_specs=[anywhere] * len(arrays),
        out_shape=[jax.ShapeDtypeStruct(array.shape, array.dtype) for array in arrays],
        scratch_shapes=[pltpu.VMEM(array.shape, array.dtype) for array in arrays]
        + [pltpu.SemaphoreType.DMA((2 * len(arrays),))] * 2,
        compiler_params=pltpu.CompilerParams(vmem_limit_bytes=62 * 2**20),
    )(*arrays)


def shards(
    tokens,
    w_query,
    query_gain,
    state_kv,
    neighbours,
    enc_gain,
    enc_query,
    enc_out,
    w_key,
    w_value,
    counts,
    d_context,
):
    gain = query_gain.reshape(32, 1, 256)
    queries, w_part, normed, keys, values, inverse = forward(
        tokens, w_query, gain, state_kv, neighbours.reshape(KEYS, E), enc_gain,
        enc_query, enc_out, w_key, w_value,
    )
    context, d_query_weight, d_hidden, d_encoded, row_dots = backward(
        counts, queries, keys, values, d_context, w_key, w_value, normed, w_part, tokens, inverse,
        gain,
    )
    context, d_query_weight, d_hidden, d_encoded, row_dots = results(
        context, d_query_weight, d_hidden, d_encoded, row_dots
    )
    return (
        context,
        d_hidden,
        d_query_weight,
        d_encoded.reshape(1, 1, NBR, RLEN, E),
        row_dots[0],
    )


def solution(mesh):
    return jax.shard_map(
        shards,
        mesh=mesh,
        in_specs=(
            P(("section", "seq"), None),
            P(("section", "seq"), "tensor"),
            P(),
            P("tensor", None),
            P("section", ("seq", "tensor"), None, None, None),
            P(),
            P(),
            P(),
            P(None, "tensor"),
            P(None, "tensor"),
            P(("section", "seq")),
            P(("section", "seq"), "tensor"),
        ),
        out_specs=(
            P(("section", "seq"), "tensor"),
            P(("section", "seq"), "tensor"),
            P(("section", "seq"), "tensor"),
            P("section", ("seq", "tensor"), None, None, None),
            P(("section", "seq")),
        ),
        check_vma=False,
    )
```

```python
import functools
import math

import jax
import jax.numpy as jnp
from jax import lax
from jax.experimental import pallas as pl
from jax.experimental.pallas import tpu as pltpu
from jax.sharding import PartitionSpec as P

HD = 128
E = 896
EHD = 64
BLOCK = 64
NBR = 2
RLEN = 128
KEYS = NBR * RLEN

EPSILON = 1e-05
NEG_LARGE = -1e30
MESH = pl.DeviceIdType.MESH
F32 = jnp.float32
BF16 = jnp.bfloat16
LAST = (((1,), (1,)), ((), ()))
FIRST = (((0,), (0,)), ((), ()))


def dot(a, b, dims=(((1,), (0,)), ((), ()))):
    return lax.dot_general(a, b, dims, preferred_element_type=F32)


class Place:
    def __init__(self):
        self.section = lax.axis_index("section")
        seq = lax.axis_index("seq")
        self.x = lax.axis_index("tensor")
        self.core = seq % 2
        self.y = seq // 4
        self.z = 2 * ((seq // 2) % 2) + self.section

    def along(self, dim, off):
        if dim == "x":
            return (self.section, self.seq_of(self.y, self.z), (self.x + off) % 4)
        if dim == "y":
            return (self.section, self.seq_of((self.y + off) % 4, self.z), self.x)
        z = (self.z + off) % 4
        return (z % 2, self.seq_of(self.y, z), self.x)

    def seq_of(self, y, z):
        return y * 4 + (z // 2) * 2 + self.core

    def sibling(self):
        return (self.section, self.y * 4 + (self.z // 2) * 2 + 1 - self.core, self.x)

    def partner(self):
        return (1 - self.section, self.seq_of(self.y, self.z), self.x)

    def chunk(self, dy, dz):
        y, z = (self.y + dy) % 4, (self.z + dz) % 4
        return (z % 2) * 8 + y * 2 + z // 2


def greet(devices):
    barrier = pltpu.get_barrier_semaphore()
    for device in devices:
        pl.semaphore_signal(barrier, inc=1, device_id=device, device_id_type=MESH)
    pl.semaphore_wait(barrier, len(devices))


class Sender:
    def __init__(self, send_sem, recv_sem):
        self.send_sem, self.recv_sem, self.copies = send_sem, recv_sem, []

    def __call__(self, src, dst, device):
        index = len(self.copies)
        copy = pltpu.make_async_remote_copy(
            src_ref=src, dst_ref=dst, send_sem=self.send_sem.at[index],
            recv_sem=self.recv_sem.at[index], device_id=device, device_id_type=MESH,
        )
        copy.start()
        self.copies.append(copy)
        return copy


Y_FIRST = 96
CHUNK = 256


def wide(column):
    return jnp.concatenate([column, column], axis=1)


def forward_kernel(
    tokens_ref, w_ref, gain_ref, state_ref, near_ref, egain_ref, equery_ref, eout_ref, wk_ref, wv_ref,
    q_ref, w_out, nrm_out, k_out, v_out, inv_ref,
    tok, wc, nrm, theirs, skv, unit, acc, q_send, q_in,
    sp, sr1, sr2, enc_in, eq_s, ectx, escore, equery, eout, enc, wk, wv, ks, vs,
    load_sem, out_sem, send_sem, recv_sem,
):
    at = Place()
    share = tok.shape[1] // 4
    send = Sender(send_sem, recv_sem)
    me = at.chunk(0, 0)
    pairs = (
        (w_ref, wc.at[me]), (tokens_ref, tok), (state_ref, skv), (equery_ref, equery),
        (eout_ref, eout), (wk_ref, wk), (wv_ref, wv),
    )
    loads = [pltpu.make_async_copy(src, dst, load_sem.at[i]) for i, (src, dst) in enumerate(pairs)]
    for load in loads:
        load.start()
    greet(
        [at.along("x", 1), at.along("x", 3), at.along("y", 1), at.along("y", 3),
         at.along("z", 1), at.along("z", 3), at.sibling()]
    )

    dims = (("y", "z"), ("z", "y"))
    spans = ((0, Y_FIRST), (Y_FIRST, CHUNK))

    def piece(half, first, second, part=None):
        dy, dz = (first, second) if half == 0 else (second, first)
        low, high = spans[half]
        middle = (low + high) // 2
        low, high = (low, high) if part is None else ((low, middle), (middle, high))[part]
        return wc.at[at.chunk(dy, dz), low:high]

    def pass_on(ref, dim, off):
        return send(ref, ref, at.along(dim, off))

    near, relay, cross, last = {}, {}, {}, {}

    def across(half, line):
        dim = dims[half][1]
        block = piece(half, line, 0)
        cross[half, line] = (pass_on(block, dim, 1), pass_on(block, dim, 3))

    def relays(half):
        dim = dims[half][0]
        near[half][0].wait_recv()
        first = pass_on(piece(half, 3, 0, 0), dim, 1)
        near[half][1].wait_recv()
        relay[half] = (first, pass_on(piece(half, 1, 0, 1), dim, 3))

    def relayed(half):
        relay[half][0].wait_recv()
        relay[half][1].wait_recv()
        across(half, 2)

    def crossed(half, line):
        dim = dims[half][1]
        cross[half, line][0].wait_recv()
        first = pass_on(piece(half, line, 3, 0), dim, 1)
        cross[half, line][1].wait_recv()
        last[half, line] = (first, pass_on(piece(half, line, 1, 1), dim, 3))

    def landed(half, line):
        last[half, line][0].wait_recv()
        last[half, line][1].wait_recv()

    outs = []

    def write(src, dst):
        copy = pltpu.make_async_copy(src, dst, out_sem.at[len(outs)])
        copy.start()
        outs.append(copy)

    def accumulate(offsets, begin=False):
        chunks = [at.chunk(dy, dz) for dy, dz in offsets]
        for k in chunks:
            write(wc.at[k], w_out.at[k])

        @pl.loop(0, 4)
        def _(i):
            rows = pl.ds(pl.multiple_of((i // 2) * 256, 256), 256)
            cols = pl.ds(pl.multiple_of((i % 2) * 512, 512), 512)
            total = dot(nrm[chunks[0], rows, :], wc[chunks[0], :, cols])
            for k in chunks[1:]:
                total = total + dot(nrm[k, rows, :], wc[k, :, cols])
            acc[rows, cols] = total if begin else acc[rows, cols] + total

    loads[0].wait()
    for half in (0, 1):
        block = piece(half, 0, 0)
        near[half] = (pass_on(block, dims[half][0], 1), pass_on(block, dims[half][0], 3))
    c_near = send(near_ref, enc_in, at.partner())
    across(1, 0)

    loads[1].wait()

    @pl.loop(0, 16)
    def _(i):
        rows = pl.ds(pl.multiple_of(i * 16, 16), 16)
        values = tok[rows, :].astype(F32)
        square = jnp.sum(values * values, axis=-1, keepdims=True)
        inverse = lax.rsqrt(square * (1.0 / tok.shape[1]) + EPSILON)
        inv_ref[rows, :] = jnp.broadcast_to(inverse, (16, 128))

    @pl.loop(0, 8)
    def _(i):
        source = pl.ds(pl.multiple_of(at.x * share + i * 256, 256), 256)
        target = pl.ds(pl.multiple_of(i * 256, 256), 256)
        unit[:, target] = (tok[:, source].astype(F32) * wide(inv_ref[...])).astype(BF16)

    loads[2].wait()

    @pl.loop(0, 7)
    def _(i):
        cols = pl.ds(pl.multiple_of(i * 256, 256), 256)
        part = dot(unit[...], skv[:, cols]).astype(BF16)
        for j in range(4):
            sp[j, :, cols] = part[64 * j : 64 * j + 64]

    far, up, down = (at.x + 2) % 4, (at.x + 1) % 4, (at.x + 3) % 4
    c_s1 = (
        send(sp.at[far, 0:32], sr1.at[0], at.along("x", 1)),
        send(sp.at[far, 32:64], sr1.at[1], at.along("x", 3)),
    )
    relays(0)
    relays(1)
    across(1, 3)
    across(1, 1)
    for line in (0, 3, 1):
        across(0, line)

    @pl.loop(0, 16)
    def _(k):
        def chunk(g):
            cols = pl.ds(pl.multiple_of(g * CHUNK, CHUNK), CHUNK)
            return (tok[:, cols].astype(F32) * wide(inv_ref[...]) * gain_ref[g]).astype(BF16)

        nrm[k, 0:256] = chunk(2 * k + at.core)
        theirs[k] = chunk(2 * k + 1 - at.core)

    c_nrm = send(theirs, nrm.at[:, 256:512], at.sibling())

    for way, block in ((0, up), (1, down)):
        c_s1[way].wait_recv()
        rows = slice(32 * way, 32 * way + 32)
        sp[block, rows] = (sp[block, rows].astype(F32) + sr1[way].astype(F32)).astype(BF16)
    c_s2 = (
        send(sp.at[up], sr2.at[0], at.along("x", 1)),
        send(sp.at[down], sr2.at[1], at.along("x", 3)),
    )
    relayed(0)
    crossed(1, 0)

    loads[3].wait()
    c_near.wait_recv()
    enc_rows = enc_in[...].astype(F32)
    mean = jnp.sum(enc_rows * enc_rows, axis=-1, keepdims=True) * (1.0 / E)
    enc_normed = (enc_rows * lax.rsqrt(mean + EPSILON) * egain_ref[...].reshape(1, E)).astype(BF16)
    eq_s[...] = dot(enc_normed, equery[...]).astype(BF16)

    c_s2[0].wait_recv()
    c_s2[1].wait_recv()
    states = (sp[at.x].astype(F32) + sr2[0].astype(F32) + sr2[1].astype(F32)).astype(BF16)
    states = states.astype(F32)
    left = lax.broadcasted_iota(jnp.int32, (BLOCK, 128), 1) < EHD
    left_wide = lax.broadcasted_iota(jnp.int32, (KEYS, 128), 1) < EHD

    def doubled(cols):
        both = states[:, cols]
        return jnp.concatenate(
            [jnp.where(left, both, 0.0), jnp.where(left, 0.0, both)], axis=0
        ).astype(BF16)

    for j in range(7):
        keys = doubled(slice(128 * j, 128 * j + 128))
        escore[j] = dot(eq_s[:, 128 * j : 128 * j + 128], keys, LAST) * (1.0 / math.sqrt(EHD))
    for j in range(7):
        scores = escore[j]
        top_left = jnp.max(jnp.where(left_wide, scores, NEG_LARGE), axis=-1, keepdims=True)
        top_right = jnp.max(jnp.where(left_wide, NEG_LARGE, scores), axis=-1, keepdims=True)
        weights = jnp.exp(scores - jnp.where(left_wide, top_left, top_right))
        sum_left = jnp.sum(jnp.where(left_wide, weights, 0.0), axis=-1, keepdims=True)
        sum_right = jnp.sum(jnp.where(left_wide, 0.0, weights), axis=-1, keepdims=True)
        escore[j] = weights / jnp.where(left_wide, sum_left, sum_right)
    for j in range(7):
        values = doubled(slice(E + 128 * j, E + 128 * j + 128))
        ectx[:, 128 * j : 128 * j + 128] = dot(escore[j].astype(BF16), values).astype(BF16)
    loads[4].wait()
    enc[at.x] = (enc_in[...].astype(F32) + dot(ectx[...], eout[...])).astype(BF16)
    c_e1 = (
        send(enc.at[at.x], enc.at[at.x], at.along("x", 1)),
        send(enc.at[at.x], enc.at[at.x], at.along("x", 3)),
    )
    relayed(1)
    loads[5].wait()
    loads[6].wait()

    def project(block):
        @pl.loop(0, 4)
        def _(i):
            cols = pl.ds(pl.multiple_of(i * 256, 256), 256)
            ks[block, :, cols] = dot(enc[block], wk[:, cols]).astype(BF16)
            vs[block, :, cols] = dot(enc[block], wv[:, cols]).astype(BF16)

        write(ks.at[block], k_out.at[block])
        write(vs.at[block], v_out.at[block])

    c_nrm.wait_recv()
    write(nrm, nrm_out)
    crossed(0, 0)
    accumulate([(0, 0), (1, 0), (3, 0), (0, 1), (0, 3)], begin=True)
    crossed(1, 3)
    crossed(1, 1)
    project(at.x)
    crossed(0, 3)
    crossed(0, 1)
    c_e1[0].wait_recv()
    c_e2 = [send(enc.at[down, 0:128], enc.at[down, 0:128], at.along("x", 1))]
    c_e1[1].wait_recv()
    c_e2.append(send(enc.at[up, 128:256], enc.at[up, 128:256], at.along("x", 3)))
    project(down)
    project(up)
    accumulate([(1, 1), (1, 3), (3, 1), (3, 3)])
    crossed(1, 2)
    crossed(0, 2)
    landed(0, 0)
    landed(1, 0)
    accumulate([(2, 0), (0, 2)])
    c_e2[0].wait_recv()
    c_e2[1].wait_recv()
    project(far)
    for line in (3, 1):
        landed(0, line)
        landed(1, line)
    accumulate([(2, 1), (2, 3), (1, 2), (3, 2)])
    landed(0, 2)
    landed(1, 2)
    final = at.chunk(2, 2)
    write(wc.at[final], w_out.at[final])
    c_q = []
    parts = (slice(0, 512), slice(512, 1024))
    for cols in parts:
        total = acc[256:512, cols] + dot(nrm[final, 256:512], wc[final, :, cols])
        q_send[:, cols] = total.astype(BF16)
        c_q.append(send(q_send.at[:, cols], q_in.at[:, cols], at.sibling()))
    for cols in parts:
        acc[0:256, cols] = acc[0:256, cols] + dot(nrm[final, 0:256], wc[final, :, cols])
    for cols, copy in zip(parts, c_q):
        copy.wait_recv()
        q_ref[:, cols] = (acc[0:256, cols] + q_in[:, cols].astype(F32)).astype(BF16)
    for copy in send.copies:
        copy.wait_send()
    for copy in outs:
        copy.wait()


FORWARD_SENDS = 4 + 1 + 4 + 2 * 6 + 2 * 2 + 16 + 2 + 2 + 1 + 2 + 2 + 2


def forward(tokens, w_query, gain, state_kv, near, enc_gain, enc_query, enc_out, w_key, w_value):
    rows, full = tokens.shape
    width = w_query.shape[1]
    vmem = pl.BlockSpec(memory_space=pltpu.VMEM)
    anywhere = pl.BlockSpec(memory_space=pl.ANY)

    def buffer(*shape, kind=BF16):
        return pltpu.VMEM(shape, kind)

    return pl.pallas_call(
        forward_kernel,
        in_specs=[anywhere, anywhere, vmem, anywhere, anywhere, vmem] + [anywhere] * 4,
        out_specs=[vmem] + [anywhere] * 4 + [vmem],
        out_shape=[
            jax.ShapeDtypeStruct((rows, width), BF16),
            jax.ShapeDtypeStruct((16, CHUNK, width), BF16),
            jax.ShapeDtypeStruct((16, 2 * rows, CHUNK), BF16),
            jax.ShapeDtypeStruct((4, KEYS, width), BF16),
            jax.ShapeDtypeStruct((4, KEYS, width), BF16),
            jax.ShapeDtypeStruct((rows, 128), F32),
        ],
        scratch_shapes=[
            buffer(rows, full),
            buffer(16, CHUNK, width),
            buffer(16, 2 * rows, CHUNK),
            buffer(16, rows, CHUNK),
            buffer(full // 4, 2 * E),
            buffer(rows, full // 4),
            buffer(2 * rows, width, kind=F32),
            buffer(rows, width),
            buffer(rows, width),
            buffer(4, BLOCK, 2 * E),
            buffer(2, BLOCK // 2, 2 * E),
            buffer(2, BLOCK, 2 * E),
            buffer(KEYS, E),
            buffer(KEYS, E),
            buffer(KEYS, E),
            buffer(7, KEYS, 128, kind=F32),
            buffer(E, E),
            buffer(E, E),
            buffer(4, KEYS, E),
            buffer(E, width),
            buffer(E, width),
            buffer(4, KEYS, width),
            buffer(4, KEYS, width),
            pltpu.SemaphoreType.DMA((7,)),
            pltpu.SemaphoreType.DMA((25,)),
            pltpu.SemaphoreType.DMA((FORWARD_SENDS,)),
            pltpu.SemaphoreType.DMA((FORWARD_SENDS,)),
        ],
        compiler_params=pltpu.CompilerParams(
            collective_id=2, has_side_effects=True, vmem_limit_bytes=60 * 2**20
        ),
        cost_estimate=pl.CostEstimate(
            flops=2 * 5400 * 2**20, bytes_accessed=40 * 2**20, transcendentals=0
        ),
    )(tokens, w_query, gain, state_kv, near, enc_gain, enc_query, enc_out, w_key, w_value)


LINES = (2, 1, 3, 0)
GROUPS = ((0, 384, 160), (384, 1024, 224))
LOADS = 20


def halves(group):
    first, stop, z_first = GROUPS[group]
    return z_first, stop - first - z_first


def backward_kernel(
    counts, q_ref, k_ref, v_ref, do_ref, wk_ref, wv_ref, nrm_ref, w_ref, tokens_ref,
    inverse_ref, gain_ref,
    ctx_ref, dw_ref, dh_ref, de_ref, dots_ref,
    qs, dos, ks, vs, wk, wv, ctx, score_s, dprob_s, weight_s, dscore_s, sum_s,
    dq2, dq_t, nrm, wc, prod, dw_t, dw_s, part, rn1, rn2, out_sib, in_sib,
    grads, g1, gs, g2, gfin, gin, sums, sums_in, tok, column,
    ra1_00, ra1_01, ra1_10, ra1_11, ra2_00, ra2_01, ra2_10, ra2_11,
    rb1_00, rb1_01, rb1_10, rb1_11, rb2_00, rb2_01, rb2_10, rb2_11,
    load_sem, out_sem, send_sem, recv_sem,
):
    at = Place()
    width = tokens_ref.shape[1]
    share = width // 4
    ra1 = ((ra1_00, ra1_01), (ra1_10, ra1_11))
    ra2 = ((ra2_00, ra2_01), (ra2_10, ra2_11))
    rb1 = ((rb1_00, rb1_01), (rb1_10, rb1_11))
    rb2 = ((rb2_00, rb2_01), (rb2_10, rb2_11))
    pairs = []
    for first, stop, _ in GROUPS:
        cols = slice(first, stop)
        pairs += [(source.at[:, cols], target.at[:, cols]) for source, target in ((q_ref, qs), (do_ref, dos))]
        pairs += [(source.at[:, :, cols], target.at[:, :, cols]) for source, target in ((k_ref, ks), (v_ref, vs))]
    pairs += [(wk_ref, wk), (wv_ref, wv), (nrm_ref, nrm), (w_ref, wc)]
    for i in range(8):
        first = pl.multiple_of(at.x * share + i * 256, 256)
        pairs.append((tokens_ref.at[:, pl.ds(first, 256)], tok.at[i]))
    loads = [pltpu.make_async_copy(src, dst, load_sem.at[i]) for i, (src, dst) in enumerate(pairs)]
    for load in loads[:4]:
        load.start()
    barrier = pltpu.get_barrier_semaphore()
    friends = [at.along("x", 1), at.along("x", 2), at.along("x", 3), at.along("y", 1),
               at.along("y", 3), at.along("z", 1), at.along("z", 3), at.sibling()]
    for friend in friends:
        pl.semaphore_signal(barrier, inc=1, device_id=friend, device_id_type=MESH)

    send = Sender(send_sem, recv_sem)
    far, up, down = (at.x + 2) % 4, (at.x + 1) % 4, (at.x + 3) % 4
    scale = 1.0 / math.sqrt(HD)

    def added(dst, first, second):
        dst[...] = (first[...].astype(F32) + second[...].astype(F32)).astype(BF16)

    def both(dim, one, other):
        return send(*one, at.along(dim, 1)), send(*other, at.along(dim, 3))

    def attention(b, group):
        first, stop, _ = GROUPS[group]
        spans = [slice(low, low + HD) for low in range(first, stop, HD)]
        rows = pl.ds(pl.multiple_of(b * BLOCK, BLOCK), BLOCK)
        count = counts[b]
        valid = lax.broadcasted_iota(jnp.int32, (BLOCK, KEYS), 1) < count * RLEN
        empty = jnp.where(count == 0, 1.0, 0.0).astype(F32)
        for i, cols in enumerate(spans):
            score_s[i] = dot(qs[rows, cols], ks[b, :, cols], LAST) * scale
            dprob_s[i] = dot(dos[rows, cols], vs[b, :, cols], LAST)
        for i in range(len(spans)):
            scores = score_s[i]
            top = jnp.max(jnp.where(valid, scores, NEG_LARGE), axis=-1, keepdims=True)
            weights = jnp.where(valid, jnp.exp(scores - top), 0.0)
            probs = weights / (jnp.sum(weights, axis=-1, keepdims=True) + empty)
            weight_s[i] = probs.astype(BF16)
            d_probs = dprob_s[i]
            inner = jnp.sum(probs * d_probs, axis=-1, keepdims=True)
            dscore_s[i] = (probs * (d_probs - inner) * scale).astype(BF16)
        total = jnp.zeros((BLOCK, HD), F32)
        for i, cols in enumerate(spans):
            ctx[rows, cols] = dot(weight_s[i], vs[b, :, cols]).astype(BF16)
            dq = dot(dscore_s[i], ks[b, :, cols])
            dq2[rows, cols] = dq.astype(BF16)
            total = total + dq * qs[rows, cols].astype(F32)
            vs[b, :, cols] = dot(weight_s[i], dos[rows, cols], FIRST).astype(BF16)
            ks[b, :, cols] = dot(dscore_s[i], qs[rows, cols], FIRST).astype(BF16)
        sum_s[rows, :] = total if group == 0 else sum_s[rows, :] + total

    def encoded_grad(b):
        grad = dot(ks[b], wk[...], LAST) + dot(vs[b], wv[...], LAST)
        grads[b] = grad.astype(BF16)

    def share_dq(group):
        first, stop, _ = GROUPS[group]
        return send(dq2.at[0:256, first:stop], dq2.at[256:512, first:stop], at.sibling())

    def transposed(group, rows):
        first, stop, _ = GROUPS[group]
        for low in range(first, stop, 128):
            dq_t[low : low + 128, rows] = jnp.transpose(dq2[rows, low : low + 128])

    def product(group, dy, dz):
        k = at.chunk(dy, dz)
        first, stop, _ = GROUPS[group]
        prod[k, first:stop] = dot(dq_t[first:stop], nrm[k]).astype(BF16)

    dims = (("z", "y"), ("y", "z"))

    def block(group, half, line, off, part=None):
        dy, dz = (line, off) if half == 0 else (off, line)
        first, stop, z_first = GROUPS[group]
        low, high = ((first, first + z_first), (first + z_first, stop))[half]
        middle = (low + high) // 2
        low, high = (low, high) if part is None else ((low, middle), (middle, high))[part]
        return prod.at[at.chunk(dy, dz), low:high]

    c1, c2, d1, d2 = {}, {}, {}, {}

    def first_hop(group, half, line):
        slot = ra1[group][half].at[LINES.index(line)]
        c1[group, half, line] = both(
            dims[half][0],
            (block(group, half, line, 2, 0), slot.at[0]),
            (block(group, half, line, 2, 1), slot.at[1]),
        )

    def second_hop(group, half, line):
        for way, off in ((0, 1), (1, 3)):
            c1[group, half, line][way].wait_recv()
            piece = block(group, half, line, off, way)
            added(piece, piece, ra1[group][half].at[LINES.index(line), way])
        slot = ra2[group][half].at[LINES.index(line)]
        c2[group, half, line] = both(
            dims[half][0],
            (block(group, half, line, 1), slot.at[0]),
            (block(group, half, line, 3), slot.at[1]),
        )

    def gathered(group, half, line):
        for way in (0, 1):
            c2[group, half, line][way].wait_recv()
        slot = ra2[group][half].at[LINES.index(line)]
        piece = block(group, half, line, 0)
        total = piece[...].astype(F32) + slot[0].astype(F32) + slot[1].astype(F32)
        piece[...] = total.astype(BF16)

    def turn(group, half):
        d1[group, half] = both(
            dims[half][1],
            (block(group, half, 2, 0, 0), rb1[group][half].at[0]),
            (block(group, half, 2, 0, 1), rb1[group][half].at[1]),
        )

    def turned(group, half):
        for way, off in ((0, 1), (1, 3)):
            d1[group, half][way].wait_recv()
            piece = block(group, half, off, 0, way)
            added(piece, piece, rb1[group][half].at[way])
        d2[group, half] = both(
            dims[half][1],
            (block(group, half, 1, 0), rb2[group][half].at[0]),
            (block(group, half, 3, 0), rb2[group][half].at[1]),
        )

    def result(group):
        first, stop, _ = GROUPS[group]
        sizes = halves(group)
        for half in (0, 1):
            for way in (0, 1):
                c2[group, half, 0][way].wait_recv()
                d2[group, half][way].wait_recv()
            own = block(group, half, 0, 0)
            slot = ra2[group][half].at[LINES.index(0)]
            total = own[...].astype(F32) + slot[0].astype(F32) + slot[1].astype(F32)
            low = half * sizes[0]
            dw_t[low : low + sizes[half]] = (
                total + rb2[group][half][0].astype(F32) + rb2[group][half][1].astype(F32)
            )
        for low in range(0, stop - first, 128):
            dw_s[:, first + low : first + low + 128] = jnp.transpose(dw_t[low : low + 128])
        write(dw_s.at[:, first:stop], dw_ref.at[:, first:stop])

    def partial(k):
        part[k] = dot(dq2[...], wc[k], LAST).astype(BF16)

    n1, n2 = [], []

    def far_partial(m):
        partial(far * 4 + m)
        n1.append(
            both("x", (part.at[far * 4 + m, 0:256], rn1.at[m, 0]),
                 (part.at[far * 4 + m, 256:512], rn1.at[m, 1]))
        )

    def summed_partial(m):
        partial(up * 4 + m)
        partial(down * 4 + m)
        n1[m][0].wait_recv()
        piece = part.at[up * 4 + m, 0:256]
        added(piece, piece, rn1.at[m, 0])
        n1[m][1].wait_recv()
        piece = part.at[down * 4 + m, 256:512]
        added(piece, piece, rn1.at[m, 1])
        n2.append(
            both("x", (part.at[up * 4 + m], rn2.at[m, 0]), (part.at[down * 4 + m], rn2.at[m, 1]))
        )

    outs = []

    def write(src, dst):
        copy = pltpu.make_async_copy(src, dst, out_sem.at[len(outs)])
        copy.start()
        outs.append(copy)

    def finish(i, d_normed):
        inverse = wide(inverse_ref[...])
        unit = tok[i].astype(F32) * inverse
        parts = d_normed * gain_ref[at.x * 8 + i]
        result = inverse * (parts - unit * (wide(column[...]) * (1.0 / width)))
        tok[i] = result.astype(BF16)
        first = pl.multiple_of(i * 256, 256)
        write(tok.at[i], dh_ref.at[:, pl.ds(first, 256)])

    c_sib = []

    def normed_sum(m):
        for copy in n2[m]:
            copy.wait_recv()

        def summed(low):
            rows = slice(low, low + 256)
            total = part[at.x * 4 + m, rows].astype(F32) + rn2[m, 0, rows].astype(F32)
            return total + rn2[m, 1, rows].astype(F32)

        out_sib[m] = summed(256).astype(BF16)
        c_sib.append(send(out_sib.at[m], in_sib.at[m], at.sibling()))
        finish(2 * m + at.core, summed(0))

    def sibling_part(m):
        c_sib[m].wait_recv()
        finish(2 * m + 1 - at.core, in_sib[m].astype(F32))

    for load in loads[:4]:
        load.wait()
    for load in loads[4:]:
        load.start()

    @pl.loop(0, 4)
    def _(b):
        attention(b, 0)

    pl.semaphore_wait(barrier, len(friends))
    c_dq = [share_dq(0)]
    own, other = slice(0, 256), slice(256, 512)
    transposed(0, own)
    for load in loads[4:12]:
        load.wait()
    attention(far, 1)
    encoded_grad(far)
    c_g1 = both("x", (grads.at[far, 0:128], g1.at[0]), (grads.at[far, 128:256], g1.at[1]))
    c_dq[0].wait_recv()
    transposed(0, other)
    product(0, 2, 2)
    first_hop(0, 1, 2)
    first_hop(0, 0, 2)

    def leading(line):
        product(0, 2, line)
        first_hop(0, 1, line)
        product(0, line, 2)
        first_hop(0, 0, line)

    leading(1)
    attention(up, 1)
    attention(down, 1)
    encoded_grad(up)
    encoded_grad(down)
    c_g1[0].wait_recv()
    c_g1[1].wait_recv()
    gs[0, 0:128] = (grads[up, 0:128].astype(F32) + g1[0].astype(F32)).astype(BF16)
    gs[0, 128:256] = grads[up, 128:256]
    gs[1, 0:128] = grads[down, 0:128]
    gs[1, 128:256] = (grads[down, 128:256].astype(F32) + g1[1].astype(F32)).astype(BF16)
    c_g2 = both("x", (gs.at[0], g2.at[0]), (gs.at[1], g2.at[1]))
    leading(3)
    leading(0)
    second_hop(0, 1, 2)
    second_hop(0, 0, 2)
    attention(at.x, 1)
    c_dq.append(share_dq(1))
    write(ctx, ctx_ref)
    corners = ((1, 1), (3, 1), (1, 3), (3, 3))
    rest = ((1, 0), (3, 0), (0, 1), (0, 3), (0, 0))
    for dy, dz in corners:
        product(0, dy, dz)
    for line in (1, 3):
        second_hop(0, 1, line)
        second_hop(0, 0, line)
    for half in (0, 1):
        gathered(0, half, 2)
        turn(0, half)
    lanes = jnp.sum(jnp.transpose(sum_s[...]), axis=0, keepdims=True)
    sums[...] = jnp.broadcast_to(lanes, (8, 256))
    c_sums = [send(sums, sums_in.at[i], at.along("x", i + 1)) for i in range(3)]
    transposed(1, own)
    c_dq[1].wait_recv()
    transposed(1, other)
    product(1, 2, 2)
    first_hop(1, 1, 2)
    first_hop(1, 0, 2)
    for m, line in enumerate((1, 3, 0)):
        product(1, 2, line)
        first_hop(1, 1, line)
        product(1, line, 2)
        first_hop(1, 0, line)
        far_partial(m)
    far_partial(3)
    for dy, dz in rest:
        product(0, dy, dz)
    for half in (0, 1):
        gathered(0, half, 1)
        gathered(0, half, 3)
        turned(0, half)
    second_hop(1, 0, 2)
    second_hop(1, 1, 2)
    for dy, dz in corners:
        product(1, dy, dz)
    for line in (1, 3):
        second_hop(1, 0, line)
        second_hop(1, 1, line)
    summed_partial(0)
    encoded_grad(at.x)
    for copy in c_g2:
        copy.wait_recv()
    gfin[...] = (grads[at.x].astype(F32) + g2[0].astype(F32) + g2[1].astype(F32)).astype(BF16)
    c_swap = send(gfin, gin, at.partner())
    for m in range(1, 4):
        summed_partial(m)
    for dy, dz in rest:
        product(1, dy, dz)
    gathered(1, 0, 2)
    turn(1, 0)
    gathered(1, 1, 2)
    turn(1, 1)
    second_hop(0, 0, 0)
    second_hop(0, 1, 0)

    for copy in c_sums:
        copy.wait_recv()
    whole = sums[...] + sums_in[0] + sums_in[1] + sums_in[2]
    dots_ref[...] = whole[0:1] * (1.0 / math.sqrt(width))
    column[...] = jnp.transpose(jnp.broadcast_to(whole[0:1], (128, 256)))
    for load in loads[12:]:
        load.wait()
    for m in range(4):
        partial(at.x * 4 + m)
    normed_sum(0)
    gathered(1, 0, 1)
    gathered(1, 0, 3)
    turned(1, 0)
    second_hop(1, 1, 0)
    gathered(1, 1, 1)
    gathered(1, 1, 3)
    turned(1, 1)
    second_hop(1, 0, 0)
    normed_sum(1)
    sibling_part(0)
    normed_sum(2)
    sibling_part(1)
    result(0)
    c_swap.wait_recv()
    write(gin, de_ref)
    sibling_part(2)
    normed_sum(3)
    result(1)
    sibling_part(3)
    for copy in send.copies:
        copy.wait_send()
    for copy in outs:
        copy.wait()


BACKWARD_SENDS = 2 + 2 + 2 + 8 + 8 + 3 + 1 + 4 + 2 * 40


def backward(
    counts, queries, keys, values, d_context, w_key, w_value, normed, w_all, tokens, inverse, gain
):
    rows, width = queries.shape
    full = tokens.shape[1]
    vmem = pl.BlockSpec(memory_space=pltpu.VMEM)
    anywhere = pl.BlockSpec(memory_space=pl.ANY)

    def buffer(*shape, kind=BF16):
        return pltpu.VMEM(shape, kind)

    sizes = [size for group in range(2) for size in halves(group)]
    return pl.pallas_call(
        backward_kernel,
        in_specs=[pl.BlockSpec(memory_space=pltpu.SMEM)] + [anywhere] * 9 + [vmem, vmem],
        out_specs=[anywhere] * 4 + [vmem],
        out_shape=[
            jax.ShapeDtypeStruct((rows, width), BF16),
            jax.ShapeDtypeStruct((256, width), F32),
            jax.ShapeDtypeStruct((rows, full // 4), BF16),
            jax.ShapeDtypeStruct((KEYS, E), BF16),
            jax.ShapeDtypeStruct((1, rows), F32),
        ],
        scratch_shapes=[
            buffer(rows, width),
            buffer(rows, width),
            buffer(4, KEYS, width),
            buffer(4, KEYS, width),
            buffer(E, width),
            buffer(E, width),
            buffer(rows, width),
            buffer(6, BLOCK, KEYS, kind=F32),
            buffer(6, BLOCK, KEYS, kind=F32),
            buffer(6, BLOCK, KEYS),
            buffer(6, BLOCK, KEYS),
            buffer(rows, HD, kind=F32),
            buffer(512, 1024),
            buffer(1024, 512),
            buffer(16, 512, 256),
            buffer(16, 256, 1024),
            buffer(16, 1024, 256),
            buffer(768, 256, kind=F32),
            buffer(256, width, kind=F32),
            buffer(16, 512, 256),
            buffer(4, 2, 256, 256),
            buffer(4, 2, 512, 256),
            buffer(4, 256, 256),
            buffer(4, 256, 256),
            buffer(4, KEYS, E),
            buffer(2, 128, E),
            buffer(2, 256, E),
            buffer(2, 256, E),
            buffer(256, E),
            buffer(256, E),
            buffer(8, 256, kind=F32),
            buffer(3, 8, 256, kind=F32),
            buffer(8, 256, 256),
            buffer(256, 128, kind=F32),
        ]
        + [buffer(4, 2, size // 2, 256) for size in sizes]
        + [buffer(4, 2, size, 256) for size in sizes]
        + [buffer(2, size // 2, 256) for size in sizes]
        + [buffer(2, size, 256) for size in sizes]
        + [
            pltpu.SemaphoreType.DMA((LOADS,)),
            pltpu.SemaphoreType.DMA((12,)),
            pltpu.SemaphoreType.DMA((BACKWARD_SENDS,)),
            pltpu.SemaphoreType.DMA((BACKWARD_SENDS,)),
        ],
        compiler_params=pltpu.CompilerParams(
            collective_id=1, has_side_effects=True, vmem_limit_bytes=62 * 2**20
        ),
        cost_estimate=pl.CostEstimate(
            flops=12 * 2**30, bytes_accessed=30 * 2**20, transcendentals=0
        ),
    )(counts, queries, keys, values, d_context, w_key, w_value, normed, w_all, tokens, inverse, gain)


def results_kernel(*refs):
    count = (len(refs) - 2) // 3
    in_sem, out_sem = refs[-2:]
    coming, going = [], []
    for source, target, held in zip(refs, refs[count:], refs[2 * count : 3 * count]):
        pieces = min(2, source.shape[0])
        rows = source.shape[0] // pieces
        for i in range(pieces):
            piece, index = pl.ds(i * rows, rows), len(coming)
            coming.append(
                pltpu.make_async_copy(source.at[piece], held.at[piece], in_sem.at[index])
            )
            going.append(
                pltpu.make_async_copy(held.at[piece], target.at[piece], out_sem.at[index])
            )
    for copy in coming:
        copy.start()
    for arrived, copy in zip(coming, going):
        arrived.wait()
        copy.start()
    for copy in going:
        copy.wait()


def results(*arrays):
    anywhere = pl.BlockSpec(memory_space=pl.ANY)
    return pl.pallas_call(
        results_kernel,
        in_specs=[anywhere] * len(arrays),
        out_specs=[anywhere] * len(arrays),
        out_shape=[jax.ShapeDtypeStruct(array.shape, array.dtype) for array in arrays],
        scratch_shapes=[pltpu.VMEM(array.shape, array.dtype) for array in arrays]
        + [pltpu.SemaphoreType.DMA((2 * len(arrays),))] * 2,
        compiler_params=pltpu.CompilerParams(vmem_limit_bytes=62 * 2**20),
    )(*arrays)


def shards(
    tokens,
    w_query,
    query_gain,
    state_kv,
    neighbours,
    enc_gain,
    enc_query,
    enc_out,
    w_key,
    w_value,
    counts,
    d_context,
):
    gain = query_gain.reshape(32, 1, 256)
    queries, w_part, normed, keys, values, inverse = forward(
        tokens, w_query, gain, state_kv, neighbours.reshape(KEYS, E), enc_gain,
        enc_query, enc_out, w_key, w_value,
    )
    context, d_query_weight, d_hidden, d_encoded, row_dots = backward(
        counts, queries, keys, values, d_context, w_key, w_value, normed, w_part, tokens, inverse,
        gain,
    )
    context, d_query_weight, d_hidden, d_encoded, row_dots = results(
        context, d_query_weight, d_hidden, d_encoded, row_dots
    )
    return (
        context,
        d_hidden,
        d_query_weight,
        d_encoded.reshape(1, 1, NBR, RLEN, E),
        row_dots[0],
    )


def solution(mesh):
    return jax.shard_map(
        shards,
        mesh=mesh,
        in_specs=(
            P(("section", "seq"), None),
            P(("section", "seq"), "tensor"),
            P(),
            P("tensor", None),
            P("section", ("seq", "tensor"), None, None, None),
            P(),
            P(),
            P(),
            P(None, "tensor"),
            P(None, "tensor"),
            P(("section", "seq")),
            P(("section", "seq"), "tensor"),
        ),
        out_specs=(
            P(("section", "seq"), "tensor"),
            P(("section", "seq"), "tensor"),
            P(("section", "seq"), "tensor"),
            P("section", ("seq", "tensor"), None, None, None),
            P(("section", "seq")),
        ),
        check_vma=False,
    )
```

```python
import functools
import math

import jax
import jax.numpy as jnp
from jax import lax
from jax.experimental import pallas as pl
from jax.experimental.pallas import tpu as pltpu
from jax.sharding import PartitionSpec as P

HD = 128
E = 896
EHD = 64
BLOCK = 64
NBR = 2
RLEN = 128
KEYS = NBR * RLEN

EPSILON = 1e-05
NEG_LARGE = -1e30
MESH = pl.DeviceIdType.MESH
F32 = jnp.float32
BF16 = jnp.bfloat16
LAST = (((1,), (1,)), ((), ()))
FIRST = (((0,), (0,)), ((), ()))


def dot(a, b, dims=(((1,), (0,)), ((), ()))):
    return lax.dot_general(a, b, dims, preferred_element_type=F32)


class Place:
    def __init__(self):
        self.section = lax.axis_index("section")
        seq = lax.axis_index("seq")
        self.x = lax.axis_index("tensor")
        self.core = seq % 2
        self.y = seq // 4
        self.z = 2 * ((seq // 2) % 2) + self.section

    def along(self, dim, off):
        if dim == "x":
            return (self.section, self.seq_of(self.y, self.z), (self.x + off) % 4)
        if dim == "y":
            return (self.section, self.seq_of((self.y + off) % 4, self.z), self.x)
        z = (self.z + off) % 4
        return (z % 2, self.seq_of(self.y, z), self.x)

    def seq_of(self, y, z):
        return y * 4 + (z // 2) * 2 + self.core

    def sibling(self):
        return (self.section, self.y * 4 + (self.z // 2) * 2 + 1 - self.core, self.x)

    def partner(self):
        return (1 - self.section, self.seq_of(self.y, self.z), self.x)

    def chunk(self, dy, dz):
        y, z = (self.y + dy) % 4, (self.z + dz) % 4
        return (z % 2) * 8 + y * 2 + z // 2


def greet(devices):
    barrier = pltpu.get_barrier_semaphore()
    for device in devices:
        pl.semaphore_signal(barrier, inc=1, device_id=device, device_id_type=MESH)
    pl.semaphore_wait(barrier, len(devices))


class Sender:
    def __init__(self, send_sem, recv_sem):
        self.send_sem, self.recv_sem, self.copies = send_sem, recv_sem, []

    def __call__(self, src, dst, device):
        index = len(self.copies)
        copy = pltpu.make_async_remote_copy(
            src_ref=src, dst_ref=dst, send_sem=self.send_sem.at[index],
            recv_sem=self.recv_sem.at[index], device_id=device, device_id_type=MESH,
        )
        copy.start()
        self.copies.append(copy)
        return copy


Y_FIRST = 96
CHUNK = 256


def wide(column):
    return jnp.concatenate([column, column], axis=1)


def forward_kernel(
    tokens_ref, w_ref, gain_ref, state_ref, near_ref, egain_ref, equery_ref, eout_ref, wk_ref, wv_ref,
    q_ref, w_out, nrm_out, k_out, v_out, inv_ref,
    tok, wc, nrm, theirs, skv, unit, acc, q_send, q_in,
    sp, sr1, sr2, enc_in, eq_s, ectx, escore, equery, eout, enc, wk, wv, ks, vs,
    load_sem, out_sem, send_sem, recv_sem,
):
    at = Place()
    share = tok.shape[1] // 4
    send = Sender(send_sem, recv_sem)
    me = at.chunk(0, 0)
    pairs = (
        (w_ref, wc.at[me]), (tokens_ref, tok), (state_ref, skv), (equery_ref, equery),
        (eout_ref, eout), (wk_ref, wk), (wv_ref, wv),
    )
    loads = [pltpu.make_async_copy(src, dst, load_sem.at[i]) for i, (src, dst) in enumerate(pairs)]
    for load in loads:
        load.start()
    greet(
        [at.along("x", 1), at.along("x", 3), at.along("y", 1), at.along("y", 3),
         at.along("z", 1), at.along("z", 3), at.sibling()]
    )

    dims = (("y", "z"), ("z", "y"))
    spans = ((0, Y_FIRST), (Y_FIRST, CHUNK))

    def piece(half, first, second, part=None):
        dy, dz = (first, second) if half == 0 else (second, first)
        low, high = spans[half]
        middle = (low + high) // 2
        low, high = (low, high) if part is None else ((low, middle), (middle, high))[part]
        return wc.at[at.chunk(dy, dz), low:high]

    def pass_on(ref, dim, off):
        return send(ref, ref, at.along(dim, off))

    near, relay, cross, last = {}, {}, {}, {}

    def across(half, line):
        dim = dims[half][1]
        block = piece(half, line, 0)
        cross[half, line] = (pass_on(block, dim, 1), pass_on(block, dim, 3))

    def relays(half):
        dim = dims[half][0]
        near[half][0].wait_recv()
        first = pass_on(piece(half, 3, 0, 0), dim, 1)
        near[half][1].wait_recv()
        relay[half] = (first, pass_on(piece(half, 1, 0, 1), dim, 3))

    def relayed(half):
        relay[half][0].wait_recv()
        relay[half][1].wait_recv()
        across(half, 2)

    def crossed(half, line):
        dim = dims[half][1]
        cross[half, line][0].wait_recv()
        first = pass_on(piece(half, line, 3, 0), dim, 1)
        cross[half, line][1].wait_recv()
        last[half, line] = (first, pass_on(piece(half, line, 1, 1), dim, 3))

    def landed(half, line):
        last[half, line][0].wait_recv()
        last[half, line][1].wait_recv()

    outs = []

    def write(src, dst):
        copy = pltpu.make_async_copy(src, dst, out_sem.at[len(outs)])
        copy.start()
        outs.append(copy)

    def accumulate(offsets, begin=False):
        chunks = [at.chunk(dy, dz) for dy, dz in offsets]
        for k in chunks:
            write(wc.at[k], w_out.at[k])

        @pl.loop(0, 4)
        def _(i):
            rows = pl.ds(pl.multiple_of((i // 2) * 256, 256), 256)
            cols = pl.ds(pl.multiple_of((i % 2) * 512, 512), 512)
            total = dot(nrm[chunks[0], rows, :], wc[chunks[0], :, cols])
            for k in chunks[1:]:
                total = total + dot(nrm[k, rows, :], wc[k, :, cols])
            acc[rows, cols] = total if begin else acc[rows, cols] + total

    loads[0].wait()
    for half in (0, 1):
        block = piece(half, 0, 0)
        near[half] = (pass_on(block, dims[half][0], 1), pass_on(block, dims[half][0], 3))
    c_near = send(near_ref, enc_in, at.partner())
    across(1, 0)

    loads[1].wait()

    @pl.loop(0, 16)
    def _(i):
        rows = pl.ds(pl.multiple_of(i * 16, 16), 16)
        values = tok[rows, :].astype(F32)
        square = jnp.sum(values * values, axis=-1, keepdims=True)
        inverse = lax.rsqrt(square * (1.0 / tok.shape[1]) + EPSILON)
        inv_ref[rows, :] = jnp.broadcast_to(inverse, (16, 128))

    @pl.loop(0, 8)
    def _(i):
        source = pl.ds(pl.multiple_of(at.x * share + i * 256, 256), 256)
        target = pl.ds(pl.multiple_of(i * 256, 256), 256)
        unit[:, target] = (tok[:, source].astype(F32) * wide(inv_ref[...])).astype(BF16)

    loads[2].wait()

    @pl.loop(0, 7)
    def _(i):
        cols = pl.ds(pl.multiple_of(i * 256, 256), 256)
        part = dot(unit[...], skv[:, cols]).astype(BF16)
        for j in range(4):
            sp[j, :, cols] = part[64 * j : 64 * j + 64]

    far, up, down = (at.x + 2) % 4, (at.x + 1) % 4, (at.x + 3) % 4
    c_s1 = (
        send(sp.at[far, 0:32], sr1.at[0], at.along("x", 1)),
        send(sp.at[far, 32:64], sr1.at[1], at.along("x", 3)),
    )
    relays(0)
    relays(1)
    across(1, 3)
    across(1, 1)
    for line in (0, 3, 1):
        across(0, line)

    @pl.loop(0, 16)
    def _(k):
        def chunk(g):
            cols = pl.ds(pl.multiple_of(g * CHUNK, CHUNK), CHUNK)
            return (tok[:, cols].astype(F32) * wide(inv_ref[...]) * gain_ref[g]).astype(BF16)

        nrm[k, 0:256] = chunk(2 * k + at.core)
        theirs[k] = chunk(2 * k + 1 - at.core)

    c_nrm = send(theirs, nrm.at[:, 256:512], at.sibling())

    for way, block in ((0, up), (1, down)):
        c_s1[way].wait_recv()
        rows = slice(32 * way, 32 * way + 32)
        sp[block, rows] = (sp[block, rows].astype(F32) + sr1[way].astype(F32)).astype(BF16)
    c_s2 = (
        send(sp.at[up], sr2.at[0], at.along("x", 1)),
        send(sp.at[down], sr2.at[1], at.along("x", 3)),
    )
    relayed(0)
    crossed(1, 0)

    loads[3].wait()
    c_near.wait_recv()
    enc_rows = enc_in[...].astype(F32)
    mean = jnp.sum(enc_rows * enc_rows, axis=-1, keepdims=True) * (1.0 / E)
    enc_normed = (enc_rows * lax.rsqrt(mean + EPSILON) * egain_ref[...].reshape(1, E)).astype(BF16)
    eq_s[...] = dot(enc_normed, equery[...]).astype(BF16)

    c_s2[0].wait_recv()
    c_s2[1].wait_recv()
    states = (sp[at.x].astype(F32) + sr2[0].astype(F32) + sr2[1].astype(F32)).astype(BF16)
    states = states.astype(F32)
    left = lax.broadcasted_iota(jnp.int32, (BLOCK, 128), 1) < EHD
    left_wide = lax.broadcasted_iota(jnp.int32, (KEYS, 128), 1) < EHD

    def doubled(cols):
        both = states[:, cols]
        return jnp.concatenate(
            [jnp.where(left, both, 0.0), jnp.where(left, 0.0, both)], axis=0
        ).astype(BF16)

    for j in range(7):
        keys = doubled(slice(128 * j, 128 * j + 128))
        escore[j] = dot(eq_s[:, 128 * j : 128 * j + 128], keys, LAST) * (1.0 / math.sqrt(EHD))
    for j in range(7):
        scores = escore[j]
        top_left = jnp.max(jnp.where(left_wide, scores, NEG_LARGE), axis=-1, keepdims=True)
        top_right = jnp.max(jnp.where(left_wide, NEG_LARGE, scores), axis=-1, keepdims=True)
        weights = jnp.exp(scores - jnp.where(left_wide, top_left, top_right))
        sum_left = jnp.sum(jnp.where(left_wide, weights, 0.0), axis=-1, keepdims=True)
        sum_right = jnp.sum(jnp.where(left_wide, 0.0, weights), axis=-1, keepdims=True)
        escore[j] = weights / jnp.where(left_wide, sum_left, sum_right)
    for j in range(7):
        values = doubled(slice(E + 128 * j, E + 128 * j + 128))
        ectx[:, 128 * j : 128 * j + 128] = dot(escore[j].astype(BF16), values).astype(BF16)
    loads[4].wait()
    enc[at.x] = (enc_in[...].astype(F32) + dot(ectx[...], eout[...])).astype(BF16)
    c_e1 = (
        send(enc.at[at.x], enc.at[at.x], at.along("x", 1)),
        send(enc.at[at.x], enc.at[at.x], at.along("x", 3)),
    )
    relayed(1)
    loads[5].wait()
    loads[6].wait()

    def project(block):
        @pl.loop(0, 4)
        def _(i):
            cols = pl.ds(pl.multiple_of(i * 256, 256), 256)
            ks[block, :, cols] = dot(enc[block], wk[:, cols]).astype(BF16)
            vs[block, :, cols] = dot(enc[block], wv[:, cols]).astype(BF16)

        write(ks.at[block], k_out.at[block])
        write(vs.at[block], v_out.at[block])

    c_nrm.wait_recv()
    write(nrm, nrm_out)
    crossed(0, 0)
    accumulate([(0, 0), (1, 0), (3, 0), (0, 1), (0, 3)], begin=True)
    crossed(1, 3)
    crossed(1, 1)
    project(at.x)
    crossed(0, 3)
    crossed(0, 1)
    c_e1[0].wait_recv()
    c_e2 = [send(enc.at[down, 0:128], enc.at[down, 0:128], at.along("x", 1))]
    c_e1[1].wait_recv()
    c_e2.append(send(enc.at[up, 128:256], enc.at[up, 128:256], at.along("x", 3)))
    project(down)
    project(up)
    accumulate([(1, 1), (1, 3), (3, 1), (3, 3)])
    crossed(1, 2)
    crossed(0, 2)
    landed(0, 0)
    landed(1, 0)
    accumulate([(2, 0), (0, 2)])
    c_e2[0].wait_recv()
    c_e2[1].wait_recv()
    project(far)
    for line in (3, 1):
        landed(0, line)
        landed(1, line)
    accumulate([(2, 1), (2, 3), (1, 2), (3, 2)])
    landed(0, 2)
    landed(1, 2)
    final = at.chunk(2, 2)
    write(wc.at[final], w_out.at[final])
    c_q = []
    parts = (slice(0, 512), slice(512, 1024))
    for cols in parts:
        total = acc[256:512, cols] + dot(nrm[final, 256:512], wc[final, :, cols])
        q_send[:, cols] = total.astype(BF16)
        c_q.append(send(q_send.at[:, cols], q_in.at[:, cols], at.sibling()))
    for cols in parts:
        acc[0:256, cols] = acc[0:256, cols] + dot(nrm[final, 0:256], wc[final, :, cols])
    for cols, copy in zip(parts, c_q):
        copy.wait_recv()
        q_ref[:, cols] = (acc[0:256, cols] + q_in[:, cols].astype(F32)).astype(BF16)
    for copy in send.copies:
        copy.wait_send()
    for copy in outs:
        copy.wait()


FORWARD_SENDS = 4 + 1 + 4 + 2 * 6 + 2 * 2 + 16 + 2 + 2 + 1 + 2 + 2 + 2


def forward(tokens, w_query, gain, state_kv, near, enc_gain, enc_query, enc_out, w_key, w_value):
    rows, full = tokens.shape
    width = w_query.shape[1]
    vmem = pl.BlockSpec(memory_space=pltpu.VMEM)
    anywhere = pl.BlockSpec(memory_space=pl.ANY)

    def buffer(*shape, kind=BF16):
        return pltpu.VMEM(shape, kind)

    return pl.pallas_call(
        forward_kernel,
        in_specs=[anywhere, anywhere, vmem, anywhere, anywhere, vmem] + [anywhere] * 4,
        out_specs=[vmem] + [anywhere] * 4 + [vmem],
        out_shape=[
            jax.ShapeDtypeStruct((rows, width), BF16),
            jax.ShapeDtypeStruct((16, CHUNK, width), BF16),
            jax.ShapeDtypeStruct((16, 2 * rows, CHUNK), BF16),
            jax.ShapeDtypeStruct((4, KEYS, width), BF16),
            jax.ShapeDtypeStruct((4, KEYS, width), BF16),
            jax.ShapeDtypeStruct((rows, 128), F32),
        ],
        scratch_shapes=[
            buffer(rows, full),
            buffer(16, CHUNK, width),
            buffer(16, 2 * rows, CHUNK),
            buffer(16, rows, CHUNK),
            buffer(full // 4, 2 * E),
            buffer(rows, full // 4),
            buffer(2 * rows, width, kind=F32),
            buffer(rows, width),
            buffer(rows, width),
            buffer(4, BLOCK, 2 * E),
            buffer(2, BLOCK // 2, 2 * E),
            buffer(2, BLOCK, 2 * E),
            buffer(KEYS, E),
            buffer(KEYS, E),
            buffer(KEYS, E),
            buffer(7, KEYS, 128, kind=F32),
            buffer(E, E),
            buffer(E, E),
            buffer(4, KEYS, E),
            buffer(E, width),
            buffer(E, width),
            buffer(4, KEYS, width),
            buffer(4, KEYS, width),
            pltpu.SemaphoreType.DMA((7,)),
            pltpu.SemaphoreType.DMA((25,)),
            pltpu.SemaphoreType.DMA((FORWARD_SENDS,)),
            pltpu.SemaphoreType.DMA((FORWARD_SENDS,)),
        ],
        compiler_params=pltpu.CompilerParams(
            collective_id=2, has_side_effects=True, vmem_limit_bytes=60 * 2**20
        ),
        cost_estimate=pl.CostEstimate(
            flops=2 * 5400 * 2**20, bytes_accessed=40 * 2**20, transcendentals=0
        ),
    )(tokens, w_query, gain, state_kv, near, enc_gain, enc_query, enc_out, w_key, w_value)


LINES = (2, 1, 3, 0)
GROUPS = ((0, 384, 192), (384, 1024, 224))
LOADS = 20


def halves(group):
    first, stop, z_first = GROUPS[group]
    return z_first, stop - first - z_first


def backward_kernel(
    counts, q_ref, k_ref, v_ref, do_ref, wk_ref, wv_ref, nrm_ref, w_ref, tokens_ref,
    inverse_ref, gain_ref,
    ctx_ref, dw_ref, dh_ref, de_ref, dots_ref,
    qs, dos, ks, vs, wk, wv, ctx, score_s, dprob_s, weight_s, dscore_s, sum_s,
    dq2, dq_t, nrm, wc, prod, dw_t, dw_s, part, rn1, rn2, out_sib, in_sib,
    grads, g1, gs, g2, gfin, gin, sums, sums_in, tok, column,
    ra1_00, ra1_01, ra1_10, ra1_11, ra2_00, ra2_01, ra2_10, ra2_11,
    rb1_00, rb1_01, rb1_10, rb1_11, rb2_00, rb2_01, rb2_10, rb2_11,
    load_sem, out_sem, send_sem, recv_sem,
):
    at = Place()
    width = tokens_ref.shape[1]
    share = width // 4
    ra1 = ((ra1_00, ra1_01), (ra1_10, ra1_11))
    ra2 = ((ra2_00, ra2_01), (ra2_10, ra2_11))
    rb1 = ((rb1_00, rb1_01), (rb1_10, rb1_11))
    rb2 = ((rb2_00, rb2_01), (rb2_10, rb2_11))
    pairs = []
    for first, stop, _ in GROUPS:
        cols = slice(first, stop)
        pairs += [(source.at[:, cols], target.at[:, cols]) for source, target in ((q_ref, qs), (do_ref, dos))]
        pairs += [(source.at[:, :, cols], target.at[:, :, cols]) for source, target in ((k_ref, ks), (v_ref, vs))]
    pairs += [(wk_ref, wk), (wv_ref, wv), (nrm_ref, nrm), (w_ref, wc)]
    for i in range(8):
        first = pl.multiple_of(at.x * share + i * 256, 256)
        pairs.append((tokens_ref.at[:, pl.ds(first, 256)], tok.at[i]))
    loads = [pltpu.make_async_copy(src, dst, load_sem.at[i]) for i, (src, dst) in enumerate(pairs)]
    for load in loads[:4]:
        load.start()
    barrier = pltpu.get_barrier_semaphore()
    friends = [at.along("x", 1), at.along("x", 2), at.along("x", 3), at.along("y", 1),
               at.along("y", 3), at.along("z", 1), at.along("z", 3), at.sibling()]
    for friend in friends:
        pl.semaphore_signal(barrier, inc=1, device_id=friend, device_id_type=MESH)

    send = Sender(send_sem, recv_sem)
    far, up, down = (at.x + 2) % 4, (at.x + 1) % 4, (at.x + 3) % 4
    scale = 1.0 / math.sqrt(HD)

    def added(dst, first, second):
        dst[...] = (first[...].astype(F32) + second[...].astype(F32)).astype(BF16)

    def both(dim, one, other):
        return send(*one, at.along(dim, 1)), send(*other, at.along(dim, 3))

    def attention(b, group):
        first, stop, _ = GROUPS[group]
        spans = [slice(low, low + HD) for low in range(first, stop, HD)]
        rows = pl.ds(pl.multiple_of(b * BLOCK, BLOCK), BLOCK)
        count = counts[b]
        valid = lax.broadcasted_iota(jnp.int32, (BLOCK, KEYS), 1) < count * RLEN
        empty = jnp.where(count == 0, 1.0, 0.0).astype(F32)
        for i, cols in enumerate(spans):
            score_s[i] = dot(qs[rows, cols], ks[b, :, cols], LAST) * scale
            dprob_s[i] = dot(dos[rows, cols], vs[b, :, cols], LAST)
        for i in range(len(spans)):
            scores = score_s[i]
            top = jnp.max(jnp.where(valid, scores, NEG_LARGE), axis=-1, keepdims=True)
            weights = jnp.where(valid, jnp.exp(scores - top), 0.0)
            probs = weights / (jnp.sum(weights, axis=-1, keepdims=True) + empty)
            weight_s[i] = probs.astype(BF16)
            d_probs = dprob_s[i]
            inner = jnp.sum(probs * d_probs, axis=-1, keepdims=True)
            dscore_s[i] = (probs * (d_probs - inner) * scale).astype(BF16)
        total = jnp.zeros((BLOCK, HD), F32)
        for i, cols in enumerate(spans):
            ctx[rows, cols] = dot(weight_s[i], vs[b, :, cols]).astype(BF16)
            dq = dot(dscore_s[i], ks[b, :, cols])
            dq2[rows, cols] = dq.astype(BF16)
            total = total + dq * qs[rows, cols].astype(F32)
            vs[b, :, cols] = dot(weight_s[i], dos[rows, cols], FIRST).astype(BF16)
            ks[b, :, cols] = dot(dscore_s[i], qs[rows, cols], FIRST).astype(BF16)
        sum_s[rows, :] = total if group == 0 else sum_s[rows, :] + total

    def encoded_grad(b):
        grad = dot(ks[b], wk[...], LAST) + dot(vs[b], wv[...], LAST)
        grads[b] = grad.astype(BF16)

    def share_dq(group):
        first, stop, _ = GROUPS[group]
        return send(dq2.at[0:256, first:stop], dq2.at[256:512, first:stop], at.sibling())

    def transposed(group, rows):
        first, stop, _ = GROUPS[group]
        for low in range(first, stop, 128):
            dq_t[low : low + 128, rows] = jnp.transpose(dq2[rows, low : low + 128])

    def product(group, dy, dz):
        k = at.chunk(dy, dz)
        first, stop, _ = GROUPS[group]
        prod[k, first:stop] = dot(dq_t[first:stop], nrm[k]).astype(BF16)

    dims = (("z", "y"), ("y", "z"))

    def block(group, half, line, off, part=None):
        dy, dz = (line, off) if half == 0 else (off, line)
        first, stop, z_first = GROUPS[group]
        low, high = ((first, first + z_first), (first + z_first, stop))[half]
        middle = (low + high) // 2
        low, high = (low, high) if part is None else ((low, middle), (middle, high))[part]
        return prod.at[at.chunk(dy, dz), low:high]

    c1, c2, d1, d2 = {}, {}, {}, {}

    def first_hop(group, half, line):
        slot = ra1[group][half].at[LINES.index(line)]
        c1[group, half, line] = both(
            dims[half][0],
            (block(group, half, line, 2, 0), slot.at[0]),
            (block(group, half, line, 2, 1), slot.at[1]),
        )

    def second_hop(group, half, line):
        for way, off in ((0, 1), (1, 3)):
            c1[group, half, line][way].wait_recv()
            piece = block(group, half, line, off, way)
            added(piece, piece, ra1[group][half].at[LINES.index(line), way])
        slot = ra2[group][half].at[LINES.index(line)]
        c2[group, half, line] = both(
            dims[half][0],
            (block(group, half, line, 1), slot.at[0]),
            (block(group, half, line, 3), slot.at[1]),
        )

    def gathered(group, half, line):
        for way in (0, 1):
            c2[group, half, line][way].wait_recv()
        slot = ra2[group][half].at[LINES.index(line)]
        piece = block(group, half, line, 0)
        total = piece[...].astype(F32) + slot[0].astype(F32) + slot[1].astype(F32)
        piece[...] = total.astype(BF16)

    def turn(group, half):
        d1[group, half] = both(
            dims[half][1],
            (block(group, half, 2, 0, 0), rb1[group][half].at[0]),
            (block(group, half, 2, 0, 1), rb1[group][half].at[1]),
        )

    def turned(group, half):
        for way, off in ((0, 1), (1, 3)):
            d1[group, half][way].wait_recv()
            piece = block(group, half, off, 0, way)
            added(piece, piece, rb1[group][half].at[way])
        d2[group, half] = both(
            dims[half][1],
            (block(group, half, 1, 0), rb2[group][half].at[0]),
            (block(group, half, 3, 0), rb2[group][half].at[1]),
        )

    def result(group):
        first, stop, _ = GROUPS[group]
        sizes = halves(group)
        for half in (0, 1):
            for way in (0, 1):
                c2[group, half, 0][way].wait_recv()
                d2[group, half][way].wait_recv()
            own = block(group, half, 0, 0)
            slot = ra2[group][half].at[LINES.index(0)]
            total = own[...].astype(F32) + slot[0].astype(F32) + slot[1].astype(F32)
            low = half * sizes[0]
            dw_t[low : low + sizes[half]] = (
                total + rb2[group][half][0].astype(F32) + rb2[group][half][1].astype(F32)
            )
        for low in range(0, stop - first, 128):
            dw_s[:, first + low : first + low + 128] = jnp.transpose(dw_t[low : low + 128])
        write(dw_s.at[:, first:stop], dw_ref.at[:, first:stop])

    def partial(k):
        part[k] = dot(dq2[...], wc[k], LAST).astype(BF16)

    n1, n2 = [], []

    def far_partial(m):
        partial(far * 4 + m)
        n1.append(
            both("x", (part.at[far * 4 + m, 0:256], rn1.at[m, 0]),
                 (part.at[far * 4 + m, 256:512], rn1.at[m, 1]))
        )

    def summed_partial(m):
        partial(up * 4 + m)
        partial(down * 4 + m)
        n1[m][0].wait_recv()
        piece = part.at[up * 4 + m, 0:256]
        added(piece, piece, rn1.at[m, 0])
        n1[m][1].wait_recv()
        piece = part.at[down * 4 + m, 256:512]
        added(piece, piece, rn1.at[m, 1])
        n2.append(
            both("x", (part.at[up * 4 + m], rn2.at[m, 0]), (part.at[down * 4 + m], rn2.at[m, 1]))
        )

    outs = []

    def write(src, dst):
        copy = pltpu.make_async_copy(src, dst, out_sem.at[len(outs)])
        copy.start()
        outs.append(copy)

    def finish(i, d_normed):
        inverse = wide(inverse_ref[...])
        unit = tok[i].astype(F32) * inverse
        parts = d_normed * gain_ref[at.x * 8 + i]
        result = inverse * (parts - unit * (wide(column[...]) * (1.0 / width)))
        tok[i] = result.astype(BF16)
        first = pl.multiple_of(i * 256, 256)
        write(tok.at[i], dh_ref.at[:, pl.ds(first, 256)])

    c_sib = []

    def normed_sum(m):
        for copy in n2[m]:
            copy.wait_recv()

        def summed(low):
            rows = slice(low, low + 256)
            total = part[at.x * 4 + m, rows].astype(F32) + rn2[m, 0, rows].astype(F32)
            return total + rn2[m, 1, rows].astype(F32)

        out_sib[m] = summed(256).astype(BF16)
        c_sib.append(send(out_sib.at[m], in_sib.at[m], at.sibling()))
        finish(2 * m + at.core, summed(0))

    def sibling_part(m):
        c_sib[m].wait_recv()
        finish(2 * m + 1 - at.core, in_sib[m].astype(F32))

    for load in loads[:4]:
        load.wait()
    for load in loads[4:]:
        load.start()

    @pl.loop(0, 4)
    def _(b):
        attention(b, 0)

    pl.semaphore_wait(barrier, len(friends))
    c_dq = [share_dq(0)]
    own, other = slice(0, 256), slice(256, 512)
    transposed(0, own)
    for load in loads[4:12]:
        load.wait()
    attention(far, 1)
    encoded_grad(far)
    c_g1 = both("x", (grads.at[far, 0:128], g1.at[0]), (grads.at[far, 128:256], g1.at[1]))
    c_dq[0].wait_recv()
    transposed(0, other)
    product(0, 2, 2)
    first_hop(0, 1, 2)
    first_hop(0, 0, 2)

    def leading(line):
        product(0, 2, line)
        first_hop(0, 1, line)
        product(0, line, 2)
        first_hop(0, 0, line)

    leading(1)
    attention(up, 1)
    attention(down, 1)
    encoded_grad(up)
    encoded_grad(down)
    c_g1[0].wait_recv()
    c_g1[1].wait_recv()
    gs[0, 0:128] = (grads[up, 0:128].astype(F32) + g1[0].astype(F32)).astype(BF16)
    gs[0, 128:256] = grads[up, 128:256]
    gs[1, 0:128] = grads[down, 0:128]
    gs[1, 128:256] = (grads[down, 128:256].astype(F32) + g1[1].astype(F32)).astype(BF16)
    c_g2 = both("x", (gs.at[0], g2.at[0]), (gs.at[1], g2.at[1]))
    leading(3)
    leading(0)
    second_hop(0, 1, 2)
    second_hop(0, 0, 2)
    attention(at.x, 1)
    c_dq.append(share_dq(1))
    write(ctx, ctx_ref)
    corners = ((1, 1), (3, 1), (1, 3), (3, 3))
    rest = ((1, 0), (3, 0), (0, 1), (0, 3), (0, 0))
    for dy, dz in corners:
        product(0, dy, dz)
    for line in (1, 3):
        second_hop(0, 1, line)
        second_hop(0, 0, line)
    for half in (0, 1):
        gathered(0, half, 2)
        turn(0, half)
    lanes = jnp.sum(jnp.transpose(sum_s[...]), axis=0, keepdims=True)
    sums[...] = jnp.broadcast_to(lanes, (8, 256))
    c_sums = [send(sums, sums_in.at[i], at.along("x", i + 1)) for i in range(3)]
    transposed(1, own)
    c_dq[1].wait_recv()
    transposed(1, other)
    product(1, 2, 2)
    first_hop(1, 1, 2)
    first_hop(1, 0, 2)
    for m, line in enumerate((1, 3, 0)):
        product(1, 2, line)
        first_hop(1, 1, line)
        product(1, line, 2)
        first_hop(1, 0, line)
        far_partial(m)
    far_partial(3)
    for dy, dz in rest:
        product(0, dy, dz)
    for half in (0, 1):
        gathered(0, half, 1)
        gathered(0, half, 3)
        turned(0, half)
    second_hop(1, 0, 2)
    second_hop(1, 1, 2)
    for dy, dz in corners:
        product(1, dy, dz)
    for line in (1, 3):
        second_hop(1, 0, line)
        second_hop(1, 1, line)
    summed_partial(0)
    encoded_grad(at.x)
    for copy in c_g2:
        copy.wait_recv()
    gfin[...] = (grads[at.x].astype(F32) + g2[0].astype(F32) + g2[1].astype(F32)).astype(BF16)
    c_swap = send(gfin, gin, at.partner())
    for m in range(1, 4):
        summed_partial(m)
    for dy, dz in rest:
        product(1, dy, dz)
    gathered(1, 0, 2)
    turn(1, 0)
    gathered(1, 1, 2)
    turn(1, 1)
    second_hop(0, 0, 0)
    second_hop(0, 1, 0)

    for copy in c_sums:
        copy.wait_recv()
    whole = sums[...] + sums_in[0] + sums_in[1] + sums_in[2]
    dots_ref[...] = whole[0:1] * (1.0 / math.sqrt(width))
    column[...] = jnp.transpose(jnp.broadcast_to(whole[0:1], (128, 256)))
    for load in loads[12:]:
        load.wait()
    for m in range(4):
        partial(at.x * 4 + m)
    normed_sum(0)
    gathered(1, 0, 1)
    gathered(1, 0, 3)
    turned(1, 0)
    second_hop(1, 1, 0)
    gathered(1, 1, 1)
    gathered(1, 1, 3)
    turned(1, 1)
    second_hop(1, 0, 0)
    normed_sum(1)
    sibling_part(0)
    normed_sum(2)
    sibling_part(1)
    result(0)
    c_swap.wait_recv()
    write(gin, de_ref)
    sibling_part(2)
    normed_sum(3)
    result(1)
    sibling_part(3)
    for copy in send.copies:
        copy.wait_send()
    for copy in outs:
        copy.wait()


BACKWARD_SENDS = 2 + 2 + 2 + 8 + 8 + 3 + 1 + 4 + 2 * 40


def backward(
    counts, queries, keys, values, d_context, w_key, w_value, normed, w_all, tokens, inverse, gain
):
    rows, width = queries.shape
    full = tokens.shape[1]
    vmem = pl.BlockSpec(memory_space=pltpu.VMEM)
    anywhere = pl.BlockSpec(memory_space=pl.ANY)

    def buffer(*shape, kind=BF16):
        return pltpu.VMEM(shape, kind)

    sizes = [size for group in range(2) for size in halves(group)]
    return pl.pallas_call(
        backward_kernel,
        in_specs=[pl.BlockSpec(memory_space=pltpu.SMEM)] + [anywhere] * 9 + [vmem, vmem],
        out_specs=[anywhere] * 4 + [vmem],
        out_shape=[
            jax.ShapeDtypeStruct((rows, width), BF16),
            jax.ShapeDtypeStruct((256, width), F32),
            jax.ShapeDtypeStruct((rows, full // 4), BF16),
            jax.ShapeDtypeStruct((KEYS, E), BF16),
            jax.ShapeDtypeStruct((1, rows), F32),
        ],
        scratch_shapes=[
            buffer(rows, width),
            buffer(rows, width),
            buffer(4, KEYS, width),
            buffer(4, KEYS, width),
            buffer(E, width),
            buffer(E, width),
            buffer(rows, width),
            buffer(6, BLOCK, KEYS, kind=F32),
            buffer(6, BLOCK, KEYS, kind=F32),
            buffer(6, BLOCK, KEYS),
            buffer(6, BLOCK, KEYS),
            buffer(rows, HD, kind=F32),
            buffer(512, 1024),
            buffer(1024, 512),
            buffer(16, 512, 256),
            buffer(16, 256, 1024),
            buffer(16, 1024, 256),
            buffer(768, 256, kind=F32),
            buffer(256, width, kind=F32),
            buffer(16, 512, 256),
            buffer(4, 2, 256, 256),
            buffer(4, 2, 512, 256),
            buffer(4, 256, 256),
            buffer(4, 256, 256),
            buffer(4, KEYS, E),
            buffer(2, 128, E),
            buffer(2, 256, E),
            buffer(2, 256, E),
            buffer(256, E),
            buffer(256, E),
            buffer(8, 256, kind=F32),
            buffer(3, 8, 256, kind=F32),
            buffer(8, 256, 256),
            buffer(256, 128, kind=F32),
        ]
        + [buffer(4, 2, size // 2, 256) for size in sizes]
        + [buffer(4, 2, size, 256) for size in sizes]
        + [buffer(2, size // 2, 256) for size in sizes]
        + [buffer(2, size, 256) for size in sizes]
        + [
            pltpu.SemaphoreType.DMA((LOADS,)),
            pltpu.SemaphoreType.DMA((12,)),
            pltpu.SemaphoreType.DMA((BACKWARD_SENDS,)),
            pltpu.SemaphoreType.DMA((BACKWARD_SENDS,)),
        ],
        compiler_params=pltpu.CompilerParams(
            collective_id=1, has_side_effects=True, vmem_limit_bytes=62 * 2**20
        ),
        cost_estimate=pl.CostEstimate(
            flops=12 * 2**30, bytes_accessed=30 * 2**20, transcendentals=0
        ),
    )(counts, queries, keys, values, d_context, w_key, w_value, normed, w_all, tokens, inverse, gain)


def results_kernel(*refs):
    count = (len(refs) - 2) // 3
    in_sem, out_sem = refs[-2:]
    coming, going = [], []
    for source, target, held in zip(refs, refs[count:], refs[2 * count : 3 * count]):
        pieces = min(2, source.shape[0])
        rows = source.shape[0] // pieces
        for i in range(pieces):
            piece, index = pl.ds(i * rows, rows), len(coming)
            coming.append(
                pltpu.make_async_copy(source.at[piece], held.at[piece], in_sem.at[index])
            )
            going.append(
                pltpu.make_async_copy(held.at[piece], target.at[piece], out_sem.at[index])
            )
    for copy in coming:
        copy.start()
    for arrived, copy in zip(coming, going):
        arrived.wait()
        copy.start()
    for copy in going:
        copy.wait()


def results(*arrays):
    anywhere = pl.BlockSpec(memory_space=pl.ANY)
    return pl.pallas_call(
        results_kernel,
        in_specs=[anywhere] * len(arrays),
        out_specs=[anywhere] * len(arrays),
        out_shape=[jax.ShapeDtypeStruct(array.shape, array.dtype) for array in arrays],
        scratch_shapes=[pltpu.VMEM(array.shape, array.dtype) for array in arrays]
        + [pltpu.SemaphoreType.DMA((2 * len(arrays),))] * 2,
        compiler_params=pltpu.CompilerParams(vmem_limit_bytes=62 * 2**20),
    )(*arrays)


def shards(
    tokens,
    w_query,
    query_gain,
    state_kv,
    neighbours,
    enc_gain,
    enc_query,
    enc_out,
    w_key,
    w_value,
    counts,
    d_context,
):
    gain = query_gain.reshape(32, 1, 256)
    queries, w_part, normed, keys, values, inverse = forward(
        tokens, w_query, gain, state_kv, neighbours.reshape(KEYS, E), enc_gain,
        enc_query, enc_out, w_key, w_value,
    )
    context, d_query_weight, d_hidden, d_encoded, row_dots = backward(
        counts, queries, keys, values, d_context, w_key, w_value, normed, w_part, tokens, inverse,
        gain,
    )
    context, d_query_weight, d_hidden, d_encoded, row_dots = results(
        context, d_query_weight, d_hidden, d_encoded, row_dots
    )
    return (
        context,
        d_hidden,
        d_query_weight,
        d_encoded.reshape(1, 1, NBR, RLEN, E),
        row_dots[0],
    )


def solution(mesh):
    return jax.shard_map(
        shards,
        mesh=mesh,
        in_specs=(
            P(("section", "seq"), None),
            P(("section", "seq"), "tensor"),
            P(),
            P("tensor", None),
            P("section", ("seq", "tensor"), None, None, None),
            P(),
            P(),
            P(),
            P(None, "tensor"),
            P(None, "tensor"),
            P(("section", "seq")),
            P(("section", "seq"), "tensor"),
        ),
        out_specs=(
            P(("section", "seq"), "tensor"),
            P(("section", "seq"), "tensor"),
            P(("section", "seq"), "tensor"),
            P("section", ("seq", "tensor"), None, None, None),
            P(("section", "seq")),
        ),
        check_vma=False,
    )
```
